128 devices in a mesh: fsdp: 128 (over x, z, y, core).
Axes of the slice: x: 4, y: 4, z: 4, core: 2. Of those that a mesh axis runs over, the one named last changes fastest.
Arguments:
- tokens: bfloat16 [128, 128, 1536], P('fsdp'), may hold values from -6 to 6
- lengths: int32 [128], P('fsdp'), may hold values from 64 to 128, as said below
- gain_attn: bfloat16 [1536], P('fsdp'), may hold values from 0.5 to 1.5
- w_query: bfloat16 [1536, 1536], P('fsdp'), may hold values from -0.15625 to 0.15625
- w_key: bfloat16 [1536, 1536], P('fsdp'), may hold values from -0.15625 to 0.15625
- w_value: bfloat16 [1536, 1536], P('fsdp'), may hold values from -0.15625 to 0.15625
- w_house: bfloat16 [1536, 1536], P('fsdp'), may hold values from -0.15625 to 0.15625
- w_beta: bfloat16 [1536, 12], P('fsdp'), may hold values from -0.15625 to 0.15625
- w_out: bfloat16 [1536, 1536], P('fsdp'), may hold values from -0.4375 to 0.4375
- gain_ffn: bfloat16 [1536], P('fsdp'), may hold values from 0.5 to 1.5
- w_gate: bfloat16 [1536, 4096], P('fsdp'), may hold values from -0.15625 to 0.15625
- w_up: bfloat16 [1536, 4096], P('fsdp'), may hold values from -0.15625 to 0.15625
- w_down: bfloat16 [4096, 1536], P('fsdp'), may hold values from -0.09375 to 0.09375
- cotangent: bfloat16 [128, 128, 1536], P('fsdp'), may hold values from -6 to 6
Outputs:
- mixed_out: bfloat16 [128, 128, 1536], P('fsdp')
- grad_tokens: float32 [128, 128, 1536], P('fsdp')
- grad_gain_attn: float32 [1536], P('fsdp')
- grad_w_query: float32 [1536, 1536], P('fsdp')
- grad_w_key: float32 [1536, 1536], P('fsdp')
- grad_w_value: float32 [1536, 1536], P('fsdp')
- grad_w_house: float32 [1536, 1536], P('fsdp')
- grad_w_beta: float32 [1536, 12], P('fsdp')
- grad_w_out: float32 [1536, 1536], P('fsdp')
- grad_gain_ffn: float32 [1536], P('fsdp')
- grad_w_gate: float32 [1536, 4096], P('fsdp')
- grad_w_up: float32 [1536, 4096], P('fsdp')
- grad_w_down: float32 [4096, 1536], P('fsdp')
The draws below stay inside these ranges and needn't reach their ends.
Inputs may be any that keep to these rules, and one draw needn't show every extreme that they name: `lengths`: some sequence has all 128 tokens valid.
All inputs are finite; a program needn't handle non-finite values.
Results may differ from the reference program's by a relative error of at most 0.02.
Values may be sent and summed in bfloat16 or wider, within the bound.
No kernel may reach another device: no remote copies, remote signals or barrier semaphores. Data moves between devices by JAX's collectives and lax.ppermute only.
A program may use at most 320 MiB of HBM per device.

```python
import jax
import jax.numpy as jnp
from jax import lax

D = 1536
HEADS = 12
FF = 4096
SLEN = 128
SEQS = 128


def draw_lengths(key, part):
    key = jax.random.fold_in(key, 7)
    drawn = jax.random.randint(key, (SEQS,), SLEN // 2, SLEN + 1, dtype=jnp.int32)
    return drawn.at[0].set(SLEN)


def block_scale(rng, extent, pieces, low, high):
    level, own = 1.0, jax.random.fold_in(rng, 6)
    for axis_at, blocks in pieces:
        draws = jnp.exp(jax.random.uniform(jax.random.fold_in(own, axis_at), (blocks,), jnp.float32, low / len(pieces), high / len(pieces)))
        level = level * jnp.repeat(draws, extent[axis_at] // blocks).reshape([-1 if axis == axis_at else 1 for axis in range(len(extent))])
    return level


def scatter_about(key, dims, scale, limit, shards=(), kind=jnp.bfloat16):
    values = scale * jax.random.normal(key, dims, jnp.float32)
    if shards:
        values = values * block_scale(key, dims, shards, -0.22, 0.18)
    return jnp.clip(values, -limit, limit).astype(kind)


def setup_inputs(seed: int = 0) -> dict:
    seeds = jax.random.split(jax.random.key(seed), 15)
    return {
        "tokens": scatter_about(seeds[0], (SEQS, SLEN, D), 1.0, 6.0, ((0, 128),)),
        "lengths": draw_lengths(jax.random.fold_in(seeds[14], 71), 0),
        "gain_attn": jnp.clip(1.0 + 0.1 * jax.random.normal(seeds[2], (D,), jnp.float32), 0.5, 1.5).astype(jnp.bfloat16),
        "w_query": scatter_about(seeds[3], (D, D), D ** -0.5, 0.15625, ((0, 128),)),
        "w_key": scatter_about(seeds[4], (D, D), D ** -0.5, 0.15625, ((0, 128),)),
        "w_value": scatter_about(seeds[5], (D, D), D ** -0.5, 0.15625, ((0, 128),)),
        "w_house": scatter_about(seeds[6], (D, D), D ** -0.5, 0.15625, ((0, 128),)),
        "w_beta": scatter_about(seeds[7], (D, HEADS), D ** -0.5, 0.15625, ((0, 128),)),
        "w_out": scatter_about(seeds[8], (D, D), (D // 8) ** -0.5, 0.4375, ((0, 128),)),
        "gain_ffn": jnp.clip(1.0 + 0.1 * jax.random.normal(seeds[9], (D,), jnp.float32), 0.5, 1.5).astype(jnp.bfloat16),
        "w_gate": scatter_about(seeds[10], (D, FF), D ** -0.5, 0.15625, ((0, 128),)),
        "w_up": scatter_about(seeds[11], (D, FF), D ** -0.5, 0.15625, ((0, 128),)),
        "w_down": scatter_about(seeds[12], (FF, D), FF ** -0.5, 0.09375, ((0, 128),)),
        "cotangent": scatter_about(seeds[13], (SEQS, SLEN, D), 1.0, 6.0, ((0, 128),)),
    }


EPSILON = 1e-06
EXACT_PRECISION = lax.Precision.HIGHEST

@jax.custom_vjp
def low(v):
    return lax.optimization_barrier(v.astype(jnp.bfloat16)).astype(jnp.float32)

@jax.custom_vjp
def low_back(v):
    return v

def low_keep(v):
    return (low(v), None)

def low_pass(kept, grad):
    return (grad,)

def back_keep(v):
    return (v, None)

def back_low(kept, grad):
    return (low(grad),)
low.defvjp(low_keep, low_pass)
low_back.defvjp(back_keep, back_low)

def rms_scale(vector, gain_vec):
    return vector * lax.rsqrt(lax.optimization_barrier(jnp.mean(vector * vector, axis=-1, keepdims=True)) + EPSILON) * gain_vec

def project(incoming_rows, weight_matrix):
    return jnp.einsum('uwk,kf->uwf', incoming_rows, weight_matrix, precision=EXACT_PRECISION)

def reflector_probabilities(queries, key_rows, house_raw, beta_raw, length):
    count = queries.shape[0]
    position = jnp.arange(count, dtype=jnp.int32)
    strict = position[:, None] > position[None, :]
    upto = position[:, None] >= position[None, :]
    unit_house = house_raw * lax.rsqrt(lax.optimization_barrier(jnp.sum(house_raw * house_raw, axis=-1, keepdims=True)) + EPSILON)
    betas = 2.0 * jax.nn.sigmoid(beta_raw)
    coupling = jnp.where(strict, betas[:, None] * jnp.dot(unit_house, unit_house.T, precision=EXACT_PRECISION), 0.0)
    system = jnp.eye(count, dtype=queries.dtype) + coupling
    source = jnp.where(strict, betas[:, None] * jnp.dot(unit_house, key_rows.T, precision=EXACT_PRECISION), 0.0)
    carried = lax.linalg.triangular_solve(system, source, left_side=True, lower=True, unit_diagonal=True)
    direct = jnp.dot(queries, key_rows.T, precision=EXACT_PRECISION)
    through = jnp.where(upto, jnp.dot(queries, unit_house.T, precision=EXACT_PRECISION), 0.0)
    logits = (direct - jnp.dot(through, carried, precision=EXACT_PRECISION)) * queries.shape[1] ** (-0.5)
    allowed = upto & (position[None, :] < length)
    logits = jnp.where(allowed, logits, -1e+30)
    highest = lax.optimization_barrier(jnp.max(logits, axis=-1, keepdims=True))
    weights = jnp.where(allowed, jnp.exp(logits - highest), 0.0)
    return weights / lax.optimization_barrier(jnp.sum(weights, axis=-1, keepdims=True))

def layer(tokens, gain_attn, w_query, w_key, w_value, w_house, w_beta, w_out, gain_ffn, w_gate, w_up, w_down, lengths):
    seqs, count, width = tokens.shape
    heads = w_beta.shape[1]
    shape_heads = (seqs, count, heads, width // heads)
    normed = low(rms_scale(tokens, gain_attn))
    queries = low_back(low(project(normed, w_query))).reshape(shape_heads)
    key_rows = low_back(low(project(normed, w_key))).reshape(shape_heads)
    values_in = low_back(low(project(normed, w_value))).reshape(shape_heads)
    house_in = low_back(low(project(normed, w_house))).reshape(shape_heads)
    beta_raw = low_back(project(normed, w_beta))

    def one_sequence(items):
        seq_query, seq_key, seq_value, seq_house, seq_beta, length = items

        def single_head_slice(head_query, head_key, head_value, head_house, head_beta):
            probs = low(reflector_probabilities(head_query, head_key, head_house, head_beta, length))
            return jnp.dot(probs, head_value, precision=EXACT_PRECISION)
        return jax.vmap(single_head_slice, in_axes=(1, 1, 1, 1, 1), out_axes=1)(seq_query, seq_key, seq_value, seq_house, seq_beta)
    mixed_heads = lax.map(jax.checkpoint(one_sequence), (queries, key_rows, values_in, house_in, beta_raw, lengths))
    attended = low_back(low(mixed_heads.reshape(seqs, count, width)))
    branch = low_back(project(attended, w_out))
    hidden = tokens + branch
    second = low(rms_scale(hidden, gain_ffn))
    gate = low_back(project(second, w_gate))
    upward = low_back(project(second, w_up))
    product = low(jax.nn.silu(gate) * upward)
    feed = low_back(project(product, w_down))
    unpadded_row_mask = (jnp.arange(count, dtype=jnp.int32)[None, :] < lengths[:, None]).astype(tokens.dtype)
    return unpadded_row_mask[:, :, None] * (hidden + feed)

def reference(tokens, lengths, gain_attn, w_query, w_key, w_value, w_house, w_beta, w_out, gain_ffn, w_gate, w_up, w_down, cotangent):
    floats = tuple((item.astype(jnp.float32) for item in (tokens, gain_attn, w_query, w_key, w_value, w_house, w_beta, w_out, gain_ffn, w_gate, w_up, w_down)))

    def bound(*items):
        return layer(*items, lengths)
    result, pullback = jax.vjp(bound, *floats)
    grads = pullback(cotangent.astype(jnp.float32))
    return (result.astype(jnp.bfloat16), grads[0], grads[1], grads[2], grads[3], grads[4], grads[5], grads[6], grads[7], grads[8], grads[9], grads[10], grads[11])
```

```python
import functools

import jax
import jax.numpy as jnp
import numpy as np
from jax import lax
from jax.experimental import pallas as pl
from jax.experimental.pallas import tpu as pltpu
from jax.sharding import PartitionSpec as P

EPSILON = 1e-06
BF = jnp.bfloat16
F32 = jnp.float32
VMEM_LIMIT = 56 * 1024 * 1024
AXIS_UNIT = {"x": 16, "z": 4, "y": 1}
ORDERS = ("xzy", "zyx", "yxz")


def step_masks(stream, core):
    masks = []
    for axis in ORDERS[stream]:
        unit = AXIS_UNIT[axis]
        masks += [unit, 3 * unit] if core == 0 else [3 * unit, unit]
    return masks


MASKS = [[step_masks(stream, core) for core in (0, 1)] for stream in range(3)]


def owner_offsets():
    table = np.zeros((2, 3, 64), np.int32)
    for core in (0, 1):
        for stream in range(3):
            for place in range(64):
                value = 0
                for step, mask in enumerate(MASKS[stream][core]):
                    if (place >> (5 - step)) & 1:
                        value ^= mask
                table[core, stream, place] = value
    return table


def dot(left, right):
    return jnp.dot(left, right, preferred_element_type=F32)


def dot_nt(left, right):
    return lax.dot_general(left, right, (((1,), (1,)), ((), ())), preferred_element_type=F32)


def dot_tn(left, right):
    return lax.dot_general(left, right, (((0,), (0,)), ((), ())), preferred_element_type=F32)


def two_parts(value):
    high = value.astype(BF)
    return high, (value - high.astype(F32)).astype(BF)


def dot_fine(left, right):
    size = right.shape[1]
    wide = jnp.concatenate(two_parts(left), axis=1)
    pair = jnp.concatenate(two_parts(right), axis=1)
    out = dot(wide, jnp.concatenate([pair, pair], axis=0))
    return out[:, :size] + out[:, size:]


def swap(value):
    count = lax.axis_size("fsdp")
    return lax.ppermute(value, "fsdp", [(d, d ^ 1) for d in range(count)])


def gain_row(misc_ref, column):
    pick = (lax.broadcasted_iota(jnp.int32, (8, 128), 1) == column).astype(F32).astype(BF)
    return dot_nt(pick, misc_ref[...])[0:1]


def triangles(count):
    row = lax.broadcasted_iota(jnp.int32, (count, count), 0)
    col = lax.broadcasted_iota(jnp.int32, (count, count), 1)
    return row, col


def beta_of(raw, head):
    lane = lax.broadcasted_iota(jnp.int32, raw.shape, 1)
    return jnp.sum(jnp.where(lane == head, raw, 0.0), axis=1, keepdims=True)


def unit_lower_inverse(systems, row, col):
    size = row.shape[0]
    eye = (row == col).astype(F32)
    step = 1
    inverses = None
    while step < size:
        lower = ((row // step) % 2 == 1) & (col // step == row // step - 1)
        parts = [jnp.where(lower, system, 0.0) for system in systems]
        if step == 1:
            inverses = [eye - part for part in parts]
        else:
            middles = [dot_fine(inv, part) for inv, part in zip(inverses, parts)]
            inverses = [inv - dot_fine(mid, inv) for inv, mid in zip(inverses, middles)]
        step *= 2
    return inverses


PER_STEP = 2


def attention_forward_kernel(
    length_ref,
    tokens_ref,
    wq_ref,
    wk_ref,
    wv_ref,
    wh_ref,
    misc_ref,
    normed_ref,
    q_ref,
    k_ref,
    v_ref,
    h_ref,
    att_ref,
    probs_ref,
    carried_ref,
    inverse_ref,
    beta_ref,
):
    at = pl.program_id(0)

    @pl.when(at == 0)
    def _():
        tokens = tokens_ref[...].astype(F32)
        scale = lax.rsqrt(jnp.mean(tokens * tokens, axis=1, keepdims=True) + EPSILON)
        normed_ref[...] = (tokens * scale * gain_row(misc_ref, 12)).astype(BF)
        beta_ref[...] = dot(normed_ref[...], misc_ref[...])

    normed = normed_ref[...]
    q_all = dot(normed, wq_ref[...]).astype(BF)
    k_all = dot(normed, wk_ref[...]).astype(BF)
    v_all = dot(normed, wv_ref[...]).astype(BF)
    h_all = dot(normed, wh_ref[...]).astype(BF)
    q_ref[...] = q_all
    k_ref[...] = k_all
    v_ref[...] = v_all
    h_ref[...] = h_all
    count = q_all.shape[0]
    row, col = triangles(count)
    strict = row > col
    upto = row >= col
    allowed = upto & (col < length_ref[0])
    raw = beta_ref[...]
    heads = range(PER_STEP)
    q, k, v, h = (
        [value[:, 128 * i : 128 * (i + 1)] for i in heads] for value in (q_all, k_all, v_all, h_all)
    )
    big = [
        dot_nt(jnp.concatenate([h[i], q[i]], axis=0), jnp.concatenate([h[i], k[i]], axis=0))
        for i in heads
    ]
    strength = []
    for i in heads:
        house = h[i].astype(F32)
        square = jnp.sum(house * house, axis=1, keepdims=True) + EPSILON
        beta = 2.0 * jax.nn.sigmoid(beta_of(raw, at * PER_STEP + i))
        strength.append(beta / square)
    systems = [jnp.where(strict, strength[i] * big[i][:count, :count], 0.0) for i in heads]
    sources = [jnp.where(strict, strength[i] * big[i][:count, count:], 0.0) for i in heads]
    inverses = unit_lower_inverse(systems, row, col)
    carried = [dot_fine(inverses[i], sources[i]) for i in heads]
    through = [
        dot_fine(jnp.where(upto, big[i][count:, :count], 0.0), carried[i]) for i in heads
    ]
    for i in heads:
        logits = (big[i][count:, count:] - through[i]) * 128 ** (-0.5)
        logits = jnp.where(allowed, logits, -1e30)
        highest = jnp.max(logits, axis=1, keepdims=True)
        weights = jnp.where(allowed, jnp.exp(logits - highest), 0.0)
        probs = weights / jnp.sum(weights, axis=1, keepdims=True)
        probs_ref[i] = probs
        carried_ref[i] = carried[i].astype(BF)
        inverse_ref[i] = inverses[i].astype(BF)
        att_ref[:, 128 * i : 128 * (i + 1)] = dot(probs.astype(BF), v[i]).astype(BF)


def attention_forward(tokens, length, attn):
    count, width = tokens.shape
    steps = width // 256
    cell = (PER_STEP, count, count)
    whole = lambda i, *_: (0, 0)
    column = lambda i, *_: (0, i)
    weight = lambda half, first: pl.BlockSpec(
        (width, 256), lambda i, *_: (half, first + i)
    )
    row_block = pl.BlockSpec((count, 256), column)
    cell_block = pl.BlockSpec(cell, lambda i, *_: (i, 0, 0))
    rows = jax.ShapeDtypeStruct((count, width), BF)
    cells = (2 * steps, count, count)
    return pl.pallas_call(
        attention_forward_kernel,
        grid_spec=pltpu.PrefetchScalarGridSpec(
            num_scalar_prefetch=1,
            grid=(steps,),
            in_specs=[
                pl.BlockSpec((count, width), whole),
                weight(0, 20),
                weight(0, 26),
                weight(1, 20),
                weight(1, 26),
                pl.BlockSpec((width, 128), lambda i, *_: (0, 6)),
            ],
            out_specs=[
                pl.BlockSpec((count, width), whole),
                row_block,
                row_block,
                row_block,
                row_block,
                row_block,
                cell_block,
                cell_block,
                cell_block,
                pl.BlockSpec((count, 128), whole),
            ],
        ),
        out_shape=[
            rows,
            rows,
            rows,
            rows,
            rows,
            rows,
            jax.ShapeDtypeStruct(cells, F32),
            jax.ShapeDtypeStruct(cells, BF),
            jax.ShapeDtypeStruct(cells, BF),
            jax.ShapeDtypeStruct((count, 128), F32),
        ],
        compiler_params=pltpu.CompilerParams(vmem_limit_bytes=VMEM_LIMIT),
        cost_estimate=pl.CostEstimate(
            flops=8 * count * width * width + 12 * 60 * 2 * 128**3,
            bytes_accessed=10 * width * width,
            transcendentals=0,
        ),
        name="attention_forward",
    )(length, tokens, attn, attn, attn, attn, attn)


FF_BLOCK = 512


def feedforward_kernel(
    length_ref,
    tokens_ref,
    att_ref,
    out_lo_ref,
    out_hi_ref,
    misc_ref,
    cot_ref,
    wg_ref,
    wu_ref,
    wd_lo_ref,
    wd_hi_ref,
    second_ref,
    acts_ref,
    mixed_ref,
    hidden_grad_ref,
    branch_ref,
    gain_grad_ref,
    hidden,
    feed,
    second_grad,
):
    at = pl.program_id(0)
    half = out_lo_ref.shape[1]

    @pl.when(at == 0)
    def _():
        att = att_ref[...]
        hidden[:, :half] = tokens_ref[:, :half].astype(F32) + dot(att, out_lo_ref[...])
        hidden[:, half:] = tokens_ref[:, half:].astype(F32) + dot(att, out_hi_ref[...])
        value = hidden[...]
        scale = lax.rsqrt(jnp.mean(value * value, axis=1, keepdims=True) + EPSILON)
        second_ref[...] = (value * scale * gain_row(misc_ref, 13)).astype(BF)
        feed[...] = jnp.zeros_like(feed)
        second_grad[...] = jnp.zeros_like(second_grad)

    second = second_ref[...]
    cot = cot_ref[...]
    gate = dot(second, wg_ref[...])
    upward = dot(second, wu_ref[...])
    sigma = jax.nn.sigmoid(gate)
    silu = gate * sigma
    product = (silu * upward).astype(BF)
    product_grad = dot_nt(cot[:, :half], wd_lo_ref[...]) + dot_nt(cot[:, half:], wd_hi_ref[...])
    gate_low = (product_grad * upward * (sigma * (1.0 + gate * (1.0 - sigma)))).astype(BF)
    up_low = (product_grad * silu).astype(BF)
    acts_ref[0] = product
    acts_ref[1] = gate_low
    acts_ref[2] = up_low
    feed[:, :half] += dot(product, wd_lo_ref[...])
    feed[:, half:] += dot(product, wd_hi_ref[...])
    second_grad[...] += dot_nt(gate_low, wg_ref[...]) + dot_nt(up_low, wu_ref[...])

    @pl.when(at == pl.num_programs(0) - 1)
    def _():
        value = hidden[...]
        valid = lax.broadcasted_iota(jnp.int32, value.shape, 0) < length_ref[0]
        mixed_ref[...] = jnp.where(valid, value + feed[...], 0.0).astype(BF)
        scale = lax.rsqrt(jnp.mean(value * value, axis=1, keepdims=True) + EPSILON)
        grad = second_grad[...]
        scaled = grad * gain_row(misc_ref, 13)
        along = jnp.mean(scaled * value, axis=1, keepdims=True)
        hidden_grad = (
            cot_ref[...].astype(F32) + scale * scaled - value * (scale * scale * scale * along)
        )
        hidden_grad_ref[...] = hidden_grad
        branch_ref[...] = hidden_grad.astype(BF)
        gain_grad_ref[...] = jnp.sum(grad * value * scale, axis=0, keepdims=True)


def feedforward(tokens, length, att, cot, attn, down):
    count, width = tokens.shape
    hidden_units = down.shape[0] // 2
    steps = hidden_units // FF_BLOCK
    half = width // 2
    whole = lambda i, *_: (0, 0)
    rows = pl.BlockSpec((count, width), whole)
    weight = lambda side: pl.BlockSpec(
        (width, FF_BLOCK), lambda i, *_: (side, 1024 // FF_BLOCK + i)
    )
    down_block = lambda side: pl.BlockSpec((FF_BLOCK, half), lambda i, *_: (side * steps + i, 0))
    return pl.pallas_call(
        feedforward_kernel,
        grid_spec=pltpu.PrefetchScalarGridSpec(
            num_scalar_prefetch=1,
            grid=(steps,),
            in_specs=[
                rows,
                rows,
                pl.BlockSpec((width, half), whole),
                pl.BlockSpec((width, half), lambda i, *_: (1, 0)),
                pl.BlockSpec((width, 128), lambda i, *_: (0, 6)),
                rows,
                weight(0),
                weight(1),
                down_block(0),
                down_block(1),
            ],
            out_specs=[
                rows,
                pl.BlockSpec((3, count, FF_BLOCK), lambda i, *_: (0, 0, i)),
                rows,
                rows,
                rows,
                pl.BlockSpec((1, width), whole),
            ],
            scratch_shapes=[
                pltpu.VMEM((count, width), F32),
                pltpu.VMEM((count, width), F32),
                pltpu.VMEM((count, width), F32),
            ],
        ),
        out_shape=[
            jax.ShapeDtypeStruct((count, width), BF),
            jax.ShapeDtypeStruct((3, count, hidden_units), BF),
            jax.ShapeDtypeStruct((count, width), BF),
            jax.ShapeDtypeStruct((count, width), F32),
            jax.ShapeDtypeStruct((count, width), BF),
            jax.ShapeDtypeStruct((1, width), F32),
        ],
        compiler_params=pltpu.CompilerParams(vmem_limit_bytes=VMEM_LIMIT),
        cost_estimate=pl.CostEstimate(
            flops=12 * count * width * hidden_units,
            bytes_accessed=6 * width * hidden_units,
            transcendentals=0,
        ),
        name="feedforward",
    )(length, tokens, att, attn, attn, attn, cot, attn, attn, down, down)


def attention_backward_kernel(
    tokens_ref,
    normed_ref,
    branch_ref,
    hidden_grad_ref,
    ffn_gain_ref,
    beta_ref,
    q_ref,
    k_ref,
    v_ref,
    h_ref,
    probs_ref,
    carried_ref,
    inverse_ref,
    wo_lo_ref,
    wo_hi_ref,
    wq_ref,
    wk_ref,
    wv_ref,
    wh_ref,
    misc_ref,
    grads_ref,
    grad_tokens_ref,
    misc_grad_ref,
    normed_grad,
    beta_grad,
):
    at = pl.program_id(0)
    half = wo_lo_ref.shape[1]

    @pl.when(at == 0)
    def _():
        normed_grad[...] = jnp.zeros_like(normed_grad)
        beta_grad[...] = jnp.zeros_like(beta_grad)

    att_grad_all = (
        dot_nt(branch_ref[:, :half], wo_lo_ref[...]) + dot_nt(branch_ref[:, half:], wo_hi_ref[...])
    ).astype(BF)
    count = att_grad_all.shape[0]
    row, col = triangles(count)
    strict = row > col
    upto = row >= col
    raw = beta_ref[...]
    lane = lax.broadcasted_iota(jnp.int32, raw.shape, 1)
    heads = range(PER_STEP)
    part = lambda ref: [ref[:, 128 * i : 128 * (i + 1)] for i in heads]
    q, k, v, h = part(q_ref), part(k_ref), part(v_ref), part(h_ref)
    att_grad = [att_grad_all[:, 128 * i : 128 * (i + 1)] for i in heads]
    big = [
        dot_nt(jnp.concatenate([h[i], q[i]], axis=0), jnp.concatenate([h[i], k[i]], axis=0))
        for i in heads
    ]
    probs = [probs_ref[i] for i in heads]
    carried = [carried_ref[i] for i in heads]
    inverse = [inverse_ref[i] for i in heads]
    probs_grad = [dot_nt(att_grad[i], v[i]) for i in heads]
    value_grad = [dot_tn(probs[i].astype(BF), att_grad[i]) for i in heads]
    logit_grad = []
    for i in heads:
        total = jnp.sum(probs_grad[i] * probs[i], axis=1, keepdims=True)
        logit_grad.append((probs[i] * (probs_grad[i] - total) * 128 ** (-0.5)).astype(BF))
    through_grad = [
        jnp.where(upto, -dot_nt(logit_grad[i], carried[i]), 0.0).astype(BF) for i in heads
    ]
    carried_grad = [
        -dot_tn(jnp.where(upto, big[i][count:, :count], 0.0).astype(BF), logit_grad[i])
        for i in heads
    ]
    solved = [dot_tn(inverse[i], carried_grad[i].astype(BF)) for i in heads]
    system_grad = [
        jnp.where(strict, -dot_nt(solved[i].astype(BF), carried[i]), 0.0) for i in heads
    ]
    source_grad = [jnp.where(strict, solved[i], 0.0) for i in heads]
    total_beta = jnp.zeros_like(raw)
    q_grads, k_grads, v_grads, h_grads = [], [], [], []
    for i in heads:
        house = h[i].astype(F32)
        inverse_square = 1.0 / (jnp.sum(house * house, axis=1, keepdims=True) + EPSILON)
        sigma = jax.nn.sigmoid(beta_of(raw, at * PER_STEP + i))
        strength = 2.0 * sigma * inverse_square
        key_part = (strength * source_grad[i]).astype(BF)
        self_part = (strength * system_grad[i]).astype(BF)
        strength_grad = jnp.sum(
            source_grad[i] * big[i][:count, count:] + system_grad[i] * big[i][:count, :count],
            axis=1,
            keepdims=True,
        )
        key_house = jnp.concatenate([k[i], h[i]], axis=0)
        query_house = jnp.concatenate([q[i], h[i]], axis=0)
        q_grads.append(
            dot(jnp.concatenate([logit_grad[i], through_grad[i]], axis=1), key_house).astype(BF)
        )
        k_grads.append(
            dot_tn(jnp.concatenate([logit_grad[i], key_part], axis=0), query_house).astype(BF)
        )
        house_grad = (
            dot_tn(jnp.concatenate([through_grad[i], self_part], axis=0), query_house)
            + dot(jnp.concatenate([key_part, self_part], axis=1), key_house)
            - (2.0 * strength_grad * strength * inverse_square) * house
        )
        h_grads.append(house_grad.astype(BF))
        v_grads.append(value_grad[i].astype(BF))
        raw_grad = strength_grad * inverse_square * (2.0 * sigma * (1.0 - sigma))
        total_beta += jnp.where(lane == at * PER_STEP + i, raw_grad, 0.0)
    beta_grad[...] += total_beta
    update = None
    for index, (pieces, weight_ref) in enumerate(
        ((q_grads, wq_ref), (k_grads, wk_ref), (v_grads, wv_ref), (h_grads, wh_ref))
    ):
        joined = jnp.concatenate(pieces, axis=1)
        grads_ref[index] = joined
        term = dot_nt(joined, weight_ref[...])
        update = term if update is None else update + term
    normed_grad[...] += update

    @pl.when(at == pl.num_programs(0) - 1)
    def _():
        beta_low = beta_grad[...].astype(BF)
        grad = normed_grad[...] + dot_nt(beta_low, misc_ref[...])
        value = tokens_ref[...].astype(F32)
        scale = lax.rsqrt(jnp.mean(value * value, axis=1, keepdims=True) + EPSILON)
        scaled = grad * gain_row(misc_ref, 12)
        along = jnp.mean(scaled * value, axis=1, keepdims=True)
        grad_tokens_ref[...] = (
            hidden_grad_ref[...] + scale * scaled - value * (scale * scale * scale * along)
        )
        attn_gain = jnp.sum(grad * value * scale, axis=0, keepdims=True)
        attn_high, attn_low = two_parts(attn_gain)
        ffn_high, ffn_low = two_parts(ffn_gain_ref[...])
        gains = jnp.concatenate(
            [
                attn_high.astype(F32),
                attn_low.astype(F32),
                ffn_high.astype(F32),
                ffn_low.astype(F32),
                jnp.zeros((4, attn_gain.shape[1]), F32),
            ],
            axis=0,
        )
        place = lax.broadcasted_iota(jnp.int32, (8, 128), 0)
        lanes = lax.broadcasted_iota(jnp.int32, (8, 128), 1)
        pick = ((place < 4) & (lanes == 12 + place // 2)).astype(F32)
        misc_grad = dot_tn(normed_ref[...], beta_low) + dot_tn(
            gains.astype(BF), pick.astype(BF)
        )
        misc_grad_ref[...] = misc_grad.astype(BF)


def attention_backward(tokens, normed, branch, hidden_grad, ffn_gain, saved, attn):
    q, k, v, h, probs, carried, inverse, beta = saved
    count, width = tokens.shape
    steps = width // 256
    half = width // 2
    whole = lambda i: (0, 0)
    rows = pl.BlockSpec((count, width), whole)
    row_block = pl.BlockSpec((count, 256), lambda i: (0, i))
    cell_block = pl.BlockSpec((PER_STEP, count, count), lambda i: (i, 0, 0))
    weight = lambda side, first: pl.BlockSpec((width, 256), lambda i: (side, first + i))
    out_rows = lambda side: pl.BlockSpec((256, half), lambda i: (side * steps + i, 0))
    return pl.pallas_call(
        attention_backward_kernel,
        grid=(steps,),
        in_specs=[
            rows,
            rows,
            rows,
            rows,
            pl.BlockSpec((1, width), whole),
            pl.BlockSpec((count, 128), whole),
            row_block,
            row_block,
            row_block,
            row_block,
            cell_block,
            cell_block,
            cell_block,
            out_rows(0),
            out_rows(1),
            weight(0, 20),
            weight(0, 26),
            weight(1, 20),
            weight(1, 26),
            pl.BlockSpec((width, 128), lambda i: (0, 6)),
        ],
        out_specs=[
            pl.BlockSpec((4, count, 256), lambda i: (0, 0, i)),
            rows,
            pl.BlockSpec((width, 128), whole),
        ],
        out_shape=[
            jax.ShapeDtypeStruct((4, count, width), BF),
            jax.ShapeDtypeStruct((count, width), F32),
            jax.ShapeDtypeStruct((width, 128), BF),
        ],
        scratch_shapes=[pltpu.VMEM((count, width), F32), pltpu.VMEM((count, 128), F32)],
        compiler_params=pltpu.CompilerParams(vmem_limit_bytes=VMEM_LIMIT),
        cost_estimate=pl.CostEstimate(
            flops=10 * count * width * width + 12 * 40 * 2 * 128**3,
            bytes_accessed=12 * width * width,
            transcendentals=0,
        ),
        name="attention_backward",
    )(
        tokens,
        normed,
        branch,
        hidden_grad,
        ffn_gain,
        beta,
        q,
        k,
        v,
        h,
        probs,
        carried,
        inverse,
        attn,
        attn,
        attn,
        attn,
        attn,
        attn,
        attn,
    )


def weight_gradient_kernel(place_ref, core_ref, mine_x, other_x, mine_y, other_y, keep, send, xt, hold):
    @pl.when(pl.program_id(0) == 0)
    def _():
        xt[:, :128] = mine_x[...].T
        xt[:, 128:] = other_x[...].T

    height = hold.shape[1]
    chips = hold.shape[0]
    y = jnp.concatenate([mine_y[...], other_y[...]], axis=0)
    group = 8 if height == 24 else 4
    for first in range(0, chips, group):
        part = dot(xt[first * height : (first + group) * height], y)
        for chip in range(group):
            hold[first + chip] = part[chip * height : (chip + 1) * height].astype(BF)
    for place in range(chips // 2):
        keep[place] = hold[place_ref[place]]
        send[place] = hold[place_ref[place + chips // 2]]


def weight_gradient(places, core, mine_x, other_x, mine_y, other_y, height, tile, y_index, tiles):
    x_spec, mine_x, other_x = x_operand(mine_x, other_x)
    width = mine_x.shape[-1]
    count = mine_x.shape[-2]
    chips = width // height
    y_spec = pl.BlockSpec((None, count, tile), y_index)
    out = pl.BlockSpec((chips // 2, height, tile), lambda i, *_: (0, 0, i))
    shape = jax.ShapeDtypeStruct((chips // 2, height, tile * tiles), BF)
    return pl.pallas_call(
        weight_gradient_kernel,
        grid_spec=pltpu.PrefetchScalarGridSpec(
            num_scalar_prefetch=2,
            grid=(tiles,),
            in_specs=[x_spec, x_spec, y_spec, y_spec],
            out_specs=[out, out],
            scratch_shapes=[
                pltpu.VMEM((width, 2 * count), BF),
                pltpu.VMEM((chips, height, tile), BF),
            ],
        ),
        out_shape=[shape, shape],
        compiler_params=pltpu.CompilerParams(vmem_limit_bytes=VMEM_LIMIT),
        cost_estimate=pl.CostEstimate(
            flops=4 * count * width * tile * tiles,
            bytes_accessed=2 * width * tile * tiles,
            transcendentals=0,
        ),
        name="weight_gradient",
    )(places, core, mine_x, other_x, mine_y, other_y)


def x_operand(mine, other):
    if mine.ndim == 3:
        return pl.BlockSpec((None,) + mine.shape[1:], lambda i, *_: (0, 0, 0)), mine, other
    return pl.BlockSpec(mine.shape, lambda i, *_: (0, 0)), mine, other


def add_kernel(*refs):
    n = len(refs) // 6
    ins, outs = refs[: 4 * n], refs[4 * n :]
    for s in range(n):
        keep_lo, keep_hi, got_lo, got_hi = ins[4 * s : 4 * s + 4]
        outs[2 * s][...] = keep_lo[...] + got_lo[...]
        outs[2 * s + 1][...] = keep_hi[...] + got_hi[...]


def add_halves(keeps, gots):
    rows = keeps[0].shape[0] // 2
    grid = max(1, rows // 2)
    block = rows // grid
    operands, in_specs, out_specs, shapes = [], [], [], []
    for keep, got in zip(keeps, gots):
        shape = (block,) + keep.shape[1:]
        low = pl.BlockSpec(shape, lambda i: (i, 0, 0))
        high = pl.BlockSpec(shape, lambda i: (i + grid, 0, 0))
        operands += [keep, keep, got, got]
        in_specs += [low, high, low, high]
        out_specs += [low, low]
        shapes += [jax.ShapeDtypeStruct((rows,) + keep.shape[1:], BF)] * 2
    size = sum(int(np.prod(k.shape)) for k in keeps)
    outs = pl.pallas_call(
        add_kernel,
        grid=(grid,),
        in_specs=in_specs,
        out_specs=out_specs,
        out_shape=shapes,
        compiler_params=pltpu.CompilerParams(vmem_limit_bytes=VMEM_LIMIT),
        cost_estimate=pl.CostEstimate(flops=size, bytes_accessed=6 * size, transcendentals=0),
        name="add_halves",
    )(*operands)
    return outs[0::2], outs[1::2]


def send_step(value, stream, step):
    count = lax.axis_size("fsdp")
    pairs = [(d, d ^ (2 * MASKS[stream][d & 1][step])) for d in range(count)]
    return lax.ppermute(value, "fsdp", pairs)


def reduce_streams(keeps, sends):
    for step in range(6):
        gots = [send_step(send, stream, step) for stream, send in enumerate(sends)]
        if step == 5:
            return [(keep + got)[0] for keep, got in zip(keeps, gots)]
        keeps, sends = add_halves(keeps, gots)


def own_rows(block, core):
    rows = block.shape[0] // 2
    first = jnp.where(core == 0, block[:rows], block[rows:])
    second = jnp.where(core == 0, block[rows:], block[:rows])
    return first, swap(second)


def both_halves(mine, other, core):
    left = jnp.where(core == 0, mine, other)
    right = jnp.where(core == 0, other, mine)
    return jnp.concatenate([left, right], axis=1).astype(F32)


def body(
    tokens,
    lengths,
    gain_attn,
    w_query,
    w_key,
    w_value,
    w_house,
    w_beta,
    w_out,
    gain_ffn,
    w_gate,
    w_up,
    w_down,
    cotangent,
):
    seqs, count, width = tokens.shape
    heads = w_beta.shape[1]
    hidden_units = w_gate.shape[1]
    half = width // 2
    devices = lax.axis_size("fsdp")
    me = lax.axis_index("fsdp")
    core, chip = me % 2, me // 2
    offsets = jnp.asarray(owner_offsets())
    places = jnp.where(core == 0, offsets[0], offsets[1]) ^ chip
    core_at = core.astype(jnp.int32)[None]

    misc = jnp.concatenate(
        [
            w_beta,
            gain_attn[:, None],
            gain_ffn[:, None],
            jnp.zeros((w_beta.shape[0], 256 - heads - 2), BF),
        ],
        axis=1,
    )
    pack_a = jnp.concatenate([w_out[:, :half], misc, w_gate, w_query, w_key], axis=1)
    pack_b = jnp.concatenate([w_out[:, half:], misc, w_up, w_value, w_house], axis=1)
    mine = jnp.where(core == 0, pack_a, pack_b)
    theirs = swap(jnp.where(core == 0, pack_b, pack_a))
    slab = jnp.where(
        core == 0,
        jnp.concatenate([mine, theirs], axis=0),
        jnp.concatenate([theirs, mine], axis=0),
    )
    mine = jnp.where(core == 0, w_down[:, :half], w_down[:, half:])
    theirs = swap(jnp.where(core == 0, w_down[:, half:], w_down[:, :half]))
    slab_down = jnp.where(
        core == 0,
        jnp.concatenate([mine, theirs], axis=0),
        jnp.concatenate([theirs, mine], axis=0),
    )
    by_core = [[*range(0, devices, 2), *range(1, devices, 2)]]
    attn = lax.all_gather(slab, "fsdp", axis=0, tiled=True, axis_index_groups=by_core)
    down = lax.all_gather(slab_down, "fsdp", axis=0, tiled=True, axis_index_groups=by_core)

    flat = tokens.reshape(count, width)
    valid = lax.broadcasted_iota(jnp.int32, (count, 1), 0) < lengths[0]
    cot = jnp.where(valid, cotangent.reshape(count, width), jnp.zeros((), BF))
    cot_other = swap(cot)

    normed, q, k, v, h, att, probs, carried, inverse, beta = attention_forward(flat, lengths, attn)
    normed_other, att_other = swap(normed), swap(att)
    second, acts, mixed, hidden_grad, branch, ffn_gain = feedforward(
        flat, lengths, att, cot, attn, down
    )
    second_other, acts_other, branch_other = swap(second), swap(acts), swap(branch)

    unit = hidden_units // 2 // 512
    pairs = [
        weight_gradient(
            places[0],
            core_at,
            second,
            second_other,
            acts,
            acts_other,
            24,
            512,
            lambda i, _, c: (1, 0, unit * c[0] + i),
            unit,
        ),
        weight_gradient(
            places[1],
            core_at,
            second,
            second_other,
            acts,
            acts_other,
            24,
            512,
            lambda i, _, c: (2, 0, unit * c[0] + i),
            unit,
        ),
        weight_gradient(
            places[2],
            core_at,
            acts,
            acts_other,
            cot[None],
            cot_other[None],
            64,
            256,
            lambda i, _, c: (0, 0, 3 * c[0] + i),
            3,
        ),
    ]
    gate_sum, up_sum, down_sum = reduce_streams([p[0] for p in pairs], [p[1] for p in pairs])

    grads, grad_tokens, misc_grad = attention_backward(
        flat, normed, branch, hidden_grad, ffn_gain, (q, k, v, h, probs, carried, inverse, beta), attn
    )
    grads_other = swap(grads)
    tile_index = lambda first: lambda i, _, c: ((first + i) // 3, 0, 3 * c[0] + (first + i) % 3)
    qkvh = lambda stream, first, tiles: weight_gradient(
        places[stream],
        core_at,
        normed,
        normed_other,
        grads,
        grads_other,
        24,
        256,
        tile_index(first),
        tiles,
    )
    out_pair = weight_gradient(
        places[2],
        core_at,
        att,
        att_other,
        branch[None],
        branch_other[None],
        24,
        256,
        lambda i, _, c: (0, 0, 3 * c[0] + i),
        3,
    )
    misc_blocks = misc_grad.reshape(-1, 24, 128)[places[2]]
    last_pair = qkvh(2, 10, 2)
    cut = misc_blocks.shape[0] // 2
    pairs = [
        qkvh(0, 0, 5),
        qkvh(1, 5, 5),
        [
            jnp.concatenate([last_pair[0], out_pair[0], misc_blocks[:cut]], axis=2),
            jnp.concatenate([last_pair[1], out_pair[1], misc_blocks[cut:]], axis=2),
        ],
    ]
    sums = reduce_streams([p[0] for p in pairs], [p[1] for p in pairs])

    gate_up = jnp.concatenate([gate_sum, up_sum], axis=1)
    mine, other = own_rows(gate_up, core)
    part = hidden_units // 2
    grad_gate = both_halves(mine[:, :part], other[:, :part], core)
    grad_up = both_halves(mine[:, part:], other[:, part:], core)
    mine, other = own_rows(down_sum, core)
    grad_down = both_halves(mine, other, core)
    joined = jnp.concatenate(sums, axis=1)
    mine, other = own_rows(joined, core)
    small = [
        both_halves(mine[:, half * i : half * (i + 1)], other[:, half * i : half * (i + 1)], core)
        for i in range(5)
    ]
    misc_sum = mine[:, 5 * half :].astype(F32) + other[:, 5 * half :].astype(F32)
    return (
        mixed.reshape(seqs, count, width),
        grad_tokens.reshape(seqs, count, width),
        misc_sum[:, heads],
        small[0],
        small[1],
        small[2],
        small[3],
        misc_sum[:, :heads],
        small[4],
        misc_sum[:, heads + 1],
        grad_gate,
        grad_up,
        grad_down,
    )


def solution(mesh):
    rows = P("fsdp", None)
    line = P("fsdp")
    cube = P("fsdp", None, None)
    in_specs = (cube, line, line, rows, rows, rows, rows, rows, rows, line, rows, rows, rows, cube)
    out_specs = (cube, cube, line, rows, rows, rows, rows, rows, rows, line, rows, rows, rows)
    return jax.shard_map(body, mesh=mesh, in_specs=in_specs, out_specs=out_specs, check_vma=False)
```

```python
import functools

import jax
import jax.numpy as jnp
import numpy as np
from jax import lax
from jax.experimental import pallas as pl
from jax.experimental.pallas import tpu as pltpu
from jax.sharding import PartitionSpec as P

EPSILON = 1e-06
BF = jnp.bfloat16
F32 = jnp.float32
MIB = 1024 * 1024
SHORT = pl.CostEstimate(flops=1, bytes_accessed=1, transcendentals=0)
AXIS_UNIT = {"x": 16, "z": 4, "y": 1}
ORDERS = ("xzy", "zyx", "yxz")


def step_masks(stream, core):
    masks = []
    for axis in ORDERS[stream]:
        unit = AXIS_UNIT[axis]
        masks += [unit, 3 * unit] if core == 0 else [3 * unit, unit]
    return masks


MASKS = [[step_masks(stream, core) for core in (0, 1)] for stream in range(3)]


def owner_offsets():
    table = np.zeros((2, 3, 64), np.int32)
    for core in (0, 1):
        for stream in range(3):
            for place in range(64):
                value = 0
                for step, mask in enumerate(MASKS[stream][core]):
                    if (place >> (5 - step)) & 1:
                        value ^= mask
                table[core, stream, place] = value
    return table


def dot(left, right):
    return jnp.dot(left, right, preferred_element_type=F32)


def dot_nt(left, right):
    return lax.dot_general(left, right, (((1,), (1,)), ((), ())), preferred_element_type=F32)


def dot_tn(left, right):
    return lax.dot_general(left, right, (((0,), (0,)), ((), ())), preferred_element_type=F32)


def two_parts(value):
    high = value.astype(BF)
    return high, (value - high.astype(F32)).astype(BF)


def dot_fine(left, right):
    size = right.shape[1]
    wide = jnp.concatenate(two_parts(left), axis=1)
    pair = jnp.concatenate(two_parts(right), axis=1)
    out = dot(wide, jnp.concatenate([pair, pair], axis=0))
    return out[:, :size] + out[:, size:]


def swap(value):
    count = lax.axis_size("fsdp")
    return lax.ppermute(value, "fsdp", [(d, d ^ 1) for d in range(count)])


def gain_row(misc_ref, column):
    pick = (lax.broadcasted_iota(jnp.int32, (8, 128), 1) == column).astype(F32).astype(BF)
    return dot_nt(pick, misc_ref[...])[0:1]


def triangles(count):
    row = lax.broadcasted_iota(jnp.int32, (count, count), 0)
    col = lax.broadcasted_iota(jnp.int32, (count, count), 1)
    return row, col


def beta_of(raw, head):
    lane = lax.broadcasted_iota(jnp.int32, raw.shape, 1)
    return jnp.sum(jnp.where(lane == head, raw, 0.0), axis=1, keepdims=True)


def unit_lower_inverse(systems, row, col):
    size = row.shape[0]
    eye = (row == col).astype(F32)
    step = 1
    inverses = None
    while step < size:
        lower = ((row // step) % 2 == 1) & (col // step == row // step - 1)
        parts = [jnp.where(lower, system, 0.0) for system in systems]
        if step == 1:
            inverses = [eye - part for part in parts]
        else:
            middles = [dot_fine(inv, part) for inv, part in zip(inverses, parts)]
            inverses = [inv - dot_fine(mid, inv) for inv, mid in zip(inverses, middles)]
        step *= 2
    return inverses


PER_STEP = 2


def attention_forward_kernel(
    length_ref,
    tokens_ref,
    wq_ref,
    wk_ref,
    wv_ref,
    wh_ref,
    misc_ref,
    normed_t_ref,
    q_ref,
    k_ref,
    v_ref,
    h_ref,
    att_ref,
    att_t_ref,
    probs_ref,
    carried_ref,
    inverse_ref,
    beta_ref,
    normed_ref,
):
    at = pl.program_id(0)

    @pl.when(at == 0)
    def _():
        tokens = tokens_ref[...].astype(F32)
        scale = lax.rsqrt(jnp.mean(tokens * tokens, axis=1, keepdims=True) + EPSILON)
        value = tokens * scale * gain_row(misc_ref, 12)
        normed_ref[...] = value.astype(BF)
        normed_t_ref[...] = value.T.astype(BF)
        beta_ref[...] = dot(normed_ref[...], misc_ref[...])

    normed = normed_ref[...]
    q_all = dot(normed, wq_ref[...]).astype(BF)
    k_all = dot(normed, wk_ref[...]).astype(BF)
    v_all = dot(normed, wv_ref[...]).astype(BF)
    h_all = dot(normed, wh_ref[...]).astype(BF)
    q_ref[...] = q_all
    k_ref[...] = k_all
    v_ref[...] = v_all
    h_ref[...] = h_all
    count = q_all.shape[0]
    row, col = triangles(count)
    strict = row > col
    upto = row >= col
    allowed = upto & (col < length_ref[0])
    raw = beta_ref[...]
    heads = range(PER_STEP)
    q, k, v, h = (
        [value[:, 128 * i : 128 * (i + 1)] for i in heads] for value in (q_all, k_all, v_all, h_all)
    )
    big = [
        dot_nt(jnp.concatenate([h[i], q[i]], axis=0), jnp.concatenate([h[i], k[i]], axis=0))
        for i in heads
    ]
    strength = []
    for i in heads:
        house = h[i].astype(F32)
        square = jnp.sum(house * house, axis=1, keepdims=True) + EPSILON
        beta = 2.0 * jax.nn.sigmoid(beta_of(raw, at * PER_STEP + i))
        strength.append(beta / square)
    systems = [jnp.where(strict, strength[i] * big[i][:count, :count], 0.0) for i in heads]
    sources = [jnp.where(strict, strength[i] * big[i][:count, count:], 0.0) for i in heads]
    inverses = unit_lower_inverse(systems, row, col)
    carried = [dot_fine(inverses[i], sources[i]) for i in heads]
    through = [
        dot_fine(jnp.where(upto, big[i][count:, :count], 0.0), carried[i]) for i in heads
    ]
    for i in heads:
        logits = (big[i][count:, count:] - through[i]) * 128 ** (-0.5)
        logits = jnp.where(allowed, logits, -1e30)
        highest = jnp.max(logits, axis=1, keepdims=True)
        weights = jnp.where(allowed, jnp.exp(logits - highest), 0.0)
        probs = weights / jnp.sum(weights, axis=1, keepdims=True)
        probs_ref[i] = probs
        carried_ref[i] = carried[i].astype(BF)
        inverse_ref[i] = inverses[i].astype(BF)
        att = dot(probs.astype(BF), v[i])
        att_ref[:, 128 * i : 128 * (i + 1)] = att.astype(BF)
        att_t_ref[128 * i : 128 * (i + 1), :] = att.T.astype(BF)


def attention_forward(tokens, length, attn):
    count, width = tokens.shape
    steps = width // 256
    cell = (PER_STEP, count, count)
    whole = lambda i, *_: (0, 0)
    column = lambda i, *_: (0, i)
    weight = lambda half, first: pl.BlockSpec(
        (width, 256), lambda i, *_: (half, first + i)
    )
    row_block = pl.BlockSpec((count, 256), column)
    cell_block = pl.BlockSpec(cell, lambda i, *_: (i, 0, 0))
    rows = jax.ShapeDtypeStruct((count, width), BF)
    turned = jax.ShapeDtypeStruct((width, count), BF)
    cells = (2 * steps, count, count)
    return pl.pallas_call(
        attention_forward_kernel,
        grid_spec=pltpu.PrefetchScalarGridSpec(
            num_scalar_prefetch=1,
            grid=(steps,),
            in_specs=[
                pl.BlockSpec((count, width), whole),
                weight(0, 20),
                weight(0, 26),
                weight(1, 20),
                weight(1, 26),
                pl.BlockSpec((width, 128), lambda i, *_: (0, 6)),
            ],
            out_specs=[
                pl.BlockSpec((width, count), whole),
                row_block,
                row_block,
                row_block,
                row_block,
                row_block,
                pl.BlockSpec((256, count), lambda i, *_: (i, 0)),
                cell_block,
                cell_block,
                cell_block,
                pl.BlockSpec((count, 128), whole),
            ],
            scratch_shapes=[pltpu.VMEM((count, width), BF)],
        ),
        out_shape=[
            turned,
            rows,
            rows,
            rows,
            rows,
            rows,
            turned,
            jax.ShapeDtypeStruct(cells, F32),
            jax.ShapeDtypeStruct(cells, BF),
            jax.ShapeDtypeStruct(cells, BF),
            jax.ShapeDtypeStruct((count, 128), F32),
        ],
        compiler_params=pltpu.CompilerParams(vmem_limit_bytes=32 * MIB),
        cost_estimate=pl.CostEstimate(
            flops=8 * count * width * width + 12 * 60 * 2 * 128**3,
            bytes_accessed=10 * width * width,
            transcendentals=0,
        ),
        name="attention_forward",
    )(length, tokens, attn, attn, attn, attn, attn)


FF_BLOCK = 512


def feedforward_kernel(
    length_ref,
    core_ref,
    tokens_ref,
    att_ref,
    out_lo_ref,
    out_hi_ref,
    misc_ref,
    cot_ref,
    cot_own_ref,
    cot_other_ref,
    wg_ref,
    wu_ref,
    down_own_ref,
    down_other_ref,
    second_t_ref,
    product_t_ref,
    acts_ref,
    mixed_ref,
    hidden_grad_ref,
    branch_ref,
    gain_grad_ref,
    hidden,
    feed,
    second_grad,
    second_ref,
):
    at = pl.program_id(0)
    half = out_lo_ref.shape[1]

    @pl.when(at == 0)
    def _():
        att = att_ref[...]
        hidden[:, :half] = tokens_ref[:, :half].astype(F32) + dot(att, out_lo_ref[...])
        hidden[:, half:] = tokens_ref[:, half:].astype(F32) + dot(att, out_hi_ref[...])
        value = hidden[...]
        scale = lax.rsqrt(jnp.mean(value * value, axis=1, keepdims=True) + EPSILON)
        value = value * scale * gain_row(misc_ref, 13)
        second_ref[...] = value.astype(BF)
        second_t_ref[...] = value.T.astype(BF)
        feed[...] = jnp.zeros_like(feed)
        second_grad[...] = jnp.zeros_like(second_grad)

    second = second_ref[...]
    gate = dot(second, wg_ref[...])
    upward = dot(second, wu_ref[...])
    sigma = jax.nn.sigmoid(gate)
    silu = gate * sigma
    product = silu * upward
    product_t_ref[...] = product.T.astype(BF)
    product = product.astype(BF)
    product_grad = dot_nt(cot_own_ref[...], down_own_ref[...]) + dot_nt(
        cot_other_ref[...], down_other_ref[...]
    )
    gate_low = (product_grad * upward * (sigma * (1.0 + gate * (1.0 - sigma)))).astype(BF)
    up_low = (product_grad * silu).astype(BF)
    acts_ref[0] = gate_low
    acts_ref[1] = up_low
    feed[0] += dot(product, down_own_ref[...])
    feed[1] += dot(product, down_other_ref[...])
    second_grad[...] += dot_nt(gate_low, wg_ref[...]) + dot_nt(up_low, wu_ref[...])

    @pl.when(at == pl.num_programs(0) - 1)
    def _():
        value = hidden[...]
        valid = lax.broadcasted_iota(jnp.int32, value.shape, 0) < length_ref[0]
        fed = jnp.concatenate([feed[core_ref[0]], feed[1 - core_ref[0]]], axis=1)
        mixed_ref[...] = jnp.where(valid, value + fed, 0.0).astype(BF)
        scale = lax.rsqrt(jnp.mean(value * value, axis=1, keepdims=True) + EPSILON)
        grad = second_grad[...]
        scaled = grad * gain_row(misc_ref, 13)
        along = jnp.mean(scaled * value, axis=1, keepdims=True)
        hidden_grad = (
            cot_ref[...].astype(F32) + scale * scaled - value * (scale * scale * scale * along)
        )
        hidden_grad_ref[...] = hidden_grad
        branch_ref[...] = hidden_grad.astype(BF)
        gain_grad_ref[...] = jnp.sum(grad * value * scale, axis=0, keepdims=True)


def feedforward(tokens, length, core, att, cots, attn, downs):
    count, width = tokens.shape
    hidden_units = downs[0].shape[0]
    steps = hidden_units // FF_BLOCK
    half = width // 2
    whole = lambda i, *_: (0, 0)
    rows = pl.BlockSpec((count, width), whole)
    weight = lambda side: pl.BlockSpec(
        (width, FF_BLOCK), lambda i, *_: (side, 1024 // FF_BLOCK + i)
    )
    down_block = pl.BlockSpec((FF_BLOCK, half), lambda i, *_: (i, 0))
    return pl.pallas_call(
        feedforward_kernel,
        grid_spec=pltpu.PrefetchScalarGridSpec(
            num_scalar_prefetch=2,
            grid=(steps,),
            in_specs=[
                rows,
                rows,
                pl.BlockSpec((width, half), whole),
                pl.BlockSpec((width, half), lambda i, *_: (1, 0)),
                pl.BlockSpec((width, 128), lambda i, *_: (0, 6)),
                rows,
                pl.BlockSpec((count, half), whole),
                pl.BlockSpec((count, half), whole),
                weight(0),
                weight(1),
                down_block,
                down_block,
            ],
            out_specs=[
                pl.BlockSpec((width, count), whole),
                pl.BlockSpec((FF_BLOCK, count), lambda i, *_: (i, 0)),
                pl.BlockSpec((2, count, FF_BLOCK), lambda i, *_: (0, 0, i)),
                rows,
                rows,
                rows,
                pl.BlockSpec((1, width), whole),
            ],
            scratch_shapes=[
                pltpu.VMEM((count, width), F32),
                pltpu.VMEM((2, count, half), F32),
                pltpu.VMEM((count, width), F32),
                pltpu.VMEM((count, width), BF),
            ],
        ),
        out_shape=[
            jax.ShapeDtypeStruct((width, count), BF),
            jax.ShapeDtypeStruct((hidden_units, count), BF),
            jax.ShapeDtypeStruct((2, count, hidden_units), BF),
            jax.ShapeDtypeStruct((count, width), BF),
            jax.ShapeDtypeStruct((count, width), F32),
            jax.ShapeDtypeStruct((count, width), BF),
            jax.ShapeDtypeStruct((1, width), F32),
        ],
        compiler_params=pltpu.CompilerParams(vmem_limit_bytes=48 * MIB),
        cost_estimate=pl.CostEstimate(
            flops=12 * count * width * hidden_units,
            bytes_accessed=6 * width * hidden_units,
            transcendentals=0,
        ),
        name="feedforward",
    )(length, core, tokens, att, attn, attn, attn, *cots, attn, attn, *downs)


def attention_backward_kernel(
    tokens_ref,
    normed_t_ref,
    branch_ref,
    hidden_grad_ref,
    ffn_gain_ref,
    beta_ref,
    q_ref,
    k_ref,
    v_ref,
    h_ref,
    probs_ref,
    carried_ref,
    inverse_ref,
    wo_lo_ref,
    wo_hi_ref,
    wq_ref,
    wk_ref,
    wv_ref,
    wh_ref,
    misc_ref,
    grads_ref,
    grad_tokens_ref,
    misc_grad_ref,
    normed_grad,
    beta_grad,
):
    at = pl.program_id(0)
    half = wo_lo_ref.shape[1]

    @pl.when(at == 0)
    def _():
        normed_grad[...] = jnp.zeros_like(normed_grad)
        beta_grad[...] = jnp.zeros_like(beta_grad)

    att_grad_all = (
        dot_nt(branch_ref[:, :half], wo_lo_ref[...]) + dot_nt(branch_ref[:, half:], wo_hi_ref[...])
    ).astype(BF)
    count = att_grad_all.shape[0]
    row, col = triangles(count)
    strict = row > col
    upto = row >= col
    raw = beta_ref[...]
    lane = lax.broadcasted_iota(jnp.int32, raw.shape, 1)
    heads = range(PER_STEP)
    part = lambda ref: [ref[:, 128 * i : 128 * (i + 1)] for i in heads]
    q, k, v, h = part(q_ref), part(k_ref), part(v_ref), part(h_ref)
    att_grad = [att_grad_all[:, 128 * i : 128 * (i + 1)] for i in heads]
    big = [
        dot_nt(jnp.concatenate([h[i], q[i]], axis=0), jnp.concatenate([h[i], k[i]], axis=0))
        for i in heads
    ]
    probs = [probs_ref[i] for i in heads]
    carried = [carried_ref[i] for i in heads]
    inverse = [inverse_ref[i] for i in heads]
    probs_grad = [dot_nt(att_grad[i], v[i]) for i in heads]
    value_grad = [dot_tn(probs[i].astype(BF), att_grad[i]) for i in heads]
    logit_grad = []
    for i in heads:
        total = jnp.sum(probs_grad[i] * probs[i], axis=1, keepdims=True)
        logit_grad.append((probs[i] * (probs_grad[i] - total) * 128 ** (-0.5)).astype(BF))
    through_grad = [
        jnp.where(upto, -dot_nt(logit_grad[i], carried[i]), 0.0).astype(BF) for i in heads
    ]
    carried_grad = [
        -dot_tn(jnp.where(upto, big[i][count:, :count], 0.0).astype(BF), logit_grad[i])
        for i in heads
    ]
    solved = [dot_tn(inverse[i], carried_grad[i].astype(BF)) for i in heads]
    system_grad = [
        jnp.where(strict, -dot_nt(solved[i].astype(BF), carried[i]), 0.0) for i in heads
    ]
    source_grad = [jnp.where(strict, solved[i], 0.0) for i in heads]
    total_beta = jnp.zeros_like(raw)
    q_grads, k_grads, v_grads, h_grads = [], [], [], []
    for i in heads:
        house = h[i].astype(F32)
        inverse_square = 1.0 / (jnp.sum(house * house, axis=1, keepdims=True) + EPSILON)
        sigma = jax.nn.sigmoid(beta_of(raw, at * PER_STEP + i))
        strength = 2.0 * sigma * inverse_square
        key_part = (strength * source_grad[i]).astype(BF)
        self_part = (strength * system_grad[i]).astype(BF)
        strength_grad = jnp.sum(
            source_grad[i] * big[i][:count, count:] + system_grad[i] * big[i][:count, :count],
            axis=1,
            keepdims=True,
        )
        key_house = jnp.concatenate([k[i], h[i]], axis=0)
        query_house = jnp.concatenate([q[i], h[i]], axis=0)
        q_grads.append(
            dot(jnp.concatenate([logit_grad[i], through_grad[i]], axis=1), key_house).astype(BF)
        )
        k_grads.append(
            dot_tn(jnp.concatenate([logit_grad[i], key_part], axis=0), query_house).astype(BF)
        )
        house_grad = (
            dot_tn(jnp.concatenate([through_grad[i], self_part], axis=0), query_house)
            + dot(jnp.concatenate([key_part, self_part], axis=1), key_house)
            - (2.0 * strength_grad * strength * inverse_square) * house
        )
        h_grads.append(house_grad.astype(BF))
        v_grads.append(value_grad[i].astype(BF))
        raw_grad = strength_grad * inverse_square * (2.0 * sigma * (1.0 - sigma))
        total_beta += jnp.where(lane == at * PER_STEP + i, raw_grad, 0.0)
    beta_grad[...] += total_beta
    update = None
    for index, (pieces, weight_ref) in enumerate(
        ((q_grads, wq_ref), (k_grads, wk_ref), (v_grads, wv_ref), (h_grads, wh_ref))
    ):
        joined = jnp.concatenate(pieces, axis=1)
        grads_ref[index] = joined
        term = dot_nt(joined, weight_ref[...])
        update = term if update is None else update + term
    normed_grad[...] += update

    @pl.when(at == pl.num_programs(0) - 1)
    def _():
        beta_low = beta_grad[...].astype(BF)
        grad = normed_grad[...] + dot_nt(beta_low, misc_ref[...])
        value = tokens_ref[...].astype(F32)
        scale = lax.rsqrt(jnp.mean(value * value, axis=1, keepdims=True) + EPSILON)
        scaled = grad * gain_row(misc_ref, 12)
        along = jnp.mean(scaled * value, axis=1, keepdims=True)
        grad_tokens_ref[...] = (
            hidden_grad_ref[...] + scale * scaled - value * (scale * scale * scale * along)
        )
        attn_gain = jnp.sum(grad * value * scale, axis=0, keepdims=True)
        attn_high, attn_low = two_parts(attn_gain)
        ffn_high, ffn_low = two_parts(ffn_gain_ref[...])
        gains = jnp.concatenate(
            [
                attn_high.astype(F32),
                attn_low.astype(F32),
                ffn_high.astype(F32),
                ffn_low.astype(F32),
                jnp.zeros((4, attn_gain.shape[1]), F32),
            ],
            axis=0,
        )
        place = lax.broadcasted_iota(jnp.int32, (8, 128), 0)
        lanes = lax.broadcasted_iota(jnp.int32, (8, 128), 1)
        pick = ((place < 4) & (lanes == 12 + place // 2)).astype(F32)
        misc_grad = dot(normed_t_ref[...], beta_low) + dot_tn(
            gains.astype(BF), pick.astype(BF)
        )
        misc_grad_ref[...] = misc_grad.astype(BF)


def attention_backward(tokens, normed_t, branch, hidden_grad, ffn_gain, saved, attn):
    q, k, v, h, probs, carried, inverse, beta = saved
    count, width = tokens.shape
    steps = width // 256
    half = width // 2
    whole = lambda i: (0, 0)
    rows = pl.BlockSpec((count, width), whole)
    row_block = pl.BlockSpec((count, 256), lambda i: (0, i))
    cell_block = pl.BlockSpec((PER_STEP, count, count), lambda i: (i, 0, 0))
    weight = lambda side, first: pl.BlockSpec((width, 256), lambda i: (side, first + i))
    out_rows = lambda side: pl.BlockSpec((256, half), lambda i: (side * steps + i, 0))
    return pl.pallas_call(
        attention_backward_kernel,
        grid=(steps,),
        in_specs=[
            rows,
            pl.BlockSpec((width, count), whole),
            rows,
            rows,
            pl.BlockSpec((1, width), whole),
            pl.BlockSpec((count, 128), whole),
            row_block,
            row_block,
            row_block,
            row_block,
            cell_block,
            cell_block,
            cell_block,
            out_rows(0),
            out_rows(1),
            weight(0, 20),
            weight(0, 26),
            weight(1, 20),
            weight(1, 26),
            pl.BlockSpec((width, 128), lambda i: (0, 6)),
        ],
        out_specs=[
            pl.BlockSpec((4, count, 256), lambda i: (0, 0, i)),
            rows,
            pl.BlockSpec((width, 128), whole),
        ],
        out_shape=[
            jax.ShapeDtypeStruct((4, count, width), BF),
            jax.ShapeDtypeStruct((count, width), F32),
            jax.ShapeDtypeStruct((width, 128), BF),
        ],
        scratch_shapes=[pltpu.VMEM((count, width), F32), pltpu.VMEM((count, 128), F32)],
        compiler_params=pltpu.CompilerParams(vmem_limit_bytes=40 * MIB),
        cost_estimate=SHORT,
        name="attention_backward",
    )(
        tokens,
        normed_t,
        branch,
        hidden_grad,
        ffn_gain,
        beta,
        q,
        k,
        v,
        h,
        probs,
        carried,
        inverse,
        attn,
        attn,
        attn,
        attn,
        attn,
        attn,
        attn,
    )


def weight_gradient_kernel(segments, n_x, n_y, has_misc, second_half, *refs):
    place_ref, refs = refs[0], refs[2:]
    xs = [(refs[2 * i], refs[2 * i + 1]) for i in range(n_x)]
    refs = refs[2 * n_x :]
    ys = [(refs[2 * i], refs[2 * i + 1]) for i in range(n_y)]
    refs = refs[2 * n_y :]
    misc_ref = None
    if has_misc:
        misc_ref, refs = refs[0], refs[1:]
    at = pl.program_id(0)
    chips, height = xs[0][0].shape[0], xs[0][0].shape[1]
    if second_half:
        spots = [(refs[0], None, i, chips // 2 + 8 * at + i) for i in range(8)]
    else:
        got_lo, got_hi, keep, send = refs
        spots = [(keep, got_lo, i, 4 * at + i) for i in range(4)]
        spots += [(send, got_hi, i, chips // 4 + 4 * at + i) for i in range(4)]
    owners = [place_ref[spot[3]] for spot in spots]
    lefts = []
    for mine, other in xs:
        rows = [
            jnp.concatenate([mine[owner].astype(F32), other[owner].astype(F32)], axis=1)
            for owner in owners
        ]
        lefts.append(jnp.concatenate(rows, axis=0).astype(BF))
    done = 0
    for x_at, y_at, matrix, start, size in segments:
        mine, other = ys[y_at]
        columns = slice(start, start + size)
        part = dot(
            lefts[x_at],
            jnp.concatenate([mine[matrix, :, columns], other[matrix, :, columns]], axis=0),
        )
        for index, (out, got, i, _) in enumerate(spots):
            value = part[index * height : (index + 1) * height]
            if got is not None:
                value = value + got[i, :, done : done + size].astype(F32)
            out[i, :, done : done + size] = value.astype(BF)
        done += size
    if has_misc:
        for (out, got, i, _), owner in zip(spots, owners):
            value = misc_ref[owner].astype(F32)
            if got is not None:
                value = value + got[i, :, done:].astype(F32)
            out[i, :, done:] = value.astype(BF)


def weight_gradient(places, core, xs, ys, segments, misc=None, got=None):
    chips, height, count = xs[0][0].shape
    columns = sum(segment[4] for segment in segments) + (128 if misc is not None else 0)
    operands, in_specs = [], []
    for mine, other in xs:
        operands += [mine, other]
        in_specs += [pl.BlockSpec(mine.shape, lambda i, *_: (0, 0, 0))] * 2
    for mine, other in ys:
        operands += [mine, other]
        half = (mine.shape[0], mine.shape[1], mine.shape[2] // 2)
        in_specs += [pl.BlockSpec(half, lambda i, _, c: (0, 0, c[0]))] * 2
    if misc is not None:
        operands.append(misc)
        in_specs.append(pl.BlockSpec(misc.shape, lambda i, *_: (0, 0, 0)))
    steps = chips // 16
    if got is None:
        out_specs = [pl.BlockSpec((8, height, columns), lambda i, *_: (i, 0, 0))]
        out_shape = [jax.ShapeDtypeStruct((chips // 2, height, columns), BF)]
    else:
        block = (4, height, columns)
        operands += [got, got]
        in_specs += [
            pl.BlockSpec(block, lambda i, *_: (i, 0, 0)),
            pl.BlockSpec(block, lambda i, *_: (steps + i, 0, 0)),
        ]
        out_specs = [pl.BlockSpec(block, lambda i, *_: (i, 0, 0))] * 2
        out_shape = [jax.ShapeDtypeStruct((chips // 4, height, columns), BF)] * 2
    return pl.pallas_call(
        functools.partial(
            weight_gradient_kernel, segments, len(xs), len(ys), misc is not None, got is None
        ),
        grid_spec=pltpu.PrefetchScalarGridSpec(
            num_scalar_prefetch=2, grid=(steps,), in_specs=in_specs, out_specs=out_specs
        ),
        out_shape=out_shape,
        compiler_params=pltpu.CompilerParams(vmem_limit_bytes=32 * MIB),
        cost_estimate=SHORT,
        name="weight_gradient" if got is None else "weight_gradient_add",
    )(places, core, *operands)


def add_kernel(widths, *refs):
    total = sum(len(group) for group in widths)
    ins, outs = refs[: 4 * total], refs[4 * total :]
    at = 0
    for index, group in enumerate(widths):
        start = 0
        for width in group:
            keep_lo, keep_hi, got_lo, got_hi = ins[4 * at : 4 * at + 4]
            columns = slice(start, start + width)
            outs[2 * index][:, :, columns] = keep_lo[...] + got_lo[...]
            outs[2 * index + 1][:, :, columns] = keep_hi[...] + got_hi[...]
            start += width
            at += 1


def add_halves(groups):
    rows = groups[0][0][0].shape[0] // 2
    grid = max(1, rows // 2)
    block = rows // grid
    operands, in_specs, out_specs, shapes, widths = [], [], [], [], []
    for group in groups:
        for keep, got in group:
            shape = (block,) + keep.shape[1:]
            low = pl.BlockSpec(shape, lambda i: (i, 0, 0))
            high = pl.BlockSpec(shape, lambda i: (i + grid, 0, 0))
            operands += [keep, keep, got, got]
            in_specs += [low, high, low, high]
        widths.append([keep.shape[2] for keep, _ in group])
        shape = (block, group[0][0].shape[1], sum(widths[-1]))
        out_specs += [pl.BlockSpec(shape, lambda i: (i, 0, 0))] * 2
        shapes += [jax.ShapeDtypeStruct((rows,) + shape[1:], BF)] * 2
    outs = pl.pallas_call(
        functools.partial(add_kernel, widths),
        grid=(grid,),
        in_specs=in_specs,
        out_specs=out_specs,
        out_shape=shapes,
        compiler_params=pltpu.CompilerParams(vmem_limit_bytes=24 * MIB),
        cost_estimate=SHORT,
        name="add_halves",
    )(*operands)
    return outs[0::2], outs[1::2]


def last_add_kernel(core_ref, *refs):
    first = core_ref[0] == 0
    *ins, mine, theirs, mine_down, theirs_down = refs
    start = 0
    for index in range(0, len(ins), 2):
        value = ins[index][0].astype(F32) + ins[index + 1][0].astype(F32)
        height, width = value.shape
        low, high = value[: height // 2], value[height // 2 :]
        own, other = jnp.where(first, low, high), jnp.where(first, high, low)
        if height == 24:
            mine[:, start : start + width] = own
            theirs[:, start : start + width] = other.astype(BF)
            start += width
        else:
            mine_down[...] = own
            theirs_down[...] = other.astype(BF)


def last_add(core, pairs):
    flat = [value for pair in pairs for value in pair]
    width = sum(keep.shape[2] for keep, _ in pairs if keep.shape[1] == 24)
    down = next(keep for keep, _ in pairs if keep.shape[1] != 24)
    shapes = [(12, width), (12, width)] + [(down.shape[1] // 2, down.shape[2])] * 2
    return pl.pallas_call(
        last_add_kernel,
        grid_spec=pltpu.PrefetchScalarGridSpec(
            num_scalar_prefetch=1,
            grid=(1,),
            in_specs=[pl.BlockSpec(v.shape, lambda i, _: (0, 0, 0)) for v in flat],
            out_specs=[pl.BlockSpec(shape, lambda i, _: (0, 0)) for shape in shapes],
        ),
        out_shape=[jax.ShapeDtypeStruct(s, t) for s, t in zip(shapes, (F32, BF, F32, BF))],
        compiler_params=pltpu.CompilerParams(vmem_limit_bytes=16 * MIB),
        cost_estimate=SHORT,
        name="last_add",
    )(core, *flat)


PLACES = (
    ((2048, 768),),
    ((2816, 512), (5376, 256)),
    ((5632, 768),),
    ((6400, 256), (6656, 512)),
    ((7168, 768),),
    ((0, 2048),),
    ((3328, 2048),),
)


def finish_kernel(core_ref, mine, other, mine_down, other_down, *outs):
    first = core_ref[0] == 0
    for pieces, out in zip(PLACES, outs):
        half = out.shape[1] // 2
        done = 0
        for start, width in pieces:
            a = mine[:, start : start + width]
            b = other[:, start : start + width].astype(F32)
            out[:, done : done + width] = jnp.where(first, a, b)
            out[:, half + done : half + done + width] = jnp.where(first, b, a)
            done += width
    a, b = mine_down[...], other_down[...].astype(F32)
    half = a.shape[1]
    outs[7][:, :half] = jnp.where(first, a, b)
    outs[7][:, half:] = jnp.where(first, b, a)
    outs[8][...] = mine[:, 7936:] + other[:, 7936:].astype(F32)


def finish(core, mine, other, mine_down, other_down):
    rows, down_rows = mine.shape[0], mine_down.shape[0]
    shapes = [(rows, 2 * sum(w for _, w in pieces)) for pieces in PLACES]
    shapes += [(down_rows, 2 * mine_down.shape[1]), (rows, 128)]
    operands = (mine, other, mine_down, other_down)
    return pl.pallas_call(
        finish_kernel,
        grid_spec=pltpu.PrefetchScalarGridSpec(
            num_scalar_prefetch=1,
            grid=(1,),
            in_specs=[pl.BlockSpec(v.shape, lambda i, _: (0, 0)) for v in operands],
            out_specs=[pl.BlockSpec(shape, lambda i, _: (0, 0)) for shape in shapes],
        ),
        out_shape=[jax.ShapeDtypeStruct(shape, F32) for shape in shapes],
        compiler_params=pltpu.CompilerParams(vmem_limit_bytes=16 * MIB),
        cost_estimate=SHORT,
        name="finish",
    )(core, *operands)


def send_step(value, stream, step):
    count = lax.axis_size("fsdp")
    pairs = [(d, d ^ (2 * MASKS[stream][d & 1][step])) for d in range(count)]
    return lax.ppermute(value, "fsdp", pairs)


def after(values, earlier):
    flat, tree = jax.tree.flatten(values)
    kept = lax.optimization_barrier((*flat, *jax.tree.leaves(earlier)))
    return jax.tree.unflatten(tree, kept[: len(flat)])


def exchange(sends, step, streams=(0, 1, 2)):
    return [send_step(send, stream, step) for stream, send in zip(streams, sends)]


def blocks(turned, height):
    return turned.reshape(turned.shape[0] // height, height, turned.shape[1])


def gather_streams(parts):
    for step in range(5, -1, -1):
        gots = [send_step(part, stream, step) for stream, part in enumerate(parts)]
        parts = [jnp.concatenate(pair, axis=0) for pair in zip(parts, gots)]
    return parts


def in_order_kernel(place_ref, *refs):
    streams, out = refs[:-1], refs[-1]
    width = streams[0].shape[2]
    for index, stream in enumerate(streams):
        for place in range(stream.shape[0]):
            out[place_ref[index, place], :, index * width : (index + 1) * width] = stream[place]


def in_order(places, streams):
    chips, height, width = streams[0].shape
    shape = (chips, height, width * len(streams))
    return pl.pallas_call(
        in_order_kernel,
        grid_spec=pltpu.PrefetchScalarGridSpec(
            num_scalar_prefetch=1,
            grid=(1,),
            in_specs=[pl.BlockSpec(s.shape, lambda i, _: (0, 0, 0)) for s in streams],
            out_specs=pl.BlockSpec(shape, lambda i, _: (0, 0, 0)),
        ),
        out_shape=jax.ShapeDtypeStruct(shape, BF),
        compiler_params=pltpu.CompilerParams(vmem_limit_bytes=40 * MIB),
        cost_estimate=SHORT,
        name="in_order",
    )(places, *streams)


def body(
    tokens,
    lengths,
    gain_attn,
    w_query,
    w_key,
    w_value,
    w_house,
    w_beta,
    w_out,
    gain_ffn,
    w_gate,
    w_up,
    w_down,
    cotangent,
):
    seqs, count, width = tokens.shape
    heads = w_beta.shape[1]
    hidden_units = w_gate.shape[1]
    half = width // 2
    devices = lax.axis_size("fsdp")
    me = lax.axis_index("fsdp")
    core, chip = me % 2, me // 2
    offsets = jnp.asarray(owner_offsets())
    places = jnp.where(core == 0, offsets[0], offsets[1]) ^ chip
    core_at = core.astype(jnp.int32)[None]

    misc = jnp.concatenate(
        [
            w_beta,
            gain_attn[:, None],
            gain_ffn[:, None],
            jnp.zeros((w_beta.shape[0], 256 - heads - 2), BF),
        ],
        axis=1,
    )
    pack_a = jnp.concatenate([w_out[:, :half], misc, w_gate, w_query, w_key], axis=1)
    pack_b = jnp.concatenate([w_out[:, half:], misc, w_up, w_value, w_house], axis=1)
    mine = jnp.where(core == 0, pack_a, pack_b)
    theirs = swap(jnp.where(core == 0, pack_b, pack_a))
    slab = jnp.where(
        core == 0,
        jnp.concatenate([mine, theirs], axis=0),
        jnp.concatenate([theirs, mine], axis=0),
    )
    mine = jnp.where(core == 0, w_down[:, :half], w_down[:, half:])
    theirs = swap(jnp.where(core == 0, w_down[:, half:], w_down[:, :half]))
    slab_down = jnp.where(
        core == 0,
        jnp.concatenate([mine, theirs], axis=0),
        jnp.concatenate([theirs, mine], axis=0),
    )
    by_core = [[*range(0, devices, 2), *range(1, devices, 2)]]
    attn = lax.all_gather(slab, "fsdp", axis=0, tiled=True, axis_index_groups=by_core)
    third = half // 3
    streams = gather_streams([slab_down[None, :, third * i : third * (i + 1)] for i in range(3)])
    down_own = in_order(places, streams).reshape(hidden_units, half)
    downs = (down_own, swap(down_own))

    flat = tokens.reshape(count, width)
    valid = lax.broadcasted_iota(jnp.int32, (count, 1), 0) < lengths[0]
    cot = jnp.where(valid, cotangent.reshape(count, width), jnp.zeros((), BF))
    cot_other = swap(cot)

    normed_t, q, k, v, h, att, att_t, probs, carried, inverse, beta = attention_forward(
        flat, lengths, attn
    )
    normed_x, att_x = (
        (blocks(value, 24), blocks(swap(value), 24)) for value in (normed_t, att_t)
    )
    cots = (
        cot,
        jnp.where(core == 0, cot[:, :half], cot[:, half:]),
        jnp.where(core == 0, cot[:, half:], cot[:, :half]),
    )
    second_t, product_t, acts, mixed, hidden_grad, branch, ffn_gain = feedforward(
        flat, lengths, core_at, att, cots, attn, downs
    )
    second_x = (blocks(second_t, 24), blocks(swap(second_t), 24))
    product_x = (blocks(product_t, 64), blocks(swap(product_t), 64))
    acts_y = (acts, swap(acts))
    cot_y = (cot[None], cot_other[None])
    branch_y = (branch[None], swap(branch)[None])

    part = hidden_units // 2
    jobs = [
        ([second_x], [acts_y], [(0, 0, 0, 0, part)]),
        ([second_x], [acts_y], [(0, 0, 1, 0, part)]),
        ([product_x], [cot_y], [(0, 0, 0, 0, half)]),
    ]
    sends = [weight_gradient(places[s], core_at, *job)[0] for s, job in enumerate(jobs)]
    gots = exchange(sends, 0)
    branch = after(branch, sends)

    grads, grad_tokens, misc_grad = attention_backward(
        flat, normed_t, branch, hidden_grad, ffn_gain, (q, k, v, h, probs, carried, inverse, beta), attn
    )
    grads_y = (grads, swap(grads))
    misc_x = misc_grad.reshape(-1, 24, 128)
    attn_jobs = [
        ([normed_x], [grads_y], [(0, 0, 0, 0, 768), (0, 0, 1, 0, 512)]),
        ([normed_x], [grads_y], [(0, 0, 1, 512, 256), (0, 0, 2, 0, 768), (0, 0, 3, 0, 256)]),
        ([normed_x, att_x], [grads_y, branch_y], [(0, 0, 3, 256, 512), (1, 1, 0, 0, 768)], misc_x),
    ]
    attn_sends = [
        weight_gradient(after(places[s], gots[s]), core_at, *job)[0]
        for s, job in enumerate(attn_jobs)
    ]
    attn_gots = exchange(attn_sends, 0)

    def kept(jobs, gots):
        pairs = [
            weight_gradient(places[s], core_at, *job, got=gots[s]) for s, job in enumerate(jobs)
        ]
        return [p[0] for p in pairs], [p[1] for p in pairs]

    keeps, sends = kept(jobs, gots)
    gots = exchange(sends, 1)
    attn_keeps, attn_sends = kept(attn_jobs, [after(got, keeps) for got in attn_gots])
    attn_gots = exchange(attn_sends, 1)
    first, second = list(zip(keeps, gots)), list(zip(attn_keeps, attn_gots))
    groups = [[first[0], second[0]], [first[1], second[1]], [first[2]], [second[2]]]
    for step in range(2, 6):
        keeps, sends = add_halves(groups)
        gots = exchange(sends, step, (0, 1, 2, 2))
        groups = [[pair] for pair in zip(keeps, gots)]
    mine, theirs, mine_down, theirs_down = last_add(core_at, [group[0] for group in groups])
    *large, misc_sum = finish(core_at, mine, swap(theirs), mine_down, swap(theirs_down))

    return (
        mixed.reshape(seqs, count, width),
        grad_tokens.reshape(seqs, count, width),
        misc_sum[:, heads],
        *large[:4],
        misc_sum[:, :heads],
        large[4],
        misc_sum[:, heads + 1],
        *large[5:],
    )


def solution(mesh):
    rows = P("fsdp", None)
    line = P("fsdp")
    cube = P("fsdp", None, None)
    in_specs = (cube, line, line, rows, rows, rows, rows, rows, rows, line, rows, rows, rows, cube)
    out_specs = (cube, cube, line, rows, rows, rows, rows, rows, rows, line, rows, rows, rows)
    return jax.shard_map(body, mesh=mesh, in_specs=in_specs, out_specs=out_specs, check_vma=False)
```

```python
import functools

import jax
import jax.numpy as jnp
import numpy as np
from jax import lax
from jax.experimental import pallas as pl
from jax.experimental.pallas import tpu as pltpu
from jax.sharding import PartitionSpec as P

EPSILON = 1e-06
BF = jnp.bfloat16
F32 = jnp.float32
MIB = 1024 * 1024
SHORT = pl.CostEstimate(flops=1, bytes_accessed=1, transcendentals=0)
AXIS_UNIT = {"x": 16, "z": 4, "y": 1}
ORDERS = ("xzy", "zyx", "yxz")


def step_masks(stream, core):
    masks = []
    for axis in ORDERS[stream]:
        unit = AXIS_UNIT[axis]
        masks += [unit, 3 * unit] if core == 0 else [3 * unit, unit]
    return masks


MASKS = [[step_masks(stream, core) for core in (0, 1)] for stream in range(3)]


def owner_offsets():
    table = np.zeros((2, 3, 64), np.int32)
    for core in (0, 1):
        for stream in range(3):
            for place in range(64):
                value = 0
                for step, mask in enumerate(MASKS[stream][core]):
                    if (place >> (5 - step)) & 1:
                        value ^= mask
                table[core, stream, place] = value
    return table


def dot(left, right):
    return jnp.dot(left, right, preferred_element_type=F32)


def dot_nt(left, right):
    return lax.dot_general(left, right, (((1,), (1,)), ((), ())), preferred_element_type=F32)


def dot_tn(left, right):
    return lax.dot_general(left, right, (((0,), (0,)), ((), ())), preferred_element_type=F32)


def two_parts(value):
    high = value.astype(BF)
    return high, (value - high.astype(F32)).astype(BF)


def dot_fine(left, right):
    size = right.shape[1]
    wide = jnp.concatenate(two_parts(left), axis=1)
    pair = jnp.concatenate(two_parts(right), axis=1)
    out = dot(wide, jnp.concatenate([pair, pair], axis=0))
    return out[:, :size] + out[:, size:]


def swap(value):
    count = lax.axis_size("fsdp")
    return lax.ppermute(value, "fsdp", [(d, d ^ 1) for d in range(count)])


def gain_row(misc_ref, column):
    pick = (lax.broadcasted_iota(jnp.int32, (8, 128), 1) == column).astype(F32).astype(BF)
    return dot_nt(pick, misc_ref[...])[0:1]


def triangles(count):
    row = lax.broadcasted_iota(jnp.int32, (count, count), 0)
    col = lax.broadcasted_iota(jnp.int32, (count, count), 1)
    return row, col


def beta_of(raw, head):
    lane = lax.broadcasted_iota(jnp.int32, raw.shape, 1)
    return jnp.sum(jnp.where(lane == head, raw, 0.0), axis=1, keepdims=True)


def unit_lower_inverse(systems, row, col):
    size = row.shape[0]
    eye = (row == col).astype(F32)
    step = 1
    inverses = None
    while step < size:
        lower = ((row // step) % 2 == 1) & (col // step == row // step - 1)
        parts = [jnp.where(lower, system, 0.0) for system in systems]
        if step == 1:
            inverses = [eye - part for part in parts]
        else:
            middles = [dot_fine(inv, part) for inv, part in zip(inverses, parts)]
            inverses = [inv - dot_fine(mid, inv) for inv, mid in zip(inverses, middles)]
        step *= 2
    return inverses


PER_STEP = 4
SPAN = 128 * PER_STEP
GATE_AT, UP_AT, FIRST_AT, SECOND_AT = 1024, 3072, 5120, 6656


def attention_forward_kernel(
    length_ref,
    tokens_ref,
    wq_ref,
    wk_ref,
    wv_ref,
    wh_ref,
    out_lo_ref,
    out_hi_ref,
    misc_ref,
    normed_t_ref,
    q_ref,
    k_ref,
    v_ref,
    h_ref,
    hidden_ref,
    second_ref,
    att_t_ref,
    probs_ref,
    carried_ref,
    inverse_ref,
    beta_ref,
    gain_ref,
    normed_ref,
):
    at = pl.program_id(0)

    @pl.when(at == 0)
    def _():
        tokens = tokens_ref[...].astype(F32)
        scale = lax.rsqrt(jnp.mean(tokens * tokens, axis=1, keepdims=True) + EPSILON)
        value = tokens * scale * gain_row(misc_ref, 12)
        normed_ref[...] = value.astype(BF)
        normed_t_ref[...] = value.T.astype(BF)
        beta_ref[...] = dot(normed_ref[...], misc_ref[...])
        hidden_ref[...] = tokens

    normed = normed_ref[...]
    q_all = dot(normed, wq_ref[...]).astype(BF)
    k_all = dot(normed, wk_ref[...]).astype(BF)
    v_all = dot(normed, wv_ref[...]).astype(BF)
    h_all = dot(normed, wh_ref[...]).astype(BF)
    q_ref[...] = q_all
    k_ref[...] = k_all
    v_ref[...] = v_all
    h_ref[...] = h_all
    count = q_all.shape[0]
    row, col = triangles(count)
    strict = row > col
    upto = row >= col
    allowed = upto & (col < length_ref[0])
    raw = beta_ref[...]
    heads = range(PER_STEP)
    q, k, v, h = (
        [value[:, 128 * i : 128 * (i + 1)] for i in heads] for value in (q_all, k_all, v_all, h_all)
    )
    big = [
        dot_nt(jnp.concatenate([h[i], q[i]], axis=0), jnp.concatenate([h[i], k[i]], axis=0))
        for i in heads
    ]
    strength = []
    for i in heads:
        house = h[i].astype(F32)
        square = jnp.sum(house * house, axis=1, keepdims=True) + EPSILON
        beta = 2.0 * jax.nn.sigmoid(beta_of(raw, at * PER_STEP + i))
        strength.append(beta / square)
    systems = [jnp.where(strict, strength[i] * big[i][:count, :count], 0.0) for i in heads]
    sources = [jnp.where(strict, strength[i] * big[i][:count, count:], 0.0) for i in heads]
    inverses = unit_lower_inverse(systems, row, col)
    carried = [dot_fine(inverses[i], sources[i]) for i in heads]
    through = [
        dot_fine(jnp.where(upto, big[i][count:, :count], 0.0), carried[i]) for i in heads
    ]
    attended = []
    for i in heads:
        logits = (big[i][count:, count:] - through[i]) * 128 ** (-0.5)
        logits = jnp.where(allowed, logits, -1e30)
        highest = jnp.max(logits, axis=1, keepdims=True)
        weights = jnp.where(allowed, jnp.exp(logits - highest), 0.0)
        probs = weights / jnp.sum(weights, axis=1, keepdims=True)
        probs_ref[i] = probs
        carried_ref[i] = carried[i].astype(BF)
        inverse_ref[i] = inverses[i].astype(BF)
        att = dot(probs.astype(BF), v[i])
        attended.append(att.astype(BF))
        att_t_ref[128 * i : 128 * (i + 1), :] = att.T.astype(BF)
    att = jnp.concatenate(attended, axis=1)
    half = out_lo_ref.shape[1]
    hidden_ref[:, :half] += dot(att, out_lo_ref[...])
    hidden_ref[:, half:] += dot(att, out_hi_ref[...])

    @pl.when(at == pl.num_programs(0) - 1)
    def _():
        value = hidden_ref[...]
        scale = lax.rsqrt(jnp.mean(value * value, axis=1, keepdims=True) + EPSILON)
        gain = gain_row(misc_ref, 13)
        gain_ref[...] = gain
        second_ref[...] = (value * scale * gain).astype(BF)


def attention_forward(tokens, length, attn):
    count, width = tokens.shape
    steps = width // SPAN
    cell = (PER_STEP, count, count)
    whole = lambda i, *_: (0, 0)
    column = lambda i, *_: (0, i)
    weight = lambda half, first: pl.BlockSpec(
        (width, SPAN), lambda i, *_: (half, first // SPAN + i)
    )
    row_block = pl.BlockSpec((count, SPAN), column)
    cell_block = pl.BlockSpec(cell, lambda i, *_: (i, 0, 0))
    rows = jax.ShapeDtypeStruct((count, width), BF)
    turned = jax.ShapeDtypeStruct((width, count), BF)
    cells = (width // 128, count, count)
    return pl.pallas_call(
        attention_forward_kernel,
        grid_spec=pltpu.PrefetchScalarGridSpec(
            num_scalar_prefetch=1,
            grid=(steps,),
            in_specs=[
                pl.BlockSpec((count, width), whole),
                weight(0, FIRST_AT),
                weight(0, SECOND_AT),
                weight(1, FIRST_AT),
                weight(1, SECOND_AT),
                pl.BlockSpec((SPAN, width // 2), lambda i, *_: (i, 0)),
                pl.BlockSpec((SPAN, width // 2), lambda i, *_: (steps + i, 0)),
                pl.BlockSpec((width, 128), lambda i, *_: (0, 6)),
            ],
            out_specs=[
                pl.BlockSpec((width, count), whole),
                row_block,
                row_block,
                row_block,
                row_block,
                pl.BlockSpec((count, width), whole),
                pl.BlockSpec((count, width), whole),
                pl.BlockSpec((SPAN, count), lambda i, *_: (i, 0)),
                cell_block,
                cell_block,
                cell_block,
                pl.BlockSpec((count, 128), whole),
                pl.BlockSpec((1, width), whole),
            ],
            scratch_shapes=[pltpu.VMEM((count, width), BF)],
        ),
        out_shape=[
            turned,
            rows,
            rows,
            rows,
            rows,
            jax.ShapeDtypeStruct((count, width), F32),
            rows,
            turned,
            jax.ShapeDtypeStruct(cells, F32),
            jax.ShapeDtypeStruct(cells, BF),
            jax.ShapeDtypeStruct(cells, BF),
            jax.ShapeDtypeStruct((count, 128), F32),
            jax.ShapeDtypeStruct((1, width), F32),
        ],
        compiler_params=pltpu.CompilerParams(vmem_limit_bytes=58 * MIB),
        cost_estimate=pl.CostEstimate(
            flops=8 * count * width * width + 12 * 60 * 2 * 128**3,
            bytes_accessed=10 * width * width,
            transcendentals=0,
        ),
        name="attention_forward",
    )(length, tokens, attn, attn, attn, attn, attn, attn, attn)


FF_BLOCK = 512


def feedforward_kernel(
    core_ref,
    second_own_ref,
    second_other_ref,
    cot_own_ref,
    cot_other_ref,
    wg_ref,
    wu_ref,
    wd_ref,
    second_t_ref,
    product_t_ref,
    gate_low_ref,
    up_low_ref,
    feed_own_ref,
    feed_other_ref,
    grad_own_ref,
    grad_other_ref,
    second,
    cot,
):
    count = second_own_ref.shape[0]

    @pl.when(pl.program_id(0) == 0)
    def _():
        second[:count] = second_own_ref[...]
        second[count:] = second_other_ref[...]
        cot[:count] = cot_own_ref[...]
        cot[count:] = cot_other_ref[...]
        second_t_ref[:, :count] = second_own_ref[...].astype(F32).T.astype(BF)
        second_t_ref[:, count:] = second_other_ref[...].astype(F32).T.astype(BF)
        feed_own_ref[...] = jnp.zeros_like(feed_own_ref)
        feed_other_ref[...] = jnp.zeros_like(feed_other_ref)
        grad_own_ref[...] = jnp.zeros_like(grad_own_ref)
        grad_other_ref[...] = jnp.zeros_like(grad_other_ref)

    gate = dot(second[...], wg_ref[...])
    upward = dot(second[...], wu_ref[...])
    sigma = jax.nn.sigmoid(gate)
    silu = gate * sigma
    product = silu * upward
    product_t_ref[...] = product.T.astype(BF)
    product_grad = dot_nt(cot[...], wd_ref[...])
    gate_low = (product_grad * upward * (sigma * (1.0 + gate * (1.0 - sigma)))).astype(BF)
    up_low = (product_grad * silu).astype(BF)
    gate_low_ref[...] = gate_low
    up_low_ref[...] = up_low
    feed = dot(product.astype(BF), wd_ref[...])
    feed_own_ref[...] += feed[:count]
    feed_other_ref[...] += feed[count:]
    grad = dot_nt(gate_low, wg_ref[...]) + dot_nt(up_low, wu_ref[...])
    grad_own_ref[...] += grad[:count]
    grad_other_ref[...] += grad[count:]


def feedforward(core, seconds, cots, attn, w_down):
    count, width = seconds[0].shape
    units = w_down.shape[0]
    whole = lambda i, _: (0, 0)
    rows = pl.BlockSpec((count, width), whole)
    columns = pl.BlockSpec((2 * count, FF_BLOCK), lambda i, _: (0, i))
    turned = pl.BlockSpec((FF_BLOCK, 2 * count), lambda i, _: (i, 0))
    weight = lambda first: pl.BlockSpec(
        (width, FF_BLOCK), lambda i, c: (c[0], first // FF_BLOCK + i)
    )
    sums = jax.ShapeDtypeStruct((count, width), F32)
    acts = jax.ShapeDtypeStruct((2 * count, units), BF)
    return pl.pallas_call(
        feedforward_kernel,
        grid_spec=pltpu.PrefetchScalarGridSpec(
            num_scalar_prefetch=1,
            grid=(units // FF_BLOCK,),
            in_specs=[rows] * 4
            + [
                weight(GATE_AT),
                weight(UP_AT),
                pl.BlockSpec((FF_BLOCK, width), lambda i, _: (i, 0)),
            ],
            out_specs=[pl.BlockSpec((width, 2 * count), whole), turned, columns, columns]
            + [rows] * 4,
            scratch_shapes=[pltpu.VMEM((2 * count, width), BF)] * 2,
        ),
        out_shape=[
            jax.ShapeDtypeStruct((width, 2 * count), BF),
            jax.ShapeDtypeStruct((units, 2 * count), BF),
            acts,
            acts,
            sums,
            sums,
            sums,
            sums,
        ],
        compiler_params=pltpu.CompilerParams(vmem_limit_bytes=58 * MIB),
        cost_estimate=pl.CostEstimate(
            flops=24 * count * width * units,
            bytes_accessed=6 * width * units,
            transcendentals=0,
        ),
        name="feedforward",
    )(core, *seconds, *cots, attn, attn, w_down)


def attention_backward_kernel(
    tokens_ref,
    normed_t_ref,
    gain_ref,
    hidden_ref,
    cot_ref,
    grad_own_ref,
    grad_got_ref,
    beta_ref,
    q_ref,
    k_ref,
    v_ref,
    h_ref,
    probs_ref,
    carried_ref,
    inverse_ref,
    wo_lo_ref,
    wo_hi_ref,
    wq_ref,
    wk_ref,
    wv_ref,
    wh_ref,
    misc_ref,
    grads_ref,
    branch_ref,
    grad_tokens_ref,
    misc_grad_ref,
    normed_grad,
    beta_grad,
    hidden_grad_ref,
    ffn_gain_ref,
):
    at = pl.program_id(0)
    half = wo_lo_ref.shape[1]

    @pl.when(at == 0)
    def _():
        normed_grad[...] = jnp.zeros_like(normed_grad)
        beta_grad[...] = jnp.zeros_like(beta_grad)
        value = hidden_ref[...]
        scale = lax.rsqrt(jnp.mean(value * value, axis=1, keepdims=True) + EPSILON)
        grad = grad_own_ref[...] + grad_got_ref[...]
        scaled = grad * gain_ref[...]
        along = jnp.mean(scaled * value, axis=1, keepdims=True)
        hidden_grad = (
            cot_ref[...].astype(F32) + scale * scaled - value * (scale * scale * scale * along)
        )
        hidden_grad_ref[...] = hidden_grad
        branch_ref[...] = hidden_grad.astype(BF)
        ffn_gain_ref[...] = jnp.sum(grad * value * scale, axis=0, keepdims=True)

    att_grad_all = (
        dot_nt(branch_ref[:, :half], wo_lo_ref[...]) + dot_nt(branch_ref[:, half:], wo_hi_ref[...])
    ).astype(BF)
    count = att_grad_all.shape[0]
    row, col = triangles(count)
    strict = row > col
    upto = row >= col
    raw = beta_ref[...]
    lane = lax.broadcasted_iota(jnp.int32, raw.shape, 1)
    heads = range(PER_STEP)
    part = lambda ref: [ref[:, 128 * i : 128 * (i + 1)] for i in heads]
    q, k, v, h = part(q_ref), part(k_ref), part(v_ref), part(h_ref)
    att_grad = [att_grad_all[:, 128 * i : 128 * (i + 1)] for i in heads]
    big = [
        dot_nt(jnp.concatenate([h[i], q[i]], axis=0), jnp.concatenate([h[i], k[i]], axis=0))
        for i in heads
    ]
    probs = [probs_ref[i] for i in heads]
    carried = [carried_ref[i] for i in heads]
    inverse = [inverse_ref[i] for i in heads]
    probs_grad = [dot_nt(att_grad[i], v[i]) for i in heads]
    value_grad = [dot_tn(probs[i].astype(BF), att_grad[i]) for i in heads]
    logit_grad = []
    for i in heads:
        total = jnp.sum(probs_grad[i] * probs[i], axis=1, keepdims=True)
        logit_grad.append((probs[i] * (probs_grad[i] - total) * 128 ** (-0.5)).astype(BF))
    through_grad = [
        jnp.where(upto, -dot_nt(logit_grad[i], carried[i]), 0.0).astype(BF) for i in heads
    ]
    carried_grad = [
        -dot_tn(jnp.where(upto, big[i][count:, :count], 0.0).astype(BF), logit_grad[i])
        for i in heads
    ]
    solved = [dot_tn(inverse[i], carried_grad[i].astype(BF)) for i in heads]
    system_grad = [
        jnp.where(strict, -dot_nt(solved[i].astype(BF), carried[i]), 0.0) for i in heads
    ]
    source_grad = [jnp.where(strict, solved[i], 0.0) for i in heads]
    total_beta = jnp.zeros_like(raw)
    q_grads, k_grads, v_grads, h_grads = [], [], [], []
    for i in heads:
        house = h[i].astype(F32)
        inverse_square = 1.0 / (jnp.sum(house * house, axis=1, keepdims=True) + EPSILON)
        sigma = jax.nn.sigmoid(beta_of(raw, at * PER_STEP + i))
        strength = 2.0 * sigma * inverse_square
        key_part = (strength * source_grad[i]).astype(BF)
        self_part = (strength * system_grad[i]).astype(BF)
        strength_grad = jnp.sum(
            source_grad[i] * big[i][:count, count:] + system_grad[i] * big[i][:count, :count],
            axis=1,
            keepdims=True,
        )
        key_house = jnp.concatenate([k[i], h[i]], axis=0)
        query_house = jnp.concatenate([q[i], h[i]], axis=0)
        q_grads.append(
            dot(jnp.concatenate([logit_grad[i], through_grad[i]], axis=1), key_house).astype(BF)
        )
        k_grads.append(
            dot_tn(jnp.concatenate([logit_grad[i], key_part], axis=0), query_house).astype(BF)
        )
        house_grad = (
            dot_tn(jnp.concatenate([through_grad[i], self_part], axis=0), query_house)
            + dot(jnp.concatenate([key_part, self_part], axis=1), key_house)
            - (2.0 * strength_grad * strength * inverse_square) * house
        )
        h_grads.append(house_grad.astype(BF))
        v_grads.append(value_grad[i].astype(BF))
        raw_grad = strength_grad * inverse_square * (2.0 * sigma * (1.0 - sigma))
        total_beta += jnp.where(lane == at * PER_STEP + i, raw_grad, 0.0)
    beta_grad[...] += total_beta
    update = None
    for index, (pieces, weight_ref) in enumerate(
        ((q_grads, wq_ref), (k_grads, wk_ref), (v_grads, wv_ref), (h_grads, wh_ref))
    ):
        joined = jnp.concatenate(pieces, axis=1)
        grads_ref[index] = joined
        term = dot_nt(joined, weight_ref[...])
        update = term if update is None else update + term
    normed_grad[...] += update

    @pl.when(at == pl.num_programs(0) - 1)
    def _():
        beta_low = beta_grad[...].astype(BF)
        grad = normed_grad[...] + dot_nt(beta_low, misc_ref[...])
        value = tokens_ref[...].astype(F32)
        scale = lax.rsqrt(jnp.mean(value * value, axis=1, keepdims=True) + EPSILON)
        scaled = grad * gain_row(misc_ref, 12)
        along = jnp.mean(scaled * value, axis=1, keepdims=True)
        grad_tokens_ref[...] = (
            hidden_grad_ref[...] + scale * scaled - value * (scale * scale * scale * along)
        )
        attn_gain = jnp.sum(grad * value * scale, axis=0, keepdims=True)
        attn_high, attn_low = two_parts(attn_gain)
        ffn_high, ffn_low = two_parts(ffn_gain_ref[...])
        gains = jnp.concatenate(
            [
                attn_high.astype(F32),
                attn_low.astype(F32),
                ffn_high.astype(F32),
                ffn_low.astype(F32),
                jnp.zeros((4, attn_gain.shape[1]), F32),
            ],
            axis=0,
        )
        place = lax.broadcasted_iota(jnp.int32, (8, 128), 0)
        lanes = lax.broadcasted_iota(jnp.int32, (8, 128), 1)
        pick = ((place < 4) & (lanes == 12 + place // 2)).astype(F32)
        misc_grad = dot(normed_t_ref[...], beta_low) + dot_tn(
            gains.astype(BF), pick.astype(BF)
        )
        misc_grad_ref[...] = misc_grad.astype(BF)


def attention_backward(tokens, normed_t, norm, saved, attn):
    q, k, v, h, probs, carried, inverse, beta = saved
    count, width = tokens.shape
    steps = width // SPAN
    half = width // 2
    whole = lambda i: (0, 0)
    rows = pl.BlockSpec((count, width), whole)
    row_block = pl.BlockSpec((count, SPAN), lambda i: (0, i))
    cell_block = pl.BlockSpec((PER_STEP, count, count), lambda i: (i, 0, 0))
    weight = lambda side, first: pl.BlockSpec((width, SPAN), lambda i: (side, first // SPAN + i))
    out_rows = lambda side: pl.BlockSpec((SPAN, half), lambda i: (side * steps + i, 0))
    return pl.pallas_call(
        attention_backward_kernel,
        grid=(steps,),
        in_specs=[
            rows,
            pl.BlockSpec((width, count), whole),
            pl.BlockSpec((1, width), whole),
            rows,
            rows,
            rows,
            rows,
            pl.BlockSpec((count, 128), whole),
            row_block,
            row_block,
            row_block,
            row_block,
            cell_block,
            cell_block,
            cell_block,
            out_rows(0),
            out_rows(1),
            weight(0, FIRST_AT),
            weight(0, SECOND_AT),
            weight(1, FIRST_AT),
            weight(1, SECOND_AT),
            pl.BlockSpec((width, 128), lambda i: (0, 6)),
        ],
        out_specs=[
            pl.BlockSpec((4, count, SPAN), lambda i: (0, 0, i)),
            rows,
            rows,
            pl.BlockSpec((width, 128), whole),
        ],
        out_shape=[
            jax.ShapeDtypeStruct((4, count, width), BF),
            jax.ShapeDtypeStruct((count, width), BF),
            jax.ShapeDtypeStruct((count, width), F32),
            jax.ShapeDtypeStruct((width, 128), BF),
        ],
        scratch_shapes=[
            pltpu.VMEM((count, width), F32),
            pltpu.VMEM((count, 128), F32),
            pltpu.VMEM((count, width), F32),
            pltpu.VMEM((1, width), F32),
        ],
        compiler_params=pltpu.CompilerParams(vmem_limit_bytes=58 * MIB),
        cost_estimate=SHORT,
        name="attention_backward",
    )(
        tokens,
        normed_t,
        *norm,
        beta,
        q,
        k,
        v,
        h,
        probs,
        carried,
        inverse,
        attn,
        attn,
        attn,
        attn,
        attn,
        attn,
        attn,
    )


def weight_gradient_kernel(segments, x_counts, y_counts, has_misc, second_half, *refs):
    place_ref, refs = refs[0], list(refs[2:])
    xs = [[refs.pop(0) for _ in range(n)] for n in x_counts]
    ys = [[refs.pop(0) for _ in range(n)] for n in y_counts]
    misc_ref = refs.pop(0) if has_misc else None
    at = pl.program_id(0)
    chips, height = xs[0][0].shape[0], xs[0][0].shape[1]
    if second_half:
        spots = [(refs[0], None, i, chips // 2 + 8 * at + i) for i in range(8)]
    else:
        got_lo, got_hi, keep, send = refs
        spots = [(keep, got_lo, i, 4 * at + i) for i in range(4)]
        spots += [(send, got_hi, i, chips // 4 + 4 * at + i) for i in range(4)]
    owners = [place_ref[spot[3]] for spot in spots]
    lefts = []
    for pieces in xs:
        rows = [
            jnp.concatenate([piece[owner].astype(F32) for piece in pieces], axis=1)
            for owner in owners
        ]
        lefts.append(jnp.concatenate(rows, axis=0).astype(BF))
    done = 0
    for x_at, y_at, matrix, start, size in segments:
        columns = slice(start, start + size)
        part = dot(
            lefts[x_at],
            jnp.concatenate([piece[matrix, :, columns] for piece in ys[y_at]], axis=0),
        )
        for index, (out, got, i, _) in enumerate(spots):
            value = part[index * height : (index + 1) * height]
            if got is not None:
                value = value + got[i, :, done : done + size].astype(F32)
            out[i, :, done : done + size] = value.astype(BF)
        done += size
    if has_misc:
        for (out, got, i, _), owner in zip(spots, owners):
            value = misc_ref[owner].astype(F32)
            if got is not None:
                value = value + got[i, :, done:].astype(F32)
            out[i, :, done:] = value.astype(BF)


def weight_gradient(places, core, xs, ys, segments, misc=None, got=None):
    chips, height = xs[0][0].shape[:2]
    columns = sum(segment[4] for segment in segments) + (128 if misc is not None else 0)
    operands, in_specs = [], []
    for pieces in xs:
        operands += pieces
        in_specs += [pl.BlockSpec(p.shape, lambda i, *_: (0, 0, 0)) for p in pieces]
    for pieces in ys:
        operands += pieces
        shape = pieces[0].shape
        if len(pieces) == 2:
            half = (shape[0], shape[1], shape[2] // 2)
            in_specs += [pl.BlockSpec(half, lambda i, _, c: (0, 0, c[0]))] * 2
        else:
            in_specs.append(pl.BlockSpec(shape, lambda i, *_: (0, 0, 0)))
    if misc is not None:
        operands.append(misc)
        in_specs.append(pl.BlockSpec(misc.shape, lambda i, *_: (0, 0, 0)))
    steps = chips // 16
    if got is None:
        out_specs = [pl.BlockSpec((8, height, columns), lambda i, *_: (i, 0, 0))]
        out_shape = [jax.ShapeDtypeStruct((chips // 2, height, columns), BF)]
    else:
        block = (4, height, columns)
        operands += [got, got]
        in_specs += [
            pl.BlockSpec(block, lambda i, *_: (i, 0, 0)),
            pl.BlockSpec(block, lambda i, *_: (steps + i, 0, 0)),
        ]
        out_specs = [pl.BlockSpec(block, lambda i, *_: (i, 0, 0))] * 2
        out_shape = [jax.ShapeDtypeStruct((chips // 4, height, columns), BF)] * 2
    x_counts, y_counts = [len(p) for p in xs], [len(p) for p in ys]
    return pl.pallas_call(
        functools.partial(
            weight_gradient_kernel, segments, x_counts, y_counts, misc is not None, got is None
        ),
        grid_spec=pltpu.PrefetchScalarGridSpec(
            num_scalar_prefetch=2, grid=(steps,), in_specs=in_specs, out_specs=out_specs
        ),
        out_shape=out_shape,
        compiler_params=pltpu.CompilerParams(vmem_limit_bytes=32 * MIB),
        cost_estimate=SHORT,
        name="weight_gradient" if got is None else "weight_gradient_add",
    )(places, core, *operands)


def fold(value):
    part = value.shape[2] // 4
    last = value[:, :, 3 * part :]
    below = jnp.concatenate([last[:, 8 * i : 8 * (i + 1)] for i in range(3)], axis=2)
    return jnp.concatenate([value[:, :, : 3 * part], below], axis=1)


def unfold(value):
    part = value.shape[1] // 3
    last = [value[24:, part * i : part * (i + 1)] for i in range(3)]
    return jnp.concatenate([value[:24], jnp.concatenate(last, axis=0)], axis=1)


def add_kernel(widths, *refs):
    total = sum(len(group) for group in widths)
    ins, outs = refs[: 4 * total], refs[4 * total :]
    at = 0
    for index, group in enumerate(widths):
        start = 0
        for width in group:
            keep_lo, keep_hi, got_lo, got_hi = ins[4 * at : 4 * at + 4]
            low = keep_lo[...].astype(F32) + got_lo[...].astype(F32)
            high = keep_hi[...].astype(F32) + got_hi[...].astype(F32)
            if low.shape[1] != outs[2 * index].shape[1]:
                pad = jnp.zeros((*low.shape[:2], 4 * width // 3 - low.shape[2]), F32)
                low = fold(jnp.concatenate([low, pad], axis=2))
                high = fold(jnp.concatenate([high, pad], axis=2))
            columns = slice(start, start + width)
            outs[2 * index][:, :, columns] = low.astype(BF)
            outs[2 * index + 1][:, :, columns] = high.astype(BF)
            start += width
            at += 1


def add_halves(groups):
    rows = groups[0][0][0].shape[0] // 2
    grid = max(1, rows // 2)
    block = rows // grid
    operands, in_specs, out_specs, shapes, widths = [], [], [], [], []
    for group in groups:
        for keep, got in group:
            shape = (block,) + keep.shape[1:]
            low = pl.BlockSpec(shape, lambda i: (i, 0, 0))
            high = pl.BlockSpec(shape, lambda i: (i + grid, 0, 0))
            operands += [keep, keep, got, got]
            in_specs += [low, high, low, high]
        height = group[0][0].shape[1]
        widths.append(
            [
                keep.shape[2] if keep.shape[1] == height else -(-keep.shape[2] // 512) * 384
                for keep, _ in group
            ]
        )
        shape = (block, height, sum(widths[-1]))
        out_specs += [pl.BlockSpec(shape, lambda i: (i, 0, 0))] * 2
        shapes += [jax.ShapeDtypeStruct((rows,) + shape[1:], BF)] * 2
    outs = pl.pallas_call(
        functools.partial(add_kernel, widths),
        grid=(grid,),
        in_specs=in_specs,
        out_specs=out_specs,
        out_shape=shapes,
        compiler_params=pltpu.CompilerParams(vmem_limit_bytes=24 * MIB),
        cost_estimate=SHORT,
        name="add_halves",
    )(*operands)
    return outs[0::2], outs[1::2]


def last_add_kernel(core_ref, *refs):
    first = core_ref[0] == 0
    *ins, mine, theirs, down = refs
    values = [
        ins[index][0].astype(F32) + ins[index + 1][0].astype(F32)
        for index in range(0, len(ins), 2)
    ]
    width = down.shape[1]
    down[...] = values[2][:, :width]
    values[2] = unfold(values[2][:, width:])
    start = 0
    for value in values:
        low, high = value[:12], value[12:]
        columns = slice(start, start + value.shape[1])
        mine[:, columns] = jnp.where(first, low, high)
        theirs[:, columns] = jnp.where(first, high, low).astype(BF)
        start += value.shape[1]


def last_add(core, pairs, down_shape):
    flat = [value for pair in pairs for value in pair]
    folded = pairs[2][0].shape[2] - down_shape[1]
    width = pairs[0][0].shape[2] + pairs[1][0].shape[2] + folded // 3 * 4
    shapes = [(12, width), (12, width), down_shape]
    return pl.pallas_call(
        last_add_kernel,
        grid_spec=pltpu.PrefetchScalarGridSpec(
            num_scalar_prefetch=1,
            grid=(1,),
            in_specs=[pl.BlockSpec(v.shape, lambda i, _: (0, 0, 0)) for v in flat],
            out_specs=[pl.BlockSpec(shape, lambda i, _: (0, 0)) for shape in shapes],
        ),
        out_shape=[jax.ShapeDtypeStruct(s, t) for s, t in zip(shapes, (F32, BF, F32))],
        compiler_params=pltpu.CompilerParams(vmem_limit_bytes=16 * MIB),
        cost_estimate=SHORT,
        name="last_add",
    )(core, *flat)


PLACES = (
    ((2048, 768),),
    ((2816, 512), (5376, 256)),
    ((5632, 768),),
    ((6400, 256), (6656, 512)),
    ((7168, 768),),
)
HIDDEN_PLACES = (0, 3328)
TILE = 256


def deal(parity):
    row = lax.broadcasted_iota(jnp.int32, (TILE // 2, TILE), 0)
    col = lax.broadcasted_iota(jnp.int32, (TILE // 2, TILE), 1)
    return (col == 64 * (row // 32) + 32 * parity + row % 32).astype(F32).astype(BF)


def finish_kernel(core_ref, mine, other, *outs):
    first = core_ref[0] == 0
    for pieces, out in zip(PLACES, outs):
        half = out.shape[1] // 2
        done = 0
        for start, width in pieces:
            a = mine[:, start : start + width]
            b = other[:, start : start + width].astype(F32)
            out[:, done : done + width] = jnp.where(first, a, b)
            out[:, half + done : half + done + width] = jnp.where(first, b, a)
            done += width
    own, their = deal(core_ref[0]), deal(1 - core_ref[0])
    rows = mine.shape[0]
    pad = jnp.zeros((16 - rows, TILE // 2), F32)
    for start, out in zip(HIDDEN_PLACES, outs[5:7]):
        tiles = out.shape[1] // TILE
        stack = lambda ref: jnp.concatenate(
            [
                jnp.concatenate(
                    [ref[:, start + 128 * t : start + 128 * (t + 1)].astype(F32), pad], axis=0
                )
                for t in range(tiles)
            ],
            axis=0,
        )
        high, low = two_parts(stack(mine))
        value = dot(high, own) + dot(low, own) + dot(stack(other).astype(BF), their)
        for t in range(tiles):
            out[:, TILE * t : TILE * (t + 1)] = value[16 * t : 16 * t + rows]
    misc = mine[:, 7936:8064] + other[:, 7936:8064].astype(F32)
    heads = outs[7].shape[1]
    outs[7][...] = misc[:, :heads]
    row = lax.broadcasted_iota(jnp.int32, (rows, 128), 0)
    col = lax.broadcasted_iota(jnp.int32, (rows, 128), 1)
    eye = (row == col).astype(F32).astype(BF)
    high, low = two_parts(misc)
    turned = dot_tn(high, eye) + dot_tn(low, eye)
    outs[8][...] = turned[heads : heads + 1, :rows]
    outs[9][...] = turned[heads + 1 : heads + 2, :rows]


def finish(core, mine, other, hidden_units, heads):
    rows = mine.shape[0]
    shapes = [(rows, 2 * sum(w for _, w in pieces)) for pieces in PLACES]
    shapes += [(rows, hidden_units), (rows, hidden_units), (rows, heads), (1, rows), (1, rows)]
    operands = (mine, other)
    return pl.pallas_call(
        finish_kernel,
        grid_spec=pltpu.PrefetchScalarGridSpec(
            num_scalar_prefetch=1,
            grid=(1,),
            in_specs=[pl.BlockSpec(v.shape, lambda i, _: (0, 0)) for v in operands],
            out_specs=[pl.BlockSpec(shape, lambda i, _: (0, 0)) for shape in shapes],
        ),
        out_shape=[jax.ShapeDtypeStruct(shape, F32) for shape in shapes],
        compiler_params=pltpu.CompilerParams(vmem_limit_bytes=16 * MIB),
        cost_estimate=SHORT,
        name="finish",
    )(core, *operands)


def pack_kernel(core_ref, gain_attn, gain_ffn, *refs):
    w_out, w_query, w_key, w_value, w_house, w_beta, w_gate, w_up = refs[:8]
    mine, theirs = refs[8:]
    first = core_ref[0] == 0
    rows, width = w_out.shape
    half, units = width // 2, w_gate.shape[1]
    gains = jnp.concatenate(
        [gain_attn[...].astype(F32), gain_ffn[...].astype(F32), jnp.zeros((6, rows), F32)], axis=0
    )
    place = lax.broadcasted_iota(jnp.int32, (8, 256), 0)
    lane = lax.broadcasted_iota(jnp.int32, (8, 256), 1)
    pick = ((place < 2) & (lane == 12 + place)).astype(F32)
    misc = dot_tn(gains.astype(BF), pick.astype(BF))
    beta = w_beta[...].astype(F32)
    misc += jnp.concatenate([beta, jnp.zeros((rows, 256 - beta.shape[1]), F32)], axis=1)
    split = lambda a, b: (jnp.where(first, a, b), jnp.where(first, b, a))
    pieces = [
        split(w_out[:, :half], w_out[:, half:]),
        (misc.astype(BF), misc.astype(BF)),
        split(w_query[...], w_value[...]),
        split(w_key[...], w_house[...]),
    ]
    for start, (own, other) in zip((0, half, FIRST_AT, SECOND_AT), pieces):
        size = own.shape[1]
        mine[:, start : start + size] = own
        theirs[:, start : start + size] = other
    pad = jnp.zeros((16 - rows, TILE), F32)
    row = lax.broadcasted_iota(jnp.int32, (TILE, TILE), 0)
    col = lax.broadcasted_iota(jnp.int32, (TILE, TILE), 1)
    parity = jnp.where(col < 128, core_ref[0], 1 - core_ref[0])
    at = col % 128
    pick = (row == 64 * (at // 32) + 32 * parity + at % 32).astype(F32).astype(BF)
    tiles = units // TILE
    for start, ref in ((GATE_AT, w_gate), (UP_AT, w_up)):
        stack = jnp.concatenate(
            [
                jnp.concatenate([ref[:, TILE * t : TILE * (t + 1)].astype(F32), pad], axis=0)
                for t in range(tiles)
            ],
            axis=0,
        ).astype(BF)
        value = dot(stack, pick)
        for t in range(tiles):
            part = value[16 * t : 16 * t + rows].astype(BF)
            mine[:, start + 128 * t : start + 128 * (t + 1)] = part[:, :128]
            theirs[:, start + 128 * t : start + 128 * (t + 1)] = part[:, 128:]


def pack(core, gains, weights):
    rows, width = weights[0].shape
    shapes = [(rows, SECOND_AT + width)] * 2
    operands = [gain[None, :] for gain in gains] + list(weights)
    return pl.pallas_call(
        pack_kernel,
        grid_spec=pltpu.PrefetchScalarGridSpec(
            num_scalar_prefetch=1,
            grid=(1,),
            in_specs=[pl.BlockSpec(v.shape, lambda i, _: (0, 0)) for v in operands],
            out_specs=[pl.BlockSpec(shape, lambda i, _: (0, 0)) for shape in shapes],
        ),
        out_shape=[jax.ShapeDtypeStruct(shape, BF) for shape in shapes],
        compiler_params=pltpu.CompilerParams(vmem_limit_bytes=58 * MIB),
        cost_estimate=SHORT,
        name="pack",
    )(core, *operands)


def send_step(value, stream, step):
    count = lax.axis_size("fsdp")
    pairs = [(d, d ^ (2 * MASKS[stream][d & 1][step])) for d in range(count)]
    return lax.ppermute(value, "fsdp", pairs)


def after(values, earlier):
    flat, tree = jax.tree.flatten(values)
    kept = lax.optimization_barrier((*flat, *jax.tree.leaves(earlier)))
    return jax.tree.unflatten(tree, kept[: len(flat)])


def exchange(sends, step):
    return [send_step(send, stream, step) for stream, send in enumerate(sends)]


def blocks(turned, height):
    return turned.reshape(turned.shape[0] // height, height, turned.shape[1])


def gather_streams(parts):
    for step in range(5, 0, -1):
        gots = exchange(parts, step)
        parts = [jnp.concatenate(pair, axis=0) for pair in zip(parts, gots)]
    return parts, exchange(parts, 0)


def in_order_kernel(place_ref, *refs):
    lows, highs, out = refs[:3], refs[3:6], refs[6]
    half, _, width = lows[0].shape
    for stream, (low, high) in enumerate(zip(lows, highs)):
        columns = slice(width * stream, width * (stream + 1))
        for place in range(half):
            out[place_ref[stream, place], :, columns] = low[place]
            out[place_ref[stream, half + place], :, columns] = high[place]


def in_order(places, lows, highs):
    half, height, width = lows[0].shape
    shape = (2 * half, height, 3 * width)
    out = pl.pallas_call(
        in_order_kernel,
        grid_spec=pltpu.PrefetchScalarGridSpec(
            num_scalar_prefetch=1,
            grid=(1,),
            in_specs=[pl.BlockSpec(lows[0].shape, lambda i, _: (0, 0, 0))] * 6,
            out_specs=pl.BlockSpec(shape, lambda i, _: (0, 0, 0)),
        ),
        out_shape=jax.ShapeDtypeStruct(shape, BF),
        compiler_params=pltpu.CompilerParams(vmem_limit_bytes=58 * MIB),
        cost_estimate=SHORT,
        name="in_order",
    )(places, *lows, *highs)
    return out.reshape(2 * half * height, 3 * width)


def body(
    tokens,
    lengths,
    gain_attn,
    w_query,
    w_key,
    w_value,
    w_house,
    w_beta,
    w_out,
    gain_ffn,
    w_gate,
    w_up,
    w_down,
    cotangent,
):
    seqs, count, width = tokens.shape
    heads = w_beta.shape[1]
    hidden_units = w_gate.shape[1]
    half = width // 2
    devices = lax.axis_size("fsdp")
    me = lax.axis_index("fsdp")
    core, chip = me % 2, me // 2
    offsets = jnp.asarray(owner_offsets())
    places = jnp.where(core == 0, offsets[0], offsets[1]) ^ chip
    core_at = core.astype(jnp.int32)[None]

    mine, theirs = pack(
        core_at,
        (gain_attn, gain_ffn),
        (w_out, w_query, w_key, w_value, w_house, w_beta, w_gate, w_up),
    )
    stack = lambda own, other: jnp.where(
        core == 0,
        jnp.concatenate([own, other], axis=0),
        jnp.concatenate([other, own], axis=0),
    )
    slab = stack(mine, swap(theirs))
    by_core = [[*range(0, devices, 2), *range(1, devices, 2)]]
    attn = lax.all_gather(slab, "fsdp", axis=0, tiled=True, axis_index_groups=by_core)
    part, third = hidden_units // 2, width // 3
    lows, highs = gather_streams([w_down[None, :, third * s : third * (s + 1)] for s in range(3)])
    full_down = in_order(places, lows, highs)

    flat = tokens.reshape(count, width)
    valid = lax.broadcasted_iota(jnp.int32, (count, 1), 0) < lengths[0]
    cot = jnp.where(valid, cotangent.reshape(count, width), jnp.zeros((), BF))
    cots = (cot, swap(cot))

    normed_t, q, k, v, h, hidden, second, att_t, *cells, beta, gain = attention_forward(
        after(flat, full_down), lengths, attn
    )
    normed_x, att_x = (
        (blocks(value, 24), blocks(swap(value), 24)) for value in (normed_t, att_t)
    )
    second_t, product_t, gate_low, up_low, feed, feed_other, second_grad, grad_other = feedforward(
        core_at, (second, swap(second)), cots, attn, full_down
    )
    grad_got = swap(grad_other)
    mixed = jnp.where(valid, hidden + feed + swap(feed_other), 0.0).astype(BF)
    second_x, product_x = (blocks(second_t, 24),), (blocks(product_t, 32),)

    jobs = [
        ([second_x], [(gate_low[None],)], [(0, 0, 0, 0, part)]),
        ([second_x], [(up_low[None],)], [(0, 0, 0, 0, part)]),
        ([product_x], [(jnp.concatenate(cots, axis=0)[None],)], [(0, 0, 0, 0, width)]),
    ]
    early = [places[0], after(places[1], (grad_got, normed_x, att_x)), places[2]]
    sends = [weight_gradient(early[s], core_at, *job)[0] for s, job in enumerate(jobs)]
    gots = exchange(sends, 0)

    grads, branch, grad_tokens, misc_grad = attention_backward(
        flat,
        normed_t,
        (gain, after(hidden, sends), cot, second_grad, grad_got),
        (q, k, v, h, *cells, beta),
        attn,
    )
    grads_y = (grads, swap(grads))
    branch_y = (branch[None], swap(branch)[None])
    misc_x = misc_grad.reshape(-1, 24, 128)
    attn_jobs = [
        ([normed_x], [grads_y], [(0, 0, 0, 0, 768), (0, 0, 1, 0, 512)]),
        ([normed_x], [grads_y], [(0, 0, 1, 512, 256), (0, 0, 2, 0, 768), (0, 0, 3, 0, 256)]),
        ([normed_x, att_x], [grads_y, branch_y], [(0, 0, 3, 256, 512), (1, 1, 0, 0, 768)], misc_x),
    ]
    attn_sends = [
        weight_gradient(after(places[s], gots[s]), core_at, *job)[0]
        for s, job in enumerate(attn_jobs)
    ]
    attn_gots = exchange(attn_sends, 0)

    def kept(jobs, gots):
        pairs = [
            weight_gradient(places[s], core_at, *job, got=gots[s]) for s, job in enumerate(jobs)
        ]
        return [p[0] for p in pairs], [p[1] for p in pairs]

    keeps, sends = kept(jobs, gots)
    gots = exchange([after(send, got) for send, got in zip(sends, attn_gots)], 1)
    attn_keeps, attn_sends = kept(attn_jobs, [after(got, keeps) for got in attn_gots])
    attn_gots = exchange(attn_sends, 1)
    first, second = list(zip(keeps, gots)), list(zip(attn_keeps, attn_gots))
    groups = [list(pair) for pair in zip(first, second)]
    for step in range(2, 6):
        keeps, sends = add_halves(groups)
        gots = exchange(sends, step)
        groups = [[pair] for pair in zip(keeps, gots)]
    mine, theirs, grad_down = last_add(core_at, [group[0] for group in groups], w_down.shape)
    *large, grad_gate, grad_up, grad_beta, attn_gain, ffn_gain = finish(
        core_at, mine, swap(theirs), hidden_units, heads
    )

    return (
        mixed.reshape(seqs, count, width),
        grad_tokens.reshape(seqs, count, width),
        attn_gain.reshape(-1),
        *large[:4],
        grad_beta,
        large[4],
        ffn_gain.reshape(-1),
        grad_gate,
        grad_up,
        grad_down,
    )


def solution(mesh):
    rows = P("fsdp", None)
    line = P("fsdp")
    cube = P("fsdp", None, None)
    in_specs = (cube, line, line, rows, rows, rows, rows, rows, rows, line, rows, rows, rows, cube)
    out_specs = (cube, cube, line, rows, rows, rows, rows, rows, rows, line, rows, rows, rows)
    return jax.shard_map(body, mesh=mesh, in_specs=in_specs, out_specs=out_specs, check_vma=False)
```

```python
import functools

import jax
import jax.numpy as jnp
import numpy as np
from jax import lax
from jax.experimental import pallas as pl
from jax.experimental.pallas import tpu as pltpu
from jax.sharding import PartitionSpec as P

EPSILON = 1e-06
BF = jnp.bfloat16
F32 = jnp.float32
MIB = 1024 * 1024
SHORT = pl.CostEstimate(flops=1, bytes_accessed=1, transcendentals=0)
AXIS_UNIT = {"x": 16, "z": 4, "y": 1}
ORDERS = ("xzy", "zyx", "yxz")


def step_masks(stream, core):
    masks = []
    for axis in ORDERS[stream]:
        unit = AXIS_UNIT[axis]
        masks += [unit, 3 * unit] if core == 0 else [3 * unit, unit]
    return masks


MASKS = [[step_masks(stream, core) for core in (0, 1)] for stream in range(3)]


def owner_offsets():
    table = np.zeros((2, 3, 64), np.int32)
    for core in (0, 1):
        for stream in range(3):
            for place in range(64):
                value = 0
                for step, mask in enumerate(MASKS[stream][core]):
                    if (place >> (5 - step)) & 1:
                        value ^= mask
                table[core, stream, place] = value
    return table


def dot(left, right):
    return jnp.dot(left, right, preferred_element_type=F32)


def dot_nt(left, right):
    return lax.dot_general(left, right, (((1,), (1,)), ((), ())), preferred_element_type=F32)


def dot_tn(left, right):
    return lax.dot_general(left, right, (((0,), (0,)), ((), ())), preferred_element_type=F32)


def two_parts(value):
    high = value.astype(BF)
    return high, (value - high.astype(F32)).astype(BF)


def dot_fine(left, right):
    size = right.shape[1]
    wide = jnp.concatenate(two_parts(left), axis=1)
    pair = jnp.concatenate(two_parts(right), axis=1)
    out = dot(wide, jnp.concatenate([pair, pair], axis=0))
    return out[:, :size] + out[:, size:]


def swap(value):
    count = lax.axis_size("fsdp")
    return lax.ppermute(value, "fsdp", [(d, d ^ 1) for d in range(count)])


def gain_row(misc_ref, column):
    pick = (lax.broadcasted_iota(jnp.int32, (8, 128), 1) == column).astype(F32).astype(BF)
    return dot_nt(pick, misc_ref[...])[0:1]


def triangles(count):
    row = lax.broadcasted_iota(jnp.int32, (count, count), 0)
    col = lax.broadcasted_iota(jnp.int32, (count, count), 1)
    return row, col


def beta_of(raw, head):
    lane = lax.broadcasted_iota(jnp.int32, raw.shape, 1)
    return jnp.sum(jnp.where(lane == head, raw, 0.0), axis=1, keepdims=True)


def unit_lower_inverse(systems, row, col):
    size = row.shape[0]
    eye = (row == col).astype(F32)
    step = 1
    inverses = None
    while step < size:
        lower = ((row // step) % 2 == 1) & (col // step == row // step - 1)
        parts = [jnp.where(lower, system, 0.0) for system in systems]
        if step == 1:
            inverses = [eye - part for part in parts]
        else:
            middles = [dot_fine(inv, part) for inv, part in zip(inverses, parts)]
            inverses = [inv - dot_fine(mid, inv) for inv, mid in zip(inverses, middles)]
        step *= 2
    return inverses


PER_STEP = 6
SPAN = 128 * PER_STEP
FIRST_AT, SECOND_AT, MISC_AT, GATE_AT, UP_AT = 768, 2304, 3840, 4096, 6144


def attention_forward_kernel(
    length_ref,
    tokens_ref,
    wq_ref,
    wk_ref,
    wv_ref,
    wh_ref,
    out_lo_ref,
    out_hi_ref,
    misc_ref,
    normed_t_ref,
    q_ref,
    k_ref,
    v_ref,
    h_ref,
    hidden_ref,
    second_ref,
    att_t_ref,
    probs_ref,
    carried_ref,
    inverse_ref,
    beta_ref,
    gain_ref,
    normed_ref,
):
    at = pl.program_id(0)

    @pl.when(at == 0)
    def _():
        tokens = tokens_ref[...].astype(F32)
        scale = lax.rsqrt(jnp.mean(tokens * tokens, axis=1, keepdims=True) + EPSILON)
        value = tokens * scale * gain_row(misc_ref, 12)
        normed_ref[...] = value.astype(BF)
        normed_t_ref[...] = value.T.astype(BF)
        beta_ref[...] = dot(normed_ref[...], misc_ref[...])
        hidden_ref[...] = tokens

    normed = normed_ref[...]
    q_all = dot(normed, wq_ref[...]).astype(BF)
    k_all = dot(normed, wk_ref[...]).astype(BF)
    v_all = dot(normed, wv_ref[...]).astype(BF)
    h_all = dot(normed, wh_ref[...]).astype(BF)
    q_ref[...] = q_all
    k_ref[...] = k_all
    v_ref[...] = v_all
    h_ref[...] = h_all
    count = q_all.shape[0]
    row, col = triangles(count)
    strict = row > col
    upto = row >= col
    allowed = upto & (col < length_ref[0])
    raw = beta_ref[...]
    heads = range(PER_STEP)
    q, k, v, h = (
        [value[:, 128 * i : 128 * (i + 1)] for i in heads] for value in (q_all, k_all, v_all, h_all)
    )
    big = [
        dot_nt(jnp.concatenate([h[i], q[i]], axis=0), jnp.concatenate([h[i], k[i]], axis=0))
        for i in heads
    ]
    strength = []
    for i in heads:
        house = h[i].astype(F32)
        square = jnp.sum(house * house, axis=1, keepdims=True) + EPSILON
        beta = 2.0 * jax.nn.sigmoid(beta_of(raw, at * PER_STEP + i))
        strength.append(beta / square)
    systems = [jnp.where(strict, strength[i] * big[i][:count, :count], 0.0) for i in heads]
    sources = [jnp.where(strict, strength[i] * big[i][:count, count:], 0.0) for i in heads]
    inverses = unit_lower_inverse(systems, row, col)
    carried = [dot_fine(inverses[i], sources[i]) for i in heads]
    through = [
        dot_fine(jnp.where(upto, big[i][count:, :count], 0.0), carried[i]) for i in heads
    ]
    attended = []
    for i in heads:
        logits = (big[i][count:, count:] - through[i]) * 128 ** (-0.5)
        logits = jnp.where(allowed, logits, -1e30)
        highest = jnp.max(logits, axis=1, keepdims=True)
        weights = jnp.where(allowed, jnp.exp(logits - highest), 0.0)
        probs = weights / jnp.sum(weights, axis=1, keepdims=True)
        probs_ref[i] = probs
        carried_ref[i] = carried[i].astype(BF)
        inverse_ref[i] = inverses[i].astype(BF)
        att = dot(probs.astype(BF), v[i])
        attended.append(att.astype(BF))
        att_t_ref[128 * i : 128 * (i + 1), :] = att.T.astype(BF)
    att = jnp.concatenate(attended, axis=1)
    half = out_lo_ref.shape[1]
    hidden_ref[:, :half] += dot(att, out_lo_ref[...])
    hidden_ref[:, half:] += dot(att, out_hi_ref[...])

    @pl.when(at == pl.num_programs(0) - 1)
    def _():
        value = hidden_ref[...]
        scale = lax.rsqrt(jnp.mean(value * value, axis=1, keepdims=True) + EPSILON)
        gain = gain_row(misc_ref, 13)
        gain_ref[...] = gain
        second_ref[...] = (value * scale * gain).astype(BF)


def attention_forward(tokens, length, attn):
    count, width = tokens.shape
    steps = width // SPAN
    cell = (PER_STEP, count, count)
    whole = lambda i, *_: (0, 0)
    column = lambda i, *_: (0, i)
    weight = lambda half, first: pl.BlockSpec(
        (width, SPAN), lambda i, *_: (half, first // SPAN + i)
    )
    row_block = pl.BlockSpec((count, SPAN), column)
    cell_block = pl.BlockSpec(cell, lambda i, *_: (i, 0, 0))
    rows = jax.ShapeDtypeStruct((count, width), BF)
    turned = jax.ShapeDtypeStruct((width, count), BF)
    cells = (width // 128, count, count)
    return pl.pallas_call(
        attention_forward_kernel,
        grid_spec=pltpu.PrefetchScalarGridSpec(
            num_scalar_prefetch=1,
            grid=(steps,),
            in_specs=[
                pl.BlockSpec((count, width), whole),
                weight(0, FIRST_AT),
                weight(0, SECOND_AT),
                weight(1, FIRST_AT),
                weight(1, SECOND_AT),
                pl.BlockSpec((SPAN, width // 2), lambda i, *_: (i, 0)),
                pl.BlockSpec((SPAN, width // 2), lambda i, *_: (steps + i, 0)),
                pl.BlockSpec((width, 128), lambda i, *_: (0, MISC_AT // 128)),
            ],
            out_specs=[
                pl.BlockSpec((width, count), whole),
                row_block,
                row_block,
                row_block,
                row_block,
                pl.BlockSpec((count, width), whole),
                pl.BlockSpec((count, width), whole),
                pl.BlockSpec((SPAN, count), lambda i, *_: (i, 0)),
                cell_block,
                cell_block,
                cell_block,
                pl.BlockSpec((count, 128), whole),
                pl.BlockSpec((1, width), whole),
            ],
            scratch_shapes=[pltpu.VMEM((count, width), BF)],
        ),
        out_shape=[
            turned,
            rows,
            rows,
            rows,
            rows,
            jax.ShapeDtypeStruct((count, width), F32),
            rows,
            turned,
            jax.ShapeDtypeStruct(cells, F32),
            jax.ShapeDtypeStruct(cells, BF),
            jax.ShapeDtypeStruct(cells, BF),
            jax.ShapeDtypeStruct((count, 128), F32),
            jax.ShapeDtypeStruct((1, width), F32),
        ],
        compiler_params=pltpu.CompilerParams(vmem_limit_bytes=58 * MIB),
        cost_estimate=pl.CostEstimate(
            flops=8 * count * width * width + 12 * 60 * 2 * 128**3,
            bytes_accessed=10 * width * width,
            transcendentals=0,
        ),
        name="attention_forward",
    )(length, tokens, attn, attn, attn, attn, attn, attn, attn)


FF_BLOCK = 512


def feedforward_kernel(
    core_ref,
    second_own_ref,
    second_other_ref,
    cot_own_ref,
    cot_other_ref,
    wg_ref,
    wu_ref,
    wd_ref,
    second_t_ref,
    product_t_ref,
    gate_low_ref,
    up_low_ref,
    feed_own_ref,
    feed_other_ref,
    grad_own_ref,
    grad_other_ref,
    second,
    cot,
):
    count = second_own_ref.shape[0]

    @pl.when(pl.program_id(0) == 0)
    def _():
        second[:count] = second_own_ref[...]
        second[count:] = second_other_ref[...]
        cot[:count] = cot_own_ref[...]
        cot[count:] = cot_other_ref[...]
        second_t_ref[:, :count] = second_own_ref[...].astype(F32).T.astype(BF)
        second_t_ref[:, count:] = second_other_ref[...].astype(F32).T.astype(BF)
        feed_own_ref[...] = jnp.zeros_like(feed_own_ref)
        feed_other_ref[...] = jnp.zeros_like(feed_other_ref)
        grad_own_ref[...] = jnp.zeros_like(grad_own_ref)
        grad_other_ref[...] = jnp.zeros_like(grad_other_ref)

    gate = dot(second[...], wg_ref[...])
    upward = dot(second[...], wu_ref[...])
    sigma = jax.nn.sigmoid(gate)
    silu = gate * sigma
    product = silu * upward
    product_t_ref[...] = product.T.astype(BF)
    product_grad = dot_nt(cot[...], wd_ref[...])
    gate_low = (product_grad * upward * (sigma * (1.0 + gate * (1.0 - sigma)))).astype(BF)
    up_low = (product_grad * silu).astype(BF)
    gate_low_ref[...] = gate_low
    up_low_ref[...] = up_low
    feed = dot(product.astype(BF), wd_ref[...])
    feed_own_ref[...] += feed[:count]
    feed_other_ref[...] += feed[count:]
    grad = dot_nt(gate_low, wg_ref[...]) + dot_nt(up_low, wu_ref[...])
    grad_own_ref[...] += grad[:count]
    grad_other_ref[...] += grad[count:]


def feedforward(core, seconds, cots, attn, w_down):
    count, width = seconds[0].shape
    units = w_down.shape[0]
    whole = lambda i, _: (0, 0)
    rows = pl.BlockSpec((count, width), whole)
    columns = pl.BlockSpec((2 * count, FF_BLOCK), lambda i, _: (0, i))
    turned = pl.BlockSpec((FF_BLOCK, 2 * count), lambda i, _: (i, 0))
    weight = lambda first: pl.BlockSpec(
        (width, FF_BLOCK), lambda i, c: (c[0], first // FF_BLOCK + i)
    )
    sums = jax.ShapeDtypeStruct((count, width), F32)
    acts = jax.ShapeDtypeStruct((2 * count, units), BF)
    return pl.pallas_call(
        feedforward_kernel,
        grid_spec=pltpu.PrefetchScalarGridSpec(
            num_scalar_prefetch=1,
            grid=(units // FF_BLOCK,),
            in_specs=[rows] * 4
            + [
                weight(GATE_AT),
                weight(UP_AT),
                pl.BlockSpec((FF_BLOCK, width), lambda i, _: (i, 0)),
            ],
            out_specs=[pl.BlockSpec((width, 2 * count), whole), turned, columns, columns]
            + [rows] * 4,
            scratch_shapes=[pltpu.VMEM((2 * count, width), BF)] * 2,
        ),
        out_shape=[
            jax.ShapeDtypeStruct((width, 2 * count), BF),
            jax.ShapeDtypeStruct((units, 2 * count), BF),
            acts,
            acts,
            sums,
            sums,
            sums,
            sums,
        ],
        compiler_params=pltpu.CompilerParams(vmem_limit_bytes=58 * MIB),
        cost_estimate=pl.CostEstimate(
            flops=24 * count * width * units,
            bytes_accessed=6 * width * units,
            transcendentals=0,
        ),
        name="feedforward",
    )(core, *seconds, *cots, attn, attn, w_down)


def attention_backward_kernel(
    tokens_ref,
    normed_t_ref,
    gain_ref,
    hidden_ref,
    cot_ref,
    grad_own_ref,
    grad_got_ref,
    beta_ref,
    q_ref,
    k_ref,
    v_ref,
    h_ref,
    probs_ref,
    carried_ref,
    inverse_ref,
    wo_lo_ref,
    wo_hi_ref,
    wq_ref,
    wk_ref,
    wv_ref,
    wh_ref,
    misc_ref,
    grads_ref,
    branch_ref,
    grad_tokens_ref,
    misc_grad_ref,
    normed_grad,
    beta_grad,
    hidden_grad_ref,
    ffn_gain_ref,
):
    at = pl.program_id(0)
    half = wo_lo_ref.shape[1]

    @pl.when(at == 0)
    def _():
        normed_grad[...] = jnp.zeros_like(normed_grad)
        beta_grad[...] = jnp.zeros_like(beta_grad)
        value = hidden_ref[...]
        scale = lax.rsqrt(jnp.mean(value * value, axis=1, keepdims=True) + EPSILON)
        grad = grad_own_ref[...] + grad_got_ref[...]
        scaled = grad * gain_ref[...]
        along = jnp.mean(scaled * value, axis=1, keepdims=True)
        hidden_grad = (
            cot_ref[...].astype(F32) + scale * scaled - value * (scale * scale * scale * along)
        )
        hidden_grad_ref[...] = hidden_grad
        branch_ref[...] = hidden_grad.astype(BF)
        ffn_gain_ref[...] = jnp.sum(grad * value * scale, axis=0, keepdims=True)

    att_grad_all = (
        dot_nt(branch_ref[:, :half], wo_lo_ref[...]) + dot_nt(branch_ref[:, half:], wo_hi_ref[...])
    ).astype(BF)
    count = att_grad_all.shape[0]
    row, col = triangles(count)
    strict = row > col
    upto = row >= col
    raw = beta_ref[...]
    lane = lax.broadcasted_iota(jnp.int32, raw.shape, 1)
    heads = range(PER_STEP)
    part = lambda ref: [ref[:, 128 * i : 128 * (i + 1)] for i in heads]
    q, k, v, h = part(q_ref), part(k_ref), part(v_ref), part(h_ref)
    att_grad = [att_grad_all[:, 128 * i : 128 * (i + 1)] for i in heads]
    big = [
        dot_nt(jnp.concatenate([h[i], q[i]], axis=0), jnp.concatenate([h[i], k[i]], axis=0))
        for i in heads
    ]
    probs = [probs_ref[i] for i in heads]
    carried = [carried_ref[i] for i in heads]
    inverse = [inverse_ref[i] for i in heads]
    probs_grad = [dot_nt(att_grad[i], v[i]) for i in heads]
    value_grad = [dot_tn(probs[i].astype(BF), att_grad[i]) for i in heads]
    logit_grad = []
    for i in heads:
        total = jnp.sum(probs_grad[i] * probs[i], axis=1, keepdims=True)
        logit_grad.append((probs[i] * (probs_grad[i] - total) * 128 ** (-0.5)).astype(BF))
    through_grad = [
        jnp.where(upto, -dot_nt(logit_grad[i], carried[i]), 0.0).astype(BF) for i in heads
    ]
    carried_grad = [
        -dot_tn(jnp.where(upto, big[i][count:, :count], 0.0).astype(BF), logit_grad[i])
        for i in heads
    ]
    solved = [dot_tn(inverse[i], carried_grad[i].astype(BF)) for i in heads]
    system_grad = [
        jnp.where(strict, -dot_nt(solved[i].astype(BF), carried[i]), 0.0) for i in heads
    ]
    source_grad = [jnp.where(strict, solved[i], 0.0) for i in heads]
    total_beta = jnp.zeros_like(raw)
    q_grads, k_grads, v_grads, h_grads = [], [], [], []
    for i in heads:
        house = h[i].astype(F32)
        inverse_square = 1.0 / (jnp.sum(house * house, axis=1, keepdims=True) + EPSILON)
        sigma = jax.nn.sigmoid(beta_of(raw, at * PER_STEP + i))
        strength = 2.0 * sigma * inverse_square
        key_part = (strength * source_grad[i]).astype(BF)
        self_part = (strength * system_grad[i]).astype(BF)
        strength_grad = jnp.sum(
            source_grad[i] * big[i][:count, count:] + system_grad[i] * big[i][:count, :count],
            axis=1,
            keepdims=True,
        )
        key_house = jnp.concatenate([k[i], h[i]], axis=0)
        query_house = jnp.concatenate([q[i], h[i]], axis=0)
        q_grads.append(
            dot(jnp.concatenate([logit_grad[i], through_grad[i]], axis=1), key_house).astype(BF)
        )
        k_grads.append(
            dot_tn(jnp.concatenate([logit_grad[i], key_part], axis=0), query_house).astype(BF)
        )
        house_grad = (
            dot_tn(jnp.concatenate([through_grad[i], self_part], axis=0), query_house)
            + dot(jnp.concatenate([key_part, self_part], axis=1), key_house)
            - (2.0 * strength_grad * strength * inverse_square) * house
        )
        h_grads.append(house_grad.astype(BF))
        v_grads.append(value_grad[i].astype(BF))
        raw_grad = strength_grad * inverse_square * (2.0 * sigma * (1.0 - sigma))
        total_beta += jnp.where(lane == at * PER_STEP + i, raw_grad, 0.0)
    beta_grad[...] += total_beta
    update = None
    for index, (pieces, weight_ref) in enumerate(
        ((q_grads, wq_ref), (k_grads, wk_ref), (v_grads, wv_ref), (h_grads, wh_ref))
    ):
        joined = jnp.concatenate(pieces, axis=1)
        grads_ref[index] = joined
        term = dot_nt(joined, weight_ref[...])
        update = term if update is None else update + term
    normed_grad[...] += update

    @pl.when(at == pl.num_programs(0) - 1)
    def _():
        beta_low = beta_grad[...].astype(BF)
        grad = normed_grad[...] + dot_nt(beta_low, misc_ref[...])
        value = tokens_ref[...].astype(F32)
        scale = lax.rsqrt(jnp.mean(value * value, axis=1, keepdims=True) + EPSILON)
        scaled = grad * gain_row(misc_ref, 12)
        along = jnp.mean(scaled * value, axis=1, keepdims=True)
        grad_tokens_ref[...] = (
            hidden_grad_ref[...] + scale * scaled - value * (scale * scale * scale * along)
        )
        attn_gain = jnp.sum(grad * value * scale, axis=0, keepdims=True)
        attn_high, attn_low = two_parts(attn_gain)
        ffn_high, ffn_low = two_parts(ffn_gain_ref[...])
        gains = jnp.concatenate(
            [
                attn_high.astype(F32),
                attn_low.astype(F32),
                ffn_high.astype(F32),
                ffn_low.astype(F32),
                jnp.zeros((4, attn_gain.shape[1]), F32),
            ],
            axis=0,
        )
        place = lax.broadcasted_iota(jnp.int32, (8, 128), 0)
        lanes = lax.broadcasted_iota(jnp.int32, (8, 128), 1)
        pick = ((place < 4) & (lanes == 12 + place // 2)).astype(F32)
        misc_grad = dot(normed_t_ref[...], beta_low) + dot_tn(
            gains.astype(BF), pick.astype(BF)
        )
        misc_grad_ref[...] = misc_grad.astype(BF)


def attention_backward(tokens, normed_t, norm, saved, attn):
    q, k, v, h, probs, carried, inverse, beta = saved
    count, width = tokens.shape
    steps = width // SPAN
    half = width // 2
    whole = lambda i: (0, 0)
    rows = pl.BlockSpec((count, width), whole)
    row_block = pl.BlockSpec((count, SPAN), lambda i: (0, i))
    cell_block = pl.BlockSpec((PER_STEP, count, count), lambda i: (i, 0, 0))
    weight = lambda side, first: pl.BlockSpec((width, SPAN), lambda i: (side, first // SPAN + i))
    out_rows = lambda side: pl.BlockSpec((SPAN, half), lambda i: (side * steps + i, 0))
    return pl.pallas_call(
        attention_backward_kernel,
        grid=(steps,),
        in_specs=[
            rows,
            pl.BlockSpec((width, count), whole),
            pl.BlockSpec((1, width), whole),
            rows,
            rows,
            rows,
            rows,
            pl.BlockSpec((count, 128), whole),
            row_block,
            row_block,
            row_block,
            row_block,
            cell_block,
            cell_block,
            cell_block,
            out_rows(0),
            out_rows(1),
            weight(0, FIRST_AT),
            weight(0, SECOND_AT),
            weight(1, FIRST_AT),
            weight(1, SECOND_AT),
            pl.BlockSpec((width, 128), lambda i: (0, MISC_AT // 128)),
        ],
        out_specs=[
            pl.BlockSpec((4, count, SPAN), lambda i: (0, 0, i)),
            rows,
            rows,
            pl.BlockSpec((width, 128), whole),
        ],
        out_shape=[
            jax.ShapeDtypeStruct((4, count, width), BF),
            jax.ShapeDtypeStruct((count, width), BF),
            jax.ShapeDtypeStruct((count, width), F32),
            jax.ShapeDtypeStruct((width, 128), BF),
        ],
        scratch_shapes=[
            pltpu.VMEM((count, width), F32),
            pltpu.VMEM((count, 128), F32),
            pltpu.VMEM((count, width), F32),
            pltpu.VMEM((1, width), F32),
        ],
        compiler_params=pltpu.CompilerParams(vmem_limit_bytes=58 * MIB),
        cost_estimate=SHORT,
        name="attention_backward",
    )(
        tokens,
        normed_t,
        *norm,
        beta,
        q,
        k,
        v,
        h,
        probs,
        carried,
        inverse,
        attn,
        attn,
        attn,
        attn,
        attn,
        attn,
        attn,
    )


OWNERS = 16
AHEAD = ((), (1,), (0, 2))


def weight_gradient_kernel(segments, x_counts, y_counts, has_misc, second_half, *refs):
    place_ref, refs = refs[0], list(refs[2:])
    xs = [[refs.pop(0) for _ in range(n)] for n in x_counts]
    ys = [[refs.pop(0) for _ in range(n)] for n in y_counts]
    misc_ref = refs.pop(0) if has_misc else None
    at = pl.program_id(0)
    chips, height = xs[0][0].shape[0], xs[0][0].shape[1]
    if second_half:
        spots = [(refs[0], None, i, chips // 2 + OWNERS * at + i) for i in range(OWNERS)]
    else:
        got_lo, got_hi, keep, send = refs
        half = OWNERS // 2
        spots = [(keep, got_lo, i, half * at + i) for i in range(half)]
        spots += [(send, got_hi, i, chips // 4 + half * at + i) for i in range(half)]
    owners = [place_ref[spot[3]] for spot in spots]
    lefts = []
    for pieces in xs:
        rows = [
            jnp.concatenate([piece[owner].astype(F32) for piece in pieces], axis=1)
            for owner in owners
        ]
        lefts.append(jnp.concatenate(rows, axis=0).astype(BF))
    done = 0
    for x_at, y_at, matrix, start, size in segments:
        columns = slice(start, start + size)
        part = dot(
            lefts[x_at],
            jnp.concatenate([piece[matrix, :, columns] for piece in ys[y_at]], axis=0),
        )
        for index, (out, got, i, _) in enumerate(spots):
            value = part[index * height : (index + 1) * height]
            if got is not None:
                value = value + got[i, :, done : done + size].astype(F32)
            out[i, :, done : done + size] = value.astype(BF)
        done += size
    if has_misc:
        for (out, got, i, _), owner in zip(spots, owners):
            value = misc_ref[owner].astype(F32)
            if got is not None:
                value = value + got[i, :, done:].astype(F32)
            out[i, :, done:] = value.astype(BF)


def weight_gradient(places, core, xs, ys, segments, misc=None, got=None):
    chips, height = xs[0][0].shape[:2]
    columns = sum(segment[4] for segment in segments) + (128 if misc is not None else 0)
    operands, in_specs = [], []
    for pieces in xs:
        operands += pieces
        in_specs += [pl.BlockSpec(p.shape, lambda i, *_: (0, 0, 0)) for p in pieces]
    for pieces in ys:
        operands += pieces
        shape = pieces[0].shape
        if len(pieces) == 2:
            half = (shape[0], shape[1], shape[2] // 2)
            in_specs += [pl.BlockSpec(half, lambda i, _, c: (0, 0, c[0]))] * 2
        else:
            in_specs.append(pl.BlockSpec(shape, lambda i, *_: (0, 0, 0)))
    if misc is not None:
        operands.append(misc)
        in_specs.append(pl.BlockSpec(misc.shape, lambda i, *_: (0, 0, 0)))
    steps = chips // 2 // OWNERS
    if got is None:
        out_specs = [pl.BlockSpec((OWNERS, height, columns), lambda i, *_: (i, 0, 0))]
        out_shape = [jax.ShapeDtypeStruct((chips // 2, height, columns), BF)]
    else:
        block = (OWNERS // 2, height, columns)
        operands += [got, got]
        in_specs += [
            pl.BlockSpec(block, lambda i, *_: (i, 0, 0)),
            pl.BlockSpec(block, lambda i, *_: (steps + i, 0, 0)),
        ]
        out_specs = [pl.BlockSpec(block, lambda i, *_: (i, 0, 0))] * 2
        out_shape = [jax.ShapeDtypeStruct((chips // 4, height, columns), BF)] * 2
    x_counts, y_counts = [len(p) for p in xs], [len(p) for p in ys]
    return pl.pallas_call(
        functools.partial(
            weight_gradient_kernel, segments, x_counts, y_counts, misc is not None, got is None
        ),
        grid_spec=pltpu.PrefetchScalarGridSpec(
            num_scalar_prefetch=2, grid=(steps,), in_specs=in_specs, out_specs=out_specs
        ),
        out_shape=out_shape,
        compiler_params=pltpu.CompilerParams(vmem_limit_bytes=32 * MIB),
        cost_estimate=SHORT,
        name="weight_gradient" if got is None else "weight_gradient_add",
    )(places, core, *operands)


def fold(value):
    part = value.shape[2] // 4
    last = value[:, :, 3 * part :]
    below = jnp.concatenate([last[:, 8 * i : 8 * (i + 1)] for i in range(3)], axis=2)
    return jnp.concatenate([value[:, :, : 3 * part], below], axis=1)


def unfold(value):
    part = value.shape[1] // 3
    last = [value[24:, part * i : part * (i + 1)] for i in range(3)]
    return jnp.concatenate([value[:24], jnp.concatenate(last, axis=0)], axis=1)


def add_kernel(widths, *refs):
    total = sum(len(group) for group in widths)
    ins, outs = refs[: 4 * total], refs[4 * total :]
    at = 0
    for index, group in enumerate(widths):
        start = 0
        for width in group:
            keep_lo, keep_hi, got_lo, got_hi = ins[4 * at : 4 * at + 4]
            low = keep_lo[...].astype(F32) + got_lo[...].astype(F32)
            high = keep_hi[...].astype(F32) + got_hi[...].astype(F32)
            if low.shape[1] != outs[2 * index].shape[1]:
                pad = jnp.zeros((*low.shape[:2], 4 * width // 3 - low.shape[2]), F32)
                low = fold(jnp.concatenate([low, pad], axis=2))
                high = fold(jnp.concatenate([high, pad], axis=2))
            columns = slice(start, start + width)
            outs[2 * index][:, :, columns] = low.astype(BF)
            outs[2 * index + 1][:, :, columns] = high.astype(BF)
            start += width
            at += 1


def add_halves(groups):
    rows = groups[0][0][0].shape[0] // 2
    grid = max(1, rows // 2)
    block = rows // grid
    operands, in_specs, out_specs, shapes, widths = [], [], [], [], []
    for group in groups:
        for keep, got in group:
            shape = (block,) + keep.shape[1:]
            low = pl.BlockSpec(shape, lambda i: (i, 0, 0))
            high = pl.BlockSpec(shape, lambda i: (i + grid, 0, 0))
            operands += [keep, keep, got, got]
            in_specs += [low, high, low, high]
        height = group[0][0].shape[1]
        widths.append(
            [
                keep.shape[2] if keep.shape[1] == height else -(-keep.shape[2] // 512) * 384
                for keep, _ in group
            ]
        )
        shape = (block, height, sum(widths[-1]))
        out_specs += [pl.BlockSpec(shape, lambda i: (i, 0, 0))] * 2
        shapes += [jax.ShapeDtypeStruct((rows,) + shape[1:], BF)] * 2
    outs = pl.pallas_call(
        functools.partial(add_kernel, widths),
        grid=(grid,),
        in_specs=in_specs,
        out_specs=out_specs,
        out_shape=shapes,
        compiler_params=pltpu.CompilerParams(vmem_limit_bytes=24 * MIB),
        cost_estimate=SHORT,
        name="add_halves",
    )(*operands)
    return outs[0::2], outs[1::2]


def last_add_kernel(core_ref, *refs):
    first = core_ref[0] == 0
    *ins, mine, theirs, down = refs
    values = [
        ins[index][0].astype(F32) + ins[index + 1][0].astype(F32)
        for index in range(0, len(ins), 2)
    ]
    width = down.shape[1]
    down[...] = values[2][:, :width]
    values[2] = unfold(values[2][:, width:])
    start = 0
    for value in values:
        low, high = value[:12], value[12:]
        columns = slice(start, start + value.shape[1])
        mine[:, columns] = jnp.where(first, low, high)
        theirs[:, columns] = jnp.where(first, high, low).astype(BF)
        start += value.shape[1]


def last_add(core, pairs, down_shape):
    flat = [value for pair in pairs for value in pair]
    folded = pairs[2][0].shape[2] - down_shape[1]
    width = pairs[0][0].shape[2] + pairs[1][0].shape[2] + folded // 3 * 4
    shapes = [(12, width), (12, width), down_shape]
    return pl.pallas_call(
        last_add_kernel,
        grid_spec=pltpu.PrefetchScalarGridSpec(
            num_scalar_prefetch=1,
            grid=(1,),
            in_specs=[pl.BlockSpec(v.shape, lambda i, _: (0, 0, 0)) for v in flat],
            out_specs=[pl.BlockSpec(shape, lambda i, _: (0, 0)) for shape in shapes],
        ),
        out_shape=[jax.ShapeDtypeStruct(s, t) for s, t in zip(shapes, (F32, BF, F32))],
        compiler_params=pltpu.CompilerParams(vmem_limit_bytes=16 * MIB),
        cost_estimate=SHORT,
        name="last_add",
    )(core, *flat)


PLACES = (
    ((2048, 768),),
    ((2816, 512), (5376, 256)),
    ((5632, 768),),
    ((6400, 256), (6656, 512)),
    ((7168, 768),),
)
HIDDEN_PLACES = (0, 3328)
TILE = 256


def deal(parity):
    row = lax.broadcasted_iota(jnp.int32, (TILE // 2, TILE), 0)
    col = lax.broadcasted_iota(jnp.int32, (TILE // 2, TILE), 1)
    return (col == 64 * (row // 32) + 32 * parity + row % 32).astype(F32).astype(BF)


def finish_kernel(core_ref, mine, other, *outs):
    first = core_ref[0] == 0
    for pieces, out in zip(PLACES, outs):
        half = out.shape[1] // 2
        done = 0
        for start, width in pieces:
            a = mine[:, start : start + width]
            b = other[:, start : start + width].astype(F32)
            out[:, done : done + width] = jnp.where(first, a, b)
            out[:, half + done : half + done + width] = jnp.where(first, b, a)
            done += width
    own, their = deal(core_ref[0]), deal(1 - core_ref[0])
    rows = mine.shape[0]
    pad = jnp.zeros((16 - rows, TILE // 2), F32)
    for start, out in zip(HIDDEN_PLACES, outs[5:7]):
        tiles = out.shape[1] // TILE
        stack = lambda ref: jnp.concatenate(
            [
                jnp.concatenate(
                    [ref[:, start + 128 * t : start + 128 * (t + 1)].astype(F32), pad], axis=0
                )
                for t in range(tiles)
            ],
            axis=0,
        )
        high, low = two_parts(stack(mine))
        value = dot(high, own) + dot(low, own) + dot(stack(other).astype(BF), their)
        for t in range(tiles):
            out[:, TILE * t : TILE * (t + 1)] = value[16 * t : 16 * t + rows]
    misc = mine[:, 7936:8064] + other[:, 7936:8064].astype(F32)
    heads = outs[7].shape[1]
    outs[7][...] = misc[:, :heads]
    row = lax.broadcasted_iota(jnp.int32, (rows, 128), 0)
    col = lax.broadcasted_iota(jnp.int32, (rows, 128), 1)
    eye = (row == col).astype(F32).astype(BF)
    high, low = two_parts(misc)
    turned = dot_tn(high, eye) + dot_tn(low, eye)
    outs[8][...] = turned[heads : heads + 1, :rows]
    outs[9][...] = turned[heads + 1 : heads + 2, :rows]


def finish(core, mine, other, hidden_units, heads):
    rows = mine.shape[0]
    shapes = [(rows, 2 * sum(w for _, w in pieces)) for pieces in PLACES]
    shapes += [(rows, hidden_units), (rows, hidden_units), (rows, heads), (1, rows), (1, rows)]
    operands = (mine, other)
    return pl.pallas_call(
        finish_kernel,
        grid_spec=pltpu.PrefetchScalarGridSpec(
            num_scalar_prefetch=1,
            grid=(1,),
            in_specs=[pl.BlockSpec(v.shape, lambda i, _: (0, 0)) for v in operands],
            out_specs=[pl.BlockSpec(shape, lambda i, _: (0, 0)) for shape in shapes],
        ),
        out_shape=[jax.ShapeDtypeStruct(shape, F32) for shape in shapes],
        compiler_params=pltpu.CompilerParams(vmem_limit_bytes=16 * MIB),
        cost_estimate=SHORT,
        name="finish",
    )(core, *operands)


def pack_kernel(core_ref, gain_attn, gain_ffn, *refs):
    w_out, w_query, w_key, w_value, w_house, w_beta, w_gate, w_up = refs[:8]
    mine, theirs = refs[8:]
    first = core_ref[0] == 0
    rows, width = w_out.shape
    half, units = width // 2, w_gate.shape[1]
    gains = jnp.concatenate(
        [gain_attn[...].astype(F32), gain_ffn[...].astype(F32), jnp.zeros((6, rows), F32)], axis=0
    )
    place = lax.broadcasted_iota(jnp.int32, (8, 256), 0)
    lane = lax.broadcasted_iota(jnp.int32, (8, 256), 1)
    pick = ((place < 2) & (lane == 12 + place)).astype(F32)
    misc = dot_tn(gains.astype(BF), pick.astype(BF))
    beta = w_beta[...].astype(F32)
    misc += jnp.concatenate([beta, jnp.zeros((rows, 256 - beta.shape[1]), F32)], axis=1)
    split = lambda a, b: (jnp.where(first, a, b), jnp.where(first, b, a))
    pieces = [
        split(w_out[:, :half], w_out[:, half:]),
        (misc.astype(BF), misc.astype(BF)),
        split(w_query[...], w_value[...]),
        split(w_key[...], w_house[...]),
    ]
    for start, (own, other) in zip((0, MISC_AT, FIRST_AT, SECOND_AT), pieces):
        size = own.shape[1]
        mine[:, start : start + size] = own
        theirs[:, start : start + size] = other
    pad = jnp.zeros((16 - rows, TILE), F32)
    row = lax.broadcasted_iota(jnp.int32, (TILE, TILE), 0)
    col = lax.broadcasted_iota(jnp.int32, (TILE, TILE), 1)
    parity = jnp.where(col < 128, core_ref[0], 1 - core_ref[0])
    at = col % 128
    pick = (row == 64 * (at // 32) + 32 * parity + at % 32).astype(F32).astype(BF)
    tiles = units // TILE
    for start, ref in ((GATE_AT, w_gate), (UP_AT, w_up)):
        stack = jnp.concatenate(
            [
                jnp.concatenate([ref[:, TILE * t : TILE * (t + 1)].astype(F32), pad], axis=0)
                for t in range(tiles)
            ],
            axis=0,
        ).astype(BF)
        value = dot(stack, pick)
        for t in range(tiles):
            part = value[16 * t : 16 * t + rows].astype(BF)
            mine[:, start + 128 * t : start + 128 * (t + 1)] = part[:, :128]
            theirs[:, start + 128 * t : start + 128 * (t + 1)] = part[:, 128:]


def pack(core, gains, weights):
    rows, width = weights[0].shape
    shapes = [(rows, UP_AT + weights[6].shape[1] // 2)] * 2
    operands = [gain[None, :] for gain in gains] + list(weights)
    return pl.pallas_call(
        pack_kernel,
        grid_spec=pltpu.PrefetchScalarGridSpec(
            num_scalar_prefetch=1,
            grid=(1,),
            in_specs=[pl.BlockSpec(v.shape, lambda i, _: (0, 0)) for v in operands],
            out_specs=[pl.BlockSpec(shape, lambda i, _: (0, 0)) for shape in shapes],
        ),
        out_shape=[jax.ShapeDtypeStruct(shape, BF) for shape in shapes],
        compiler_params=pltpu.CompilerParams(vmem_limit_bytes=58 * MIB),
        cost_estimate=SHORT,
        name="pack",
    )(core, *operands)


def send_step(value, stream, step):
    count = lax.axis_size("fsdp")
    pairs = [(d, d ^ (2 * MASKS[stream][d & 1][step])) for d in range(count)]
    return lax.ppermute(value, "fsdp", pairs)


def after(values, earlier):
    flat, tree = jax.tree.flatten(values)
    kept = lax.optimization_barrier((*flat, *jax.tree.leaves(earlier)))
    return jax.tree.unflatten(tree, kept[: len(flat)])


def exchange(sends, step):
    return [send_step(send, stream, step) for stream, send in enumerate(sends)]


def blocks(turned, height):
    return turned.reshape(turned.shape[0] // height, height, turned.shape[1])


def gather_streams(parts):
    for step in range(5, 0, -1):
        gots = exchange(parts, step)
        parts = [jnp.concatenate(pair, axis=0) for pair in zip(parts, gots)]
    return parts, exchange(parts, 0)


def in_order_kernel(place_ref, *refs):
    lows, highs, out = refs[:3], refs[3:6], refs[6]
    half, _, width = lows[0].shape
    for stream, (low, high) in enumerate(zip(lows, highs)):
        columns = slice(width * stream, width * (stream + 1))
        for place in range(half):
            out[place_ref[stream, place], :, columns] = low[place]
            out[place_ref[stream, half + place], :, columns] = high[place]


def in_order(places, lows, highs):
    half, height, width = lows[0].shape
    shape = (2 * half, height, 3 * width)
    out = pl.pallas_call(
        in_order_kernel,
        grid_spec=pltpu.PrefetchScalarGridSpec(
            num_scalar_prefetch=1,
            grid=(1,),
            in_specs=[pl.BlockSpec(lows[0].shape, lambda i, _: (0, 0, 0))] * 6,
            out_specs=pl.BlockSpec(shape, lambda i, _: (0, 0, 0)),
        ),
        out_shape=jax.ShapeDtypeStruct(shape, BF),
        compiler_params=pltpu.CompilerParams(vmem_limit_bytes=58 * MIB),
        cost_estimate=SHORT,
        name="in_order",
    )(places, *lows, *highs)
    return out.reshape(2 * half * height, 3 * width)


def body(
    tokens,
    lengths,
    gain_attn,
    w_query,
    w_key,
    w_value,
    w_house,
    w_beta,
    w_out,
    gain_ffn,
    w_gate,
    w_up,
    w_down,
    cotangent,
):
    seqs, count, width = tokens.shape
    heads = w_beta.shape[1]
    hidden_units = w_gate.shape[1]
    half = width // 2
    devices = lax.axis_size("fsdp")
    me = lax.axis_index("fsdp")
    core, chip = me % 2, me // 2
    offsets = jnp.asarray(owner_offsets())
    places = jnp.where(core == 0, offsets[0], offsets[1]) ^ chip
    core_at = core.astype(jnp.int32)[None]

    mine, theirs = pack(
        core_at,
        (gain_attn, gain_ffn),
        (w_out, w_query, w_key, w_value, w_house, w_beta, w_gate, w_up),
    )
    stack = lambda own, other: jnp.where(
        core == 0,
        jnp.concatenate([own, other], axis=0),
        jnp.concatenate([other, own], axis=0),
    )
    slab = stack(mine, swap(theirs))
    by_core = [[*range(0, devices, 2), *range(1, devices, 2)]]
    attn = lax.all_gather(slab, "fsdp", axis=0, tiled=True, axis_index_groups=by_core)
    part, third = hidden_units // 2, width // 3
    lows, highs = gather_streams([w_down[None, :, third * s : third * (s + 1)] for s in range(3)])
    full_down = in_order(places, lows, highs)

    flat = tokens.reshape(count, width)
    valid = lax.broadcasted_iota(jnp.int32, (count, 1), 0) < lengths[0]
    cot = jnp.where(valid, cotangent.reshape(count, width), jnp.zeros((), BF))
    cots = (cot, swap(cot))

    normed_t, q, k, v, h, hidden, second, att_t, *cells, beta, gain = attention_forward(
        after(flat, full_down), lengths, attn
    )
    normed_x, att_x = (
        (blocks(value, 24), blocks(swap(value), 24)) for value in (normed_t, att_t)
    )
    second_t, product_t, gate_low, up_low, feed, feed_other, second_grad, grad_other = feedforward(
        core_at, (second, swap(second)), cots, attn, full_down
    )
    grad_got = swap(grad_other)
    mixed = jnp.where(valid, hidden + feed + swap(feed_other), 0.0).astype(BF)
    second_x, product_x = (blocks(second_t, 24),), (blocks(product_t, 32),)

    jobs = [
        ([second_x], [(gate_low[None],)], [(0, 0, 0, 0, part)]),
        ([second_x], [(up_low[None],)], [(0, 0, 0, 0, part)]),
        ([product_x], [(jnp.concatenate(cots, axis=0)[None],)], [(0, 0, 0, 0, width)]),
    ]
    late = after(places, (grad_got, normed_x, att_x))
    early = [places[0], late[1], late[2]]
    sends = [weight_gradient(early[s], core_at, *job)[0] for s, job in enumerate(jobs)]
    gots = exchange(sends, 0)

    grads, branch, grad_tokens, misc_grad = attention_backward(
        flat,
        normed_t,
        (gain, after(hidden, sends), cot, second_grad, grad_got),
        (q, k, v, h, *cells, beta),
        attn,
    )
    grads_y = (grads, swap(grads))
    branch_y = (branch[None], swap(branch)[None])
    misc_x = misc_grad.reshape(-1, 24, 128)
    attn_jobs = [
        ([normed_x], [grads_y], [(0, 0, 0, 0, 768), (0, 0, 1, 0, 512)]),
        ([normed_x], [grads_y], [(0, 0, 1, 512, 256), (0, 0, 2, 0, 768), (0, 0, 3, 0, 256)]),
        ([normed_x, att_x], [grads_y, branch_y], [(0, 0, 3, 256, 512), (1, 1, 0, 0, 768)], misc_x),
    ]
    attn_sends = [
        weight_gradient(after(places[s], [gots[t] for t in AHEAD[s]]), core_at, *job)[0]
        for s, job in enumerate(attn_jobs)
    ]
    attn_gots = exchange(attn_sends, 0)

    def kept(jobs, gots):
        pairs = [
            weight_gradient(places[s], core_at, *job, got=gots[s]) for s, job in enumerate(jobs)
        ]
        return [p[0] for p in pairs], [p[1] for p in pairs]

    keeps, sends = kept(jobs, gots)
    gots = exchange([after(sends[0], attn_gots[0]), *sends[1:]], 1)
    attn_keeps, attn_sends = kept(attn_jobs, [after(got, keeps) for got in attn_gots])
    attn_gots = exchange(attn_sends, 1)
    first, second = list(zip(keeps, gots)), list(zip(attn_keeps, attn_gots))
    groups = [list(pair) for pair in zip(first, second)]
    for step in range(2, 6):
        keeps, sends = add_halves(groups)
        gots = exchange(sends, step)
        groups = [[pair] for pair in zip(keeps, gots)]
    mine, theirs, grad_down = last_add(core_at, [group[0] for group in groups], w_down.shape)
    *large, grad_gate, grad_up, grad_beta, attn_gain, ffn_gain = finish(
        core_at, mine, swap(theirs), hidden_units, heads
    )

    return (
        mixed.reshape(seqs, count, width),
        grad_tokens.reshape(seqs, count, width),
        attn_gain.reshape(-1),
        *large[:4],
        grad_beta,
        large[4],
        ffn_gain.reshape(-1),
        grad_gate,
        grad_up,
        grad_down,
    )


def solution(mesh):
    rows = P("fsdp", None)
    line = P("fsdp")
    cube = P("fsdp", None, None)
    in_specs = (cube, line, line, rows, rows, rows, rows, rows, rows, line, rows, rows, rows, cube)
    out_specs = (cube, cube, line, rows, rows, rows, rows, rows, rows, line, rows, rows, rows)
    return jax.shard_map(body, mesh=mesh, in_specs=in_specs, out_specs=out_specs, check_vma=False)
```

```python
import functools

import jax
import jax.numpy as jnp
import numpy as np
from jax import lax
from jax.experimental import pallas as pl
from jax.experimental.pallas import tpu as pltpu
from jax.sharding import PartitionSpec as P

EPSILON = 1e-06
BF = jnp.bfloat16
F32 = jnp.float32
MIB = 1024 * 1024
SHORT = pl.CostEstimate(flops=1, bytes_accessed=1, transcendentals=0)
AXIS_UNIT = {"x": 16, "z": 4, "y": 1}
ORDERS = ("xzy", "zyx", "yxz")


def step_masks(stream, core):
    masks = []
    for axis in ORDERS[stream]:
        unit = AXIS_UNIT[axis]
        masks += [unit, 3 * unit] if core == 0 else [3 * unit, unit]
    return masks


MASKS = [[step_masks(stream, core) for core in (0, 1)] for stream in range(3)]


def owner_offsets():
    table = np.zeros((2, 3, 64), np.int32)
    for core in (0, 1):
        for stream in range(3):
            for place in range(64):
                value = 0
                for step, mask in enumerate(MASKS[stream][core]):
                    if (place >> (5 - step)) & 1:
                        value ^= mask
                table[core, stream, place] = value
    return table


def dot(left, right):
    return jnp.dot(left, right, preferred_element_type=F32)


def dot_nt(left, right):
    return lax.dot_general(left, right, (((1,), (1,)), ((), ())), preferred_element_type=F32)


def dot_tn(left, right):
    return lax.dot_general(left, right, (((0,), (0,)), ((), ())), preferred_element_type=F32)


def two_parts(value):
    high = value.astype(BF)
    return high, (value - high.astype(F32)).astype(BF)


def dot_fine(left, right):
    size = right.shape[1]
    wide = jnp.concatenate(two_parts(left), axis=1)
    pair = jnp.concatenate(two_parts(right), axis=1)
    out = dot(wide, jnp.concatenate([pair, pair], axis=0))
    return out[:, :size] + out[:, size:]


def swap(value):
    count = lax.axis_size("fsdp")
    return lax.ppermute(value, "fsdp", [(d, d ^ 1) for d in range(count)])


def gain_row(misc_ref, column):
    pick = (lax.broadcasted_iota(jnp.int32, (8, 128), 1) == column).astype(F32).astype(BF)
    return dot_nt(pick, misc_ref[...])[0:1]


def triangles(count):
    row = lax.broadcasted_iota(jnp.int32, (count, count), 0)
    col = lax.broadcasted_iota(jnp.int32, (count, count), 1)
    return row, col


def beta_of(raw, head):
    lane = lax.broadcasted_iota(jnp.int32, raw.shape, 1)
    return jnp.sum(jnp.where(lane == head, raw, 0.0), axis=1, keepdims=True)


def unit_lower_inverse(systems, row, col):
    size = row.shape[0]
    eye = (row == col).astype(F32)
    step = 1
    inverses = None
    while step < size:
        lower = ((row // step) % 2 == 1) & (col // step == row // step - 1)
        parts = [jnp.where(lower, system, 0.0) for system in systems]
        if step == 1:
            inverses = [eye - part for part in parts]
        else:
            middles = [dot_fine(inv, part) for inv, part in zip(inverses, parts)]
            inverses = [inv - dot_fine(mid, inv) for inv, mid in zip(inverses, middles)]
        step *= 2
    return inverses


PER_STEP = 6
SPAN = 128 * PER_STEP
BACK_STEP = 3
BACK_SPAN = 128 * BACK_STEP
FIRST_AT, SECOND_AT, GATE_AT, UP_AT, MISC_AT = 768, 2304, 3840, 5888, 7936


def attention_forward_kernel(
    length_ref,
    tokens_ref,
    wq_ref,
    wk_ref,
    wv_ref,
    wh_ref,
    out_lo_ref,
    out_hi_ref,
    misc_ref,
    normed_t_ref,
    q_ref,
    k_ref,
    v_ref,
    h_ref,
    hidden_ref,
    second_ref,
    att_t_ref,
    probs_ref,
    carried_ref,
    inverse_ref,
    beta_ref,
    gain_ref,
    normed_ref,
):
    at = pl.program_id(0)

    @pl.when(at == 0)
    def _():
        tokens = tokens_ref[...].astype(F32)
        scale = lax.rsqrt(jnp.mean(tokens * tokens, axis=1, keepdims=True) + EPSILON)
        value = tokens * scale * gain_row(misc_ref, 12)
        normed_ref[...] = value.astype(BF)
        normed_t_ref[...] = value.T.astype(BF)
        beta_ref[...] = dot(normed_ref[...], misc_ref[...])
        hidden_ref[...] = tokens

    normed = normed_ref[...]
    q_all = dot(normed, wq_ref[...]).astype(BF)
    k_all = dot(normed, wk_ref[...]).astype(BF)
    v_all = dot(normed, wv_ref[...]).astype(BF)
    h_all = dot(normed, wh_ref[...]).astype(BF)
    q_ref[...] = q_all
    k_ref[...] = k_all
    v_ref[...] = v_all
    h_ref[...] = h_all
    count = q_all.shape[0]
    row, col = triangles(count)
    strict = row > col
    upto = row >= col
    allowed = upto & (col < length_ref[0])
    raw = beta_ref[...]
    heads = range(PER_STEP)
    q, k, v, h = (
        [value[:, 128 * i : 128 * (i + 1)] for i in heads] for value in (q_all, k_all, v_all, h_all)
    )
    big = [
        dot_nt(jnp.concatenate([h[i], q[i]], axis=0), jnp.concatenate([h[i], k[i]], axis=0))
        for i in heads
    ]
    strength = []
    for i in heads:
        house = h[i].astype(F32)
        square = jnp.sum(house * house, axis=1, keepdims=True) + EPSILON
        beta = 2.0 * jax.nn.sigmoid(beta_of(raw, at * PER_STEP + i))
        strength.append(beta / square)
    systems = [jnp.where(strict, strength[i] * big[i][:count, :count], 0.0) for i in heads]
    sources = [jnp.where(strict, strength[i] * big[i][:count, count:], 0.0) for i in heads]
    inverses = unit_lower_inverse(systems, row, col)
    carried = [dot_fine(inverses[i], sources[i]) for i in heads]
    through = [
        dot_fine(jnp.where(upto, big[i][count:, :count], 0.0), carried[i]) for i in heads
    ]
    attended = []
    for i in heads:
        logits = (big[i][count:, count:] - through[i]) * 128 ** (-0.5)
        logits = jnp.where(allowed, logits, -1e30)
        highest = jnp.max(logits, axis=1, keepdims=True)
        weights = jnp.where(allowed, jnp.exp(logits - highest), 0.0)
        probs = weights / jnp.sum(weights, axis=1, keepdims=True)
        probs_ref[i] = probs
        carried_ref[i] = carried[i].astype(BF)
        inverse_ref[i] = inverses[i].astype(BF)
        att = dot(probs.astype(BF), v[i])
        attended.append(att.astype(BF))
        att_t_ref[128 * i : 128 * (i + 1), :] = att.T.astype(BF)
    att = jnp.concatenate(attended, axis=1)
    half = out_lo_ref.shape[1]
    hidden_ref[:, :half] += dot(att, out_lo_ref[...])
    hidden_ref[:, half:] += dot(att, out_hi_ref[...])

    @pl.when(at == pl.num_programs(0) - 1)
    def _():
        value = hidden_ref[...]
        scale = lax.rsqrt(jnp.mean(value * value, axis=1, keepdims=True) + EPSILON)
        gain = gain_row(misc_ref, 13)
        gain_ref[...] = gain
        second_ref[...] = (value * scale * gain).astype(BF)


def attention_forward(tokens, length, attn):
    count, width = tokens.shape
    steps = width // SPAN
    cell = (PER_STEP, count, count)
    whole = lambda i, *_: (0, 0)
    column = lambda i, *_: (0, i)
    weight = lambda half, first: pl.BlockSpec(
        (width, SPAN), lambda i, *_: (half, first // SPAN + i)
    )
    row_block = pl.BlockSpec((count, SPAN), column)
    cell_block = pl.BlockSpec(cell, lambda i, *_: (i, 0, 0))
    rows = jax.ShapeDtypeStruct((count, width), BF)
    turned = jax.ShapeDtypeStruct((width, count), BF)
    cells = (width // 128, count, count)
    return pl.pallas_call(
        attention_forward_kernel,
        grid_spec=pltpu.PrefetchScalarGridSpec(
            num_scalar_prefetch=1,
            grid=(steps,),
            in_specs=[
                pl.BlockSpec((count, width), whole),
                weight(0, FIRST_AT),
                weight(0, SECOND_AT),
                weight(1, FIRST_AT),
                weight(1, SECOND_AT),
                pl.BlockSpec((SPAN, width // 2), lambda i, *_: (i, 0)),
                pl.BlockSpec((SPAN, width // 2), lambda i, *_: (steps + i, 0)),
                pl.BlockSpec((width, 128), lambda i, *_: (0, MISC_AT // 128)),
            ],
            out_specs=[
                pl.BlockSpec((width, count), whole),
                row_block,
                row_block,
                row_block,
                row_block,
                pl.BlockSpec((count, width), whole),
                pl.BlockSpec((count, width), whole),
                pl.BlockSpec((SPAN, count), lambda i, *_: (i, 0)),
                cell_block,
                cell_block,
                cell_block,
                pl.BlockSpec((count, 128), whole),
                pl.BlockSpec((1, width), whole),
            ],
            scratch_shapes=[pltpu.VMEM((count, width), BF)],
        ),
        out_shape=[
            turned,
            rows,
            rows,
            rows,
            rows,
            jax.ShapeDtypeStruct((count, width), F32),
            rows,
            turned,
            jax.ShapeDtypeStruct(cells, F32),
            jax.ShapeDtypeStruct(cells, BF),
            jax.ShapeDtypeStruct(cells, BF),
            jax.ShapeDtypeStruct((count, 128), F32),
            jax.ShapeDtypeStruct((1, width), F32),
        ],
        compiler_params=pltpu.CompilerParams(vmem_limit_bytes=58 * MIB),
        cost_estimate=pl.CostEstimate(
            flops=8 * count * width * width + 12 * 60 * 2 * 128**3,
            bytes_accessed=10 * width * width,
            transcendentals=0,
        ),
        name="attention_forward",
    )(length, tokens, attn, attn, attn, attn, attn, attn, attn)


FF_BLOCK = 256


def feedforward_kernel(
    core_ref,
    second_own_ref,
    second_other_ref,
    cot_own_ref,
    cot_other_ref,
    wg_ref,
    wu_ref,
    wd_ref,
    second_t_ref,
    product_t_ref,
    gate_low_ref,
    up_low_ref,
    feed_own_ref,
    feed_other_ref,
    grad_own_ref,
    grad_other_ref,
    second,
    cot,
):
    count = second_own_ref.shape[0]

    @pl.when(pl.program_id(0) == 0)
    def _():
        second[:count] = second_own_ref[...]
        second[count:] = second_other_ref[...]
        cot[:count] = cot_own_ref[...]
        cot[count:] = cot_other_ref[...]
        second_t_ref[:, :count] = second_own_ref[...].astype(F32).T.astype(BF)
        second_t_ref[:, count:] = second_other_ref[...].astype(F32).T.astype(BF)
        feed_own_ref[...] = jnp.zeros_like(feed_own_ref)
        feed_other_ref[...] = jnp.zeros_like(feed_other_ref)
        grad_own_ref[...] = jnp.zeros_like(grad_own_ref)
        grad_other_ref[...] = jnp.zeros_like(grad_other_ref)

    gate = dot(second[...], wg_ref[...])
    upward = dot(second[...], wu_ref[...])
    sigma = jax.nn.sigmoid(gate)
    silu = gate * sigma
    product = silu * upward
    product_t_ref[...] = product.T.astype(BF)
    product_grad = dot_nt(cot[...], wd_ref[...])
    gate_low = (product_grad * upward * (sigma * (1.0 + gate * (1.0 - sigma)))).astype(BF)
    up_low = (product_grad * silu).astype(BF)
    gate_low_ref[...] = gate_low
    up_low_ref[...] = up_low
    feed = dot(product.astype(BF), wd_ref[...])
    feed_own_ref[...] += feed[:count]
    feed_other_ref[...] += feed[count:]
    grad = dot_nt(gate_low, wg_ref[...]) + dot_nt(up_low, wu_ref[...])
    grad_own_ref[...] += grad[:count]
    grad_other_ref[...] += grad[count:]


def feedforward(core, seconds, cots, attn, w_down):
    count, width = seconds[0].shape
    units = w_down.shape[0]
    whole = lambda i, _: (0, 0)
    rows = pl.BlockSpec((count, width), whole)
    columns = pl.BlockSpec((2 * count, FF_BLOCK), lambda i, _: (0, i))
    turned = pl.BlockSpec((FF_BLOCK, 2 * count), lambda i, _: (i, 0))
    weight = lambda first: pl.BlockSpec(
        (width, FF_BLOCK), lambda i, c: (c[0], first // FF_BLOCK + i)
    )
    sums = jax.ShapeDtypeStruct((count, width), F32)
    acts = jax.ShapeDtypeStruct((2 * count, units), BF)
    return pl.pallas_call(
        feedforward_kernel,
        grid_spec=pltpu.PrefetchScalarGridSpec(
            num_scalar_prefetch=1,
            grid=(units // FF_BLOCK,),
            in_specs=[rows] * 4
            + [
                weight(GATE_AT),
                weight(UP_AT),
                pl.BlockSpec((FF_BLOCK, width), lambda i, _: (i, 0)),
            ],
            out_specs=[pl.BlockSpec((width, 2 * count), whole), turned, columns, columns]
            + [rows] * 4,
            scratch_shapes=[pltpu.VMEM((2 * count, width), BF)] * 2,
        ),
        out_shape=[
            jax.ShapeDtypeStruct((width, 2 * count), BF),
            jax.ShapeDtypeStruct((units, 2 * count), BF),
            acts,
            acts,
            sums,
            sums,
            sums,
            sums,
        ],
        compiler_params=pltpu.CompilerParams(vmem_limit_bytes=46 * MIB),
        cost_estimate=pl.CostEstimate(
            flops=24 * count * width * units,
            bytes_accessed=6 * width * units,
            transcendentals=0,
        ),
        name="feedforward",
    )(core, *seconds, *cots, attn, attn, w_down)


def attention_backward_kernel(
    tokens_ref,
    normed_t_ref,
    gain_ref,
    hidden_ref,
    cot_ref,
    grad_own_ref,
    grad_got_ref,
    beta_ref,
    q_ref,
    k_ref,
    v_ref,
    h_ref,
    probs_ref,
    carried_ref,
    inverse_ref,
    wo_lo_ref,
    wo_hi_ref,
    wq_ref,
    wk_ref,
    wv_ref,
    wh_ref,
    misc_ref,
    grads_ref,
    branch_ref,
    grad_tokens_ref,
    misc_grad_ref,
    normed_grad,
    beta_grad,
    hidden_grad_ref,
    ffn_gain_ref,
):
    at = pl.program_id(0)
    half = wo_lo_ref.shape[1]

    @pl.when(at == 0)
    def _():
        normed_grad[...] = jnp.zeros_like(normed_grad)
        beta_grad[...] = jnp.zeros_like(beta_grad)
        value = hidden_ref[...]
        scale = lax.rsqrt(jnp.mean(value * value, axis=1, keepdims=True) + EPSILON)
        grad = grad_own_ref[...] + grad_got_ref[...]
        scaled = grad * gain_ref[...]
        along = jnp.mean(scaled * value, axis=1, keepdims=True)
        hidden_grad = (
            cot_ref[...].astype(F32) + scale * scaled - value * (scale * scale * scale * along)
        )
        hidden_grad_ref[...] = hidden_grad
        branch_ref[...] = hidden_grad.astype(BF)
        ffn_gain_ref[...] = jnp.sum(grad * value * scale, axis=0, keepdims=True)

    att_grad_all = (
        dot_nt(branch_ref[:, :half], wo_lo_ref[...]) + dot_nt(branch_ref[:, half:], wo_hi_ref[...])
    ).astype(BF)
    count = att_grad_all.shape[0]
    row, col = triangles(count)
    strict = row > col
    upto = row >= col
    raw = beta_ref[...]
    lane = lax.broadcasted_iota(jnp.int32, raw.shape, 1)
    heads = range(BACK_STEP)
    part = lambda ref: [ref[:, 128 * i : 128 * (i + 1)] for i in heads]
    q, k, v, h = part(q_ref), part(k_ref), part(v_ref), part(h_ref)
    att_grad = [att_grad_all[:, 128 * i : 128 * (i + 1)] for i in heads]
    big = [
        dot_nt(jnp.concatenate([h[i], q[i]], axis=0), jnp.concatenate([h[i], k[i]], axis=0))
        for i in heads
    ]
    probs = [probs_ref[i] for i in heads]
    carried = [carried_ref[i] for i in heads]
    inverse = [inverse_ref[i] for i in heads]
    probs_grad = [dot_nt(att_grad[i], v[i]) for i in heads]
    value_grad = [dot_tn(probs[i].astype(BF), att_grad[i]) for i in heads]
    logit_grad = []
    for i in heads:
        total = jnp.sum(probs_grad[i] * probs[i], axis=1, keepdims=True)
        logit_grad.append((probs[i] * (probs_grad[i] - total) * 128 ** (-0.5)).astype(BF))
    through_grad = [
        jnp.where(upto, -dot_nt(logit_grad[i], carried[i]), 0.0).astype(BF) for i in heads
    ]
    carried_grad = [
        -dot_tn(jnp.where(upto, big[i][count:, :count], 0.0).astype(BF), logit_grad[i])
        for i in heads
    ]
    solved = [dot_tn(inverse[i], carried_grad[i].astype(BF)) for i in heads]
    system_grad = [
        jnp.where(strict, -dot_nt(solved[i].astype(BF), carried[i]), 0.0) for i in heads
    ]
    source_grad = [jnp.where(strict, solved[i], 0.0) for i in heads]
    total_beta = jnp.zeros_like(raw)
    q_grads, k_grads, v_grads, h_grads = [], [], [], []
    for i in heads:
        house = h[i].astype(F32)
        inverse_square = 1.0 / (jnp.sum(house * house, axis=1, keepdims=True) + EPSILON)
        sigma = jax.nn.sigmoid(beta_of(raw, at * BACK_STEP + i))
        strength = 2.0 * sigma * inverse_square
        key_part = (strength * source_grad[i]).astype(BF)
        self_part = (strength * system_grad[i]).astype(BF)
        strength_grad = jnp.sum(
            source_grad[i] * big[i][:count, count:] + system_grad[i] * big[i][:count, :count],
            axis=1,
            keepdims=True,
        )
        key_house = jnp.concatenate([k[i], h[i]], axis=0)
        query_house = jnp.concatenate([q[i], h[i]], axis=0)
        q_grads.append(
            dot(jnp.concatenate([logit_grad[i], through_grad[i]], axis=1), key_house).astype(BF)
        )
        k_grads.append(
            dot_tn(jnp.concatenate([logit_grad[i], key_part], axis=0), query_house).astype(BF)
        )
        house_grad = (
            dot_tn(jnp.concatenate([through_grad[i], self_part], axis=0), query_house)
            + dot(jnp.concatenate([key_part, self_part], axis=1), key_house)
            - (2.0 * strength_grad * strength * inverse_square) * house
        )
        h_grads.append(house_grad.astype(BF))
        v_grads.append(value_grad[i].astype(BF))
        raw_grad = strength_grad * inverse_square * (2.0 * sigma * (1.0 - sigma))
        total_beta += jnp.where(lane == at * BACK_STEP + i, raw_grad, 0.0)
    beta_grad[...] += total_beta
    update = None
    for index, (pieces, weight_ref) in enumerate(
        ((q_grads, wq_ref), (k_grads, wk_ref), (v_grads, wv_ref), (h_grads, wh_ref))
    ):
        joined = jnp.concatenate(pieces, axis=1)
        grads_ref[index] = joined
        term = dot_nt(joined, weight_ref[...])
        update = term if update is None else update + term
    normed_grad[...] += update

    @pl.when(at == pl.num_programs(0) - 1)
    def _():
        beta_low = beta_grad[...].astype(BF)
        grad = normed_grad[...] + dot_nt(beta_low, misc_ref[...])
        value = tokens_ref[...].astype(F32)
        scale = lax.rsqrt(jnp.mean(value * value, axis=1, keepdims=True) + EPSILON)
        scaled = grad * gain_row(misc_ref, 12)
        along = jnp.mean(scaled * value, axis=1, keepdims=True)
        grad_tokens_ref[...] = (
            hidden_grad_ref[...] + scale * scaled - value * (scale * scale * scale * along)
        )
        attn_gain = jnp.sum(grad * value * scale, axis=0, keepdims=True)
        attn_high, attn_low = two_parts(attn_gain)
        ffn_high, ffn_low = two_parts(ffn_gain_ref[...])
        gains = jnp.concatenate(
            [
                attn_high.astype(F32),
                attn_low.astype(F32),
                ffn_high.astype(F32),
                ffn_low.astype(F32),
                jnp.zeros((4, attn_gain.shape[1]), F32),
            ],
            axis=0,
        )
        place = lax.broadcasted_iota(jnp.int32, (8, 128), 0)
        lanes = lax.broadcasted_iota(jnp.int32, (8, 128), 1)
        pick = ((place < 4) & (lanes == 12 + place // 2)).astype(F32)
        misc_grad = dot(normed_t_ref[...], beta_low) + dot_tn(
            gains.astype(BF), pick.astype(BF)
        )
        misc_grad_ref[...] = misc_grad.astype(BF)


def attention_backward(tokens, normed_t, norm, saved, attn):
    q, k, v, h, probs, carried, inverse, beta = saved
    count, width = tokens.shape
    steps = width // BACK_SPAN
    half = width // 2
    whole = lambda i: (0, 0)
    rows = pl.BlockSpec((count, width), whole)
    row_block = pl.BlockSpec((count, BACK_SPAN), lambda i: (0, i))
    cell_block = pl.BlockSpec((BACK_STEP, count, count), lambda i: (i, 0, 0))
    weight = lambda side, first: pl.BlockSpec((width, BACK_SPAN), lambda i: (side, first // BACK_SPAN + i))
    out_rows = lambda side: pl.BlockSpec((BACK_SPAN, half), lambda i: (side * steps + i, 0))
    return pl.pallas_call(
        attention_backward_kernel,
        grid=(steps,),
        in_specs=[
            rows,
            pl.BlockSpec((width, count), whole),
            pl.BlockSpec((1, width), whole),
            rows,
            rows,
            rows,
            rows,
            pl.BlockSpec((count, 128), whole),
            row_block,
            row_block,
            row_block,
            row_block,
            cell_block,
            cell_block,
            cell_block,
            out_rows(0),
            out_rows(1),
            weight(0, FIRST_AT),
            weight(0, SECOND_AT),
            weight(1, FIRST_AT),
            weight(1, SECOND_AT),
            pl.BlockSpec((width, 128), lambda i: (0, MISC_AT // 128)),
        ],
        out_specs=[
            pl.BlockSpec((4, count, BACK_SPAN), lambda i: (0, 0, i)),
            rows,
            rows,
            pl.BlockSpec((width, 128), whole),
        ],
        out_shape=[
            jax.ShapeDtypeStruct((4, count, width), BF),
            jax.ShapeDtypeStruct((count, width), BF),
            jax.ShapeDtypeStruct((count, width), F32),
            jax.ShapeDtypeStruct((width, 128), BF),
        ],
        scratch_shapes=[
            pltpu.VMEM((count, width), F32),
            pltpu.VMEM((count, 128), F32),
            pltpu.VMEM((count, width), F32),
            pltpu.VMEM((1, width), F32),
        ],
        compiler_params=pltpu.CompilerParams(vmem_limit_bytes=58 * MIB),
        cost_estimate=SHORT,
        name="attention_backward",
    )(
        tokens,
        normed_t,
        *norm,
        beta,
        q,
        k,
        v,
        h,
        probs,
        carried,
        inverse,
        attn,
        attn,
        attn,
        attn,
        attn,
        attn,
        attn,
    )


OWNERS = 16
AHEAD = ((), (1,), (0, 2))


def weight_gradient_kernel(segments, x_counts, y_counts, has_misc, second_half, *refs):
    place_ref, refs = refs[0], list(refs[2:])
    xs = [[refs.pop(0) for _ in range(n)] for n in x_counts]
    ys = [[refs.pop(0) for _ in range(n)] for n in y_counts]
    misc_ref = refs.pop(0) if has_misc else None
    at = pl.program_id(0)
    chips, height = xs[0][0].shape[0], xs[0][0].shape[1]
    if second_half:
        spots = [(refs[0], None, i, chips // 2 + OWNERS * at + i) for i in range(OWNERS)]
    else:
        got_lo, got_hi, keep, send = refs
        half = OWNERS // 2
        spots = [(keep, got_lo, i, half * at + i) for i in range(half)]
        spots += [(send, got_hi, i, chips // 4 + half * at + i) for i in range(half)]
    owners = [place_ref[spot[3]] for spot in spots]
    lefts = []
    for pieces in xs:
        rows = [
            jnp.concatenate([piece[owner].astype(F32) for piece in pieces], axis=1)
            for owner in owners
        ]
        lefts.append(jnp.concatenate(rows, axis=0).astype(BF))
    done = 0
    for x_at, y_at, matrix, start, size in segments:
        columns = slice(start, start + size)
        part = dot(
            lefts[x_at],
            jnp.concatenate([piece[matrix, :, columns] for piece in ys[y_at]], axis=0),
        )
        for index, (out, got, i, _) in enumerate(spots):
            value = part[index * height : (index + 1) * height]
            if got is not None:
                value = value + got[i, :, done : done + size].astype(F32)
            out[i, :, done : done + size] = value.astype(BF)
        done += size
    if has_misc:
        for (out, got, i, _), owner in zip(spots, owners):
            value = misc_ref[owner].astype(F32)
            if got is not None:
                value = value + got[i, :, done:].astype(F32)
            out[i, :, done:] = value.astype(BF)


def weight_gradient(places, core, xs, ys, segments, misc=None, got=None):
    chips, height = xs[0][0].shape[:2]
    columns = sum(segment[4] for segment in segments) + (128 if misc is not None else 0)
    operands, in_specs = [], []
    for pieces in xs:
        operands += pieces
        in_specs += [pl.BlockSpec(p.shape, lambda i, *_: (0, 0, 0)) for p in pieces]
    for pieces in ys:
        operands += pieces
        shape = pieces[0].shape
        if len(pieces) == 2:
            half = (shape[0], shape[1], shape[2] // 2)
            in_specs += [pl.BlockSpec(half, lambda i, _, c: (0, 0, c[0]))] * 2
        else:
            in_specs.append(pl.BlockSpec(shape, lambda i, *_: (0, 0, 0)))
    if misc is not None:
        operands.append(misc)
        in_specs.append(pl.BlockSpec(misc.shape, lambda i, *_: (0, 0, 0)))
    steps = chips // 2 // OWNERS
    if got is None:
        out_specs = [pl.BlockSpec((OWNERS, height, columns), lambda i, *_: (i, 0, 0))]
        out_shape = [jax.ShapeDtypeStruct((chips // 2, height, columns), BF)]
    else:
        block = (OWNERS // 2, height, columns)
        operands += [got, got]
        in_specs += [
            pl.BlockSpec(block, lambda i, *_: (i, 0, 0)),
            pl.BlockSpec(block, lambda i, *_: (steps + i, 0, 0)),
        ]
        out_specs = [pl.BlockSpec(block, lambda i, *_: (i, 0, 0))] * 2
        out_shape = [jax.ShapeDtypeStruct((chips // 4, height, columns), BF)] * 2
    x_counts, y_counts = [len(p) for p in xs], [len(p) for p in ys]
    return pl.pallas_call(
        functools.partial(
            weight_gradient_kernel, segments, x_counts, y_counts, misc is not None, got is None
        ),
        grid_spec=pltpu.PrefetchScalarGridSpec(
            num_scalar_prefetch=2, grid=(steps,), in_specs=in_specs, out_specs=out_specs
        ),
        out_shape=out_shape,
        compiler_params=pltpu.CompilerParams(vmem_limit_bytes=32 * MIB),
        cost_estimate=SHORT,
        name="weight_gradient" if got is None else "weight_gradient_add",
    )(places, core, *operands)


def fold(value):
    part = value.shape[2] // 4
    last = value[:, :, 3 * part :]
    below = jnp.concatenate([last[:, 8 * i : 8 * (i + 1)] for i in range(3)], axis=2)
    return jnp.concatenate([value[:, :, : 3 * part], below], axis=1)


def unfold(value):
    part = value.shape[1] // 3
    last = [value[24:, part * i : part * (i + 1)] for i in range(3)]
    return jnp.concatenate([value[:24], jnp.concatenate(last, axis=0)], axis=1)


def add_kernel(widths, *refs):
    total = sum(len(group) for group in widths)
    ins, outs = refs[: 4 * total], refs[4 * total :]
    at = 0
    for index, group in enumerate(widths):
        start = 0
        for width in group:
            keep_lo, keep_hi, got_lo, got_hi = ins[4 * at : 4 * at + 4]
            low = keep_lo[...].astype(F32) + got_lo[...].astype(F32)
            high = keep_hi[...].astype(F32) + got_hi[...].astype(F32)
            if low.shape[1] != outs[2 * index].shape[1]:
                pad = jnp.zeros((*low.shape[:2], 4 * width // 3 - low.shape[2]), F32)
                low = fold(jnp.concatenate([low, pad], axis=2))
                high = fold(jnp.concatenate([high, pad], axis=2))
            columns = slice(start, start + width)
            outs[2 * index][:, :, columns] = low.astype(BF)
            outs[2 * index + 1][:, :, columns] = high.astype(BF)
            start += width
            at += 1


def add_halves(groups):
    rows = groups[0][0][0].shape[0] // 2
    grid = max(1, rows // 2)
    block = rows // grid
    operands, in_specs, out_specs, shapes, widths = [], [], [], [], []
    for group in groups:
        for keep, got in group:
            shape = (block,) + keep.shape[1:]
            low = pl.BlockSpec(shape, lambda i: (i, 0, 0))
            high = pl.BlockSpec(shape, lambda i: (i + grid, 0, 0))
            operands += [keep, keep, got, got]
            in_specs += [low, high, low, high]
        height = group[0][0].shape[1]
        widths.append(
            [
                keep.shape[2] if keep.shape[1] == height else -(-keep.shape[2] // 512) * 384
                for keep, _ in group
            ]
        )
        shape = (block, height, sum(widths[-1]))
        out_specs += [pl.BlockSpec(shape, lambda i: (i, 0, 0))] * 2
        shapes += [jax.ShapeDtypeStruct((rows,) + shape[1:], BF)] * 2
    outs = pl.pallas_call(
        functools.partial(add_kernel, widths),
        grid=(grid,),
        in_specs=in_specs,
        out_specs=out_specs,
        out_shape=shapes,
        compiler_params=pltpu.CompilerParams(vmem_limit_bytes=24 * MIB),
        cost_estimate=SHORT,
        name="add_halves",
    )(*operands)
    return outs[0::2], outs[1::2]


def last_add_kernel(core_ref, *refs):
    first = core_ref[0] == 0
    *ins, mine, theirs, down = refs
    values = [
        ins[index][0].astype(F32) + ins[index + 1][0].astype(F32)
        for index in range(0, len(ins), 2)
    ]
    width = down.shape[1]
    down[...] = values[2][:, :width]
    values[2] = unfold(values[2][:, width:])
    start = 0
    for value in values:
        low, high = value[:12], value[12:]
        columns = slice(start, start + value.shape[1])
        mine[:, columns] = jnp.where(first, low, high)
        theirs[:, columns] = jnp.where(first, high, low).astype(BF)
        start += value.shape[1]


def last_add(core, pairs, down_shape):
    flat = [value for pair in pairs for value in pair]
    folded = pairs[2][0].shape[2] - down_shape[1]
    width = pairs[0][0].shape[2] + pairs[1][0].shape[2] + folded // 3 * 4
    shapes = [(12, width), (12, width), down_shape]
    return pl.pallas_call(
        last_add_kernel,
        grid_spec=pltpu.PrefetchScalarGridSpec(
            num_scalar_prefetch=1,
            grid=(1,),
            in_specs=[pl.BlockSpec(v.shape, lambda i, _: (0, 0, 0)) for v in flat],
            out_specs=[pl.BlockSpec(shape, lambda i, _: (0, 0)) for shape in shapes],
        ),
        out_shape=[jax.ShapeDtypeStruct(s, t) for s, t in zip(shapes, (F32, BF, F32))],
        compiler_params=pltpu.CompilerParams(vmem_limit_bytes=16 * MIB),
        cost_estimate=SHORT,
        name="last_add",
    )(core, *flat)


PLACES = (
    ((2048, 768),),
    ((2816, 512), (5376, 256)),
    ((5632, 768),),
    ((6400, 256), (6656, 512)),
    ((7168, 768),),
)
HIDDEN_PLACES = (0, 3328)
TILE = 256


def deal(parity):
    row = lax.broadcasted_iota(jnp.int32, (TILE // 2, TILE), 0)
    col = lax.broadcasted_iota(jnp.int32, (TILE // 2, TILE), 1)
    return (col == 64 * (row // 32) + 32 * parity + row % 32).astype(F32).astype(BF)


def finish_kernel(core_ref, mine, other, *outs):
    first = core_ref[0] == 0
    for pieces, out in zip(PLACES, outs):
        half = out.shape[1] // 2
        done = 0
        for start, width in pieces:
            a = mine[:, start : start + width]
            b = other[:, start : start + width].astype(F32)
            out[:, done : done + width] = jnp.where(first, a, b)
            out[:, half + done : half + done + width] = jnp.where(first, b, a)
            done += width
    own, their = deal(core_ref[0]), deal(1 - core_ref[0])
    rows = mine.shape[0]
    pad = jnp.zeros((16 - rows, TILE // 2), F32)
    for start, out in zip(HIDDEN_PLACES, outs[5:7]):
        tiles = out.shape[1] // TILE
        stack = lambda ref: jnp.concatenate(
            [
                jnp.concatenate(
                    [ref[:, start + 128 * t : start + 128 * (t + 1)].astype(F32), pad], axis=0
                )
                for t in range(tiles)
            ],
            axis=0,
        )
        high, low = two_parts(stack(mine))
        value = dot(high, own) + dot(low, own) + dot(stack(other).astype(BF), their)
        for t in range(tiles):
            out[:, TILE * t : TILE * (t + 1)] = value[16 * t : 16 * t + rows]
    misc = mine[:, 7936:8064] + other[:, 7936:8064].astype(F32)
    heads = outs[7].shape[1]
    outs[7][...] = misc[:, :heads]
    row = lax.broadcasted_iota(jnp.int32, (rows, 128), 0)
    col = lax.broadcasted_iota(jnp.int32, (rows, 128), 1)
    eye = (row == col).astype(F32).astype(BF)
    high, low = two_parts(misc)
    turned = dot_tn(high, eye) + dot_tn(low, eye)
    outs[8][...] = turned[heads : heads + 1, :rows]
    outs[9][...] = turned[heads + 1 : heads + 2, :rows]


def finish(core, mine, other, hidden_units, heads):
    rows = mine.shape[0]
    shapes = [(rows, 2 * sum(w for _, w in pieces)) for pieces in PLACES]
    shapes += [(rows, hidden_units), (rows, hidden_units), (rows, heads), (1, rows), (1, rows)]
    operands = (mine, other)
    return pl.pallas_call(
        finish_kernel,
        grid_spec=pltpu.PrefetchScalarGridSpec(
            num_scalar_prefetch=1,
            grid=(1,),
            in_specs=[pl.BlockSpec(v.shape, lambda i, _: (0, 0)) for v in operands],
            out_specs=[pl.BlockSpec(shape, lambda i, _: (0, 0)) for shape in shapes],
        ),
        out_shape=[jax.ShapeDtypeStruct(shape, F32) for shape in shapes],
        compiler_params=pltpu.CompilerParams(vmem_limit_bytes=16 * MIB),
        cost_estimate=SHORT,
        name="finish",
    )(core, *operands)


def pack_kernel(core_ref, gain_attn, gain_ffn, *refs):
    w_out, w_query, w_key, w_value, w_house, w_beta, w_gate, w_up = refs[:8]
    mine, theirs = refs[8:]
    first = core_ref[0] == 0
    rows, width = w_out.shape
    half, units = width // 2, w_gate.shape[1]
    gains = jnp.concatenate(
        [gain_attn[...].astype(F32), gain_ffn[...].astype(F32), jnp.zeros((6, rows), F32)], axis=0
    )
    place = lax.broadcasted_iota(jnp.int32, (8, 128), 0)
    lane = lax.broadcasted_iota(jnp.int32, (8, 128), 1)
    pick = ((place < 2) & (lane == 12 + place)).astype(F32)
    misc = dot_tn(gains.astype(BF), pick.astype(BF))
    beta = w_beta[...].astype(F32)
    misc += jnp.concatenate([beta, jnp.zeros((rows, 128 - beta.shape[1]), F32)], axis=1)
    split = lambda a, b: (jnp.where(first, a, b), jnp.where(first, b, a))
    pieces = [
        split(w_out[:, :half], w_out[:, half:]),
        (misc.astype(BF), misc.astype(BF)),
        split(w_query[...], w_value[...]),
        split(w_key[...], w_house[...]),
    ]
    for start, (own, other) in zip((0, MISC_AT, FIRST_AT, SECOND_AT), pieces):
        size = own.shape[1]
        mine[:, start : start + size] = own
        theirs[:, start : start + size] = other
    pad = jnp.zeros((16 - rows, TILE), F32)
    row = lax.broadcasted_iota(jnp.int32, (TILE, TILE), 0)
    col = lax.broadcasted_iota(jnp.int32, (TILE, TILE), 1)
    parity = jnp.where(col < 128, core_ref[0], 1 - core_ref[0])
    at = col % 128
    pick = (row == 64 * (at // 32) + 32 * parity + at % 32).astype(F32).astype(BF)
    tiles = units // TILE
    for start, ref in ((GATE_AT, w_gate), (UP_AT, w_up)):
        stack = jnp.concatenate(
            [
                jnp.concatenate([ref[:, TILE * t : TILE * (t + 1)].astype(F32), pad], axis=0)
                for t in range(tiles)
            ],
            axis=0,
        ).astype(BF)
        value = dot(stack, pick)
        for t in range(tiles):
            part = value[16 * t : 16 * t + rows].astype(BF)
            mine[:, start + 128 * t : start + 128 * (t + 1)] = part[:, :128]
            theirs[:, start + 128 * t : start + 128 * (t + 1)] = part[:, 128:]


def pack(core, gains, weights):
    rows, width = weights[0].shape
    shapes = [(rows, MISC_AT + 128)] * 2
    operands = [gain[None, :] for gain in gains] + list(weights)
    return pl.pallas_call(
        pack_kernel,
        grid_spec=pltpu.PrefetchScalarGridSpec(
            num_scalar_prefetch=1,
            grid=(1,),
            in_specs=[pl.BlockSpec(v.shape, lambda i, _: (0, 0)) for v in operands],
            out_specs=[pl.BlockSpec(shape, lambda i, _: (0, 0)) for shape in shapes],
        ),
        out_shape=[jax.ShapeDtypeStruct(shape, BF) for shape in shapes],
        compiler_params=pltpu.CompilerParams(vmem_limit_bytes=58 * MIB),
        cost_estimate=SHORT,
        name="pack",
    )(core, *operands)


def send_step(value, stream, step):
    count = lax.axis_size("fsdp")
    pairs = [(d, d ^ (2 * MASKS[stream][d & 1][step])) for d in range(count)]
    return lax.ppermute(value, "fsdp", pairs)


def after(values, earlier):
    flat, tree = jax.tree.flatten(values)
    kept = lax.optimization_barrier((*flat, *jax.tree.leaves(earlier)))
    return jax.tree.unflatten(tree, kept[: len(flat)])


def exchange(sends, step):
    return [send_step(send, stream, step) for stream, send in enumerate(sends)]


def blocks(turned, height):
    return turned.reshape(turned.shape[0] // height, height, turned.shape[1])


def gather_streams(parts):
    for step in range(5, 0, -1):
        gots = exchange(parts, step)
        parts = [jnp.concatenate(pair, axis=0) for pair in zip(parts, gots)]
    return parts, exchange(parts, 0)


def in_order_kernel(place_ref, *refs):
    lows, highs, out = refs[:3], refs[3:6], refs[6]
    half, _, width = lows[0].shape
    for stream, (low, high) in enumerate(zip(lows, highs)):
        columns = slice(width * stream, width * (stream + 1))
        for place in range(half):
            out[place_ref[stream, place], :, columns] = low[place]
            out[place_ref[stream, half + place], :, columns] = high[place]


def in_order(places, lows, highs):
    half, height, width = lows[0].shape
    shape = (2 * half, height, 3 * width)
    out = pl.pallas_call(
        in_order_kernel,
        grid_spec=pltpu.PrefetchScalarGridSpec(
            num_scalar_prefetch=1,
            grid=(1,),
            in_specs=[pl.BlockSpec(lows[0].shape, lambda i, _: (0, 0, 0))] * 6,
            out_specs=pl.BlockSpec(shape, lambda i, _: (0, 0, 0)),
        ),
        out_shape=jax.ShapeDtypeStruct(shape, BF),
        compiler_params=pltpu.CompilerParams(vmem_limit_bytes=58 * MIB),
        cost_estimate=SHORT,
        name="in_order",
    )(places, *lows, *highs)
    return out.reshape(2 * half * height, 3 * width)


def body(
    tokens,
    lengths,
    gain_attn,
    w_query,
    w_key,
    w_value,
    w_house,
    w_beta,
    w_out,
    gain_ffn,
    w_gate,
    w_up,
    w_down,
    cotangent,
):
    seqs, count, width = tokens.shape
    heads = w_beta.shape[1]
    hidden_units = w_gate.shape[1]
    half = width // 2
    devices = lax.axis_size("fsdp")
    me = lax.axis_index("fsdp")
    core, chip = me % 2, me // 2
    offsets = jnp.asarray(owner_offsets())
    places = jnp.where(core == 0, offsets[0], offsets[1]) ^ chip
    core_at = core.astype(jnp.int32)[None]

    mine, theirs = pack(
        core_at,
        (gain_attn, gain_ffn),
        (w_out, w_query, w_key, w_value, w_house, w_beta, w_gate, w_up),
    )
    stack = lambda own, other: jnp.where(
        core == 0,
        jnp.concatenate([own, other], axis=0),
        jnp.concatenate([other, own], axis=0),
    )
    slab = stack(mine, swap(theirs))
    by_core = [[*range(0, devices, 2), *range(1, devices, 2)]]
    attn = lax.all_gather(slab, "fsdp", axis=0, tiled=True, axis_index_groups=by_core)
    part, third = hidden_units // 2, width // 3
    lows, highs = gather_streams([w_down[None, :, third * s : third * (s + 1)] for s in range(3)])
    full_down = in_order(places, lows, highs)

    flat = tokens.reshape(count, width)
    valid = lax.broadcasted_iota(jnp.int32, (count, 1), 0) < lengths[0]
    cot = jnp.where(valid, cotangent.reshape(count, width), jnp.zeros((), BF))
    cots = (cot, swap(cot))

    normed_t, q, k, v, h, hidden, second, att_t, *cells, beta, gain = attention_forward(
        after(flat, full_down), lengths, attn
    )
    normed_x, att_x = (
        (blocks(value, 24), blocks(swap(value), 24)) for value in (normed_t, att_t)
    )
    second_t, product_t, gate_low, up_low, feed, feed_other, second_grad, grad_other = feedforward(
        core_at, (second, swap(second)), cots, attn, full_down
    )
    grad_got = swap(grad_other)
    mixed = jnp.where(valid, hidden + feed + swap(feed_other), 0.0).astype(BF)
    second_x, product_x = (blocks(second_t, 24),), (blocks(product_t, 32),)

    jobs = [
        ([second_x], [(gate_low[None],)], [(0, 0, 0, 0, part)]),
        ([second_x], [(up_low[None],)], [(0, 0, 0, 0, part)]),
        ([product_x], [(jnp.concatenate(cots, axis=0)[None],)], [(0, 0, 0, 0, width)]),
    ]
    late = after(places, (grad_got, normed_x, att_x))
    early = [places[0], late[1], late[2]]
    sends = [weight_gradient(early[s], core_at, *job)[0] for s, job in enumerate(jobs)]
    gots = exchange(sends, 0)

    grads, branch, grad_tokens, misc_grad = attention_backward(
        flat,
        normed_t,
        (gain, after(hidden, sends), cot, second_grad, grad_got),
        (q, k, v, h, *cells, beta),
        attn,
    )
    grads_y = (grads, swap(grads))
    branch_y = (branch[None], swap(branch)[None])
    misc_x = misc_grad.reshape(-1, 24, 128)
    attn_jobs = [
        ([normed_x], [grads_y], [(0, 0, 0, 0, 768), (0, 0, 1, 0, 512)]),
        ([normed_x], [grads_y], [(0, 0, 1, 512, 256), (0, 0, 2, 0, 768), (0, 0, 3, 0, 256)]),
        ([normed_x, att_x], [grads_y, branch_y], [(0, 0, 3, 256, 512), (1, 1, 0, 0, 768)], misc_x),
    ]
    attn_sends = [
        weight_gradient(after(places[s], [gots[t] for t in AHEAD[s]]), core_at, *job)[0]
        for s, job in enumerate(attn_jobs)
    ]
    attn_gots = exchange(attn_sends, 0)

    def kept(jobs, gots):
        pairs = [
            weight_gradient(places[s], core_at, *job, got=gots[s]) for s, job in enumerate(jobs)
        ]
        return [p[0] for p in pairs], [p[1] for p in pairs]

    keeps, sends = kept(jobs, gots)
    gots = exchange([after(sends[0], attn_gots[0]), *sends[1:]], 1)
    attn_keeps, attn_sends = kept(attn_jobs, [after(got, keeps) for got in attn_gots])
    attn_gots = exchange(attn_sends, 1)
    first, second = list(zip(keeps, gots)), list(zip(attn_keeps, attn_gots))
    groups = [list(pair) for pair in zip(first, second)]
    for step in range(2, 6):
        keeps, sends = add_halves(groups)
        gots = exchange(sends, step)
        groups = [[pair] for pair in zip(keeps, gots)]
    mine, theirs, grad_down = last_add(core_at, [group[0] for group in groups], w_down.shape)
    *large, grad_gate, grad_up, grad_beta, attn_gain, ffn_gain = finish(
        core_at, mine, swap(theirs), hidden_units, heads
    )

    return (
        mixed.reshape(seqs, count, width),
        grad_tokens.reshape(seqs, count, width),
        attn_gain.reshape(-1),
        *large[:4],
        grad_beta,
        large[4],
        ffn_gain.reshape(-1),
        grad_gate,
        grad_up,
        grad_down,
    )


def solution(mesh):
    rows = P("fsdp", None)
    line = P("fsdp")
    cube = P("fsdp", None, None)
    in_specs = (cube, line, line, rows, rows, rows, rows, rows, rows, line, rows, rows, rows, cube)
    out_specs = (cube, cube, line, rows, rows, rows, rows, rows, rows, line, rows, rows, rows)
    return jax.shard_map(body, mesh=mesh, in_specs=in_specs, out_specs=out_specs, check_vma=False)
```

```python
import functools

import jax
import jax.numpy as jnp
import numpy as np
from jax import lax
from jax.experimental import pallas as pl
from jax.experimental.pallas import tpu as pltpu
from jax.sharding import PartitionSpec as P

EPSILON = 1e-06
BF = jnp.bfloat16
F32 = jnp.float32
MIB = 1024 * 1024
SHORT = pl.CostEstimate(flops=1, bytes_accessed=1, transcendentals=0)
AXIS_UNIT = {"x": 16, "z": 4, "y": 1}
ORDERS = ("xzy", "zyx", "yxz")


def step_masks(stream, core):
    masks = []
    for axis in ORDERS[stream]:
        unit = AXIS_UNIT[axis]
        masks += [unit, 3 * unit] if core == 0 else [3 * unit, unit]
    return masks


MASKS = [[step_masks(stream, core) for core in (0, 1)] for stream in range(3)]


def owner_offsets():
    table = np.zeros((2, 3, 64), np.int32)
    for core in (0, 1):
        for stream in range(3):
            for place in range(64):
                value = 0
                for step, mask in enumerate(MASKS[stream][core]):
                    if (place >> (5 - step)) & 1:
                        value ^= mask
                table[core, stream, place] = value
    return table


def dot(left, right):
    return jnp.dot(left, right, preferred_element_type=F32)


def dot_nt(left, right):
    return lax.dot_general(left, right, (((1,), (1,)), ((), ())), preferred_element_type=F32)


def dot_tn(left, right):
    return lax.dot_general(left, right, (((0,), (0,)), ((), ())), preferred_element_type=F32)


def two_parts(value):
    high = value.astype(BF)
    return high, (value - high.astype(F32)).astype(BF)


def dot_fine(left, right):
    size = right.shape[1]
    wide = jnp.concatenate(two_parts(left), axis=1)
    pair = jnp.concatenate(two_parts(right), axis=1)
    out = dot(wide, jnp.concatenate([pair, pair], axis=0))
    return out[:, :size] + out[:, size:]


def swap(value):
    count = lax.axis_size("fsdp")
    return lax.ppermute(value, "fsdp", [(d, d ^ 1) for d in range(count)])


def gain_row(misc_ref, column):
    pick = (lax.broadcasted_iota(jnp.int32, (8, 128), 1) == column).astype(F32).astype(BF)
    return dot_nt(pick, misc_ref[...])[0:1]


def triangles(count):
    row = lax.broadcasted_iota(jnp.int32, (count, count), 0)
    col = lax.broadcasted_iota(jnp.int32, (count, count), 1)
    return row, col


def beta_of(raw, head):
    lane = lax.broadcasted_iota(jnp.int32, raw.shape, 1)
    return jnp.sum(jnp.where(lane == head, raw, 0.0), axis=1, keepdims=True)


def unit_lower_inverse(systems, row, col):
    size = row.shape[0]
    eye = (row == col).astype(F32)
    step = 1
    inverses = None
    while step < size:
        lower = ((row // step) % 2 == 1) & (col // step == row // step - 1)
        parts = [jnp.where(lower, system, 0.0) for system in systems]
        if step == 1:
            inverses = [eye - part for part in parts]
        else:
            middles = [dot_fine(inv, part) for inv, part in zip(inverses, parts)]
            inverses = [inv - dot_fine(mid, inv) for inv, mid in zip(inverses, middles)]
        step *= 2
    return inverses


PER_STEP = 6
SPAN = 128 * PER_STEP
BACK_STEP = 3
BACK_SPAN = 128 * BACK_STEP
FIRST_AT, SECOND_AT, GATE_AT, UP_AT, MISC_AT = 768, 2304, 3840, 5888, 7936


def attention_forward_kernel(
    length_ref,
    tokens_ref,
    wq_ref,
    wk_ref,
    wv_ref,
    wh_ref,
    out_lo_ref,
    out_hi_ref,
    misc_ref,
    normed_t_ref,
    q_ref,
    k_ref,
    v_ref,
    h_ref,
    hidden_ref,
    second_ref,
    att_t_ref,
    probs_ref,
    carried_ref,
    inverse_ref,
    beta_ref,
    gain_ref,
    normed_ref,
):
    at = pl.program_id(0)

    @pl.when(at == 0)
    def _():
        tokens = tokens_ref[...].astype(F32)
        scale = lax.rsqrt(jnp.mean(tokens * tokens, axis=1, keepdims=True) + EPSILON)
        value = tokens * scale * gain_row(misc_ref, 12)
        normed_ref[...] = value.astype(BF)
        normed_t_ref[...] = value.T.astype(BF)
        beta_ref[...] = dot(normed_ref[...], misc_ref[...])
        hidden_ref[...] = tokens

    normed = normed_ref[...]
    q_all = dot(normed, wq_ref[...]).astype(BF)
    k_all = dot(normed, wk_ref[...]).astype(BF)
    v_all = dot(normed, wv_ref[...]).astype(BF)
    h_all = dot(normed, wh_ref[...]).astype(BF)
    q_ref[...] = q_all
    k_ref[...] = k_all
    v_ref[...] = v_all
    h_ref[...] = h_all
    count = q_all.shape[0]
    row, col = triangles(count)
    strict = row > col
    upto = row >= col
    allowed = upto & (col < length_ref[0])
    raw = beta_ref[...]
    heads = range(PER_STEP)
    q, k, v, h = (
        [value[:, 128 * i : 128 * (i + 1)] for i in heads] for value in (q_all, k_all, v_all, h_all)
    )
    big = [
        dot_nt(jnp.concatenate([h[i], q[i]], axis=0), jnp.concatenate([h[i], k[i]], axis=0))
        for i in heads
    ]
    strength = []
    for i in heads:
        house = h[i].astype(F32)
        square = jnp.sum(house * house, axis=1, keepdims=True) + EPSILON
        beta = 2.0 * jax.nn.sigmoid(beta_of(raw, at * PER_STEP + i))
        strength.append(beta / square)
    systems = [jnp.where(strict, strength[i] * big[i][:count, :count], 0.0) for i in heads]
    sources = [jnp.where(strict, strength[i] * big[i][:count, count:], 0.0) for i in heads]
    inverses = unit_lower_inverse(systems, row, col)
    carried = [dot_fine(inverses[i], sources[i]) for i in heads]
    through = [
        dot_fine(jnp.where(upto, big[i][count:, :count], 0.0), carried[i]) for i in heads
    ]
    attended = []
    for i in heads:
        logits = (big[i][count:, count:] - through[i]) * 128 ** (-0.5)
        logits = jnp.where(allowed, logits, -1e30)
        highest = jnp.max(logits, axis=1, keepdims=True)
        weights = jnp.where(allowed, jnp.exp(logits - highest), 0.0)
        probs = weights / jnp.sum(weights, axis=1, keepdims=True)
        probs_ref[i] = probs
        carried_ref[i] = carried[i].astype(BF)
        inverse_ref[i] = inverses[i].astype(BF)
        att = dot(probs.astype(BF), v[i])
        attended.append(att.astype(BF))
        att_t_ref[128 * i : 128 * (i + 1), :] = att.T.astype(BF)
    att = jnp.concatenate(attended, axis=1)
    half = out_lo_ref.shape[1]
    hidden_ref[:, :half] += dot(att, out_lo_ref[...])
    hidden_ref[:, half:] += dot(att, out_hi_ref[...])

    @pl.when(at == pl.num_programs(0) - 1)
    def _():
        value = hidden_ref[...]
        scale = lax.rsqrt(jnp.mean(value * value, axis=1, keepdims=True) + EPSILON)
        gain = gain_row(misc_ref, 13)
        gain_ref[...] = gain
        second_ref[...] = (value * scale * gain).astype(BF)


def attention_forward(tokens, length, attn):
    count, width = tokens.shape
    steps = width // SPAN
    cell = (PER_STEP, count, count)
    whole = lambda i, *_: (0, 0)
    column = lambda i, *_: (0, i)
    weight = lambda half, first: pl.BlockSpec(
        (width, SPAN), lambda i, *_: (half, first // SPAN + i)
    )
    row_block = pl.BlockSpec((count, SPAN), column)
    cell_block = pl.BlockSpec(cell, lambda i, *_: (i, 0, 0))
    rows = jax.ShapeDtypeStruct((count, width), BF)
    turned = jax.ShapeDtypeStruct((width, count), BF)
    cells = (width // 128, count, count)
    return pl.pallas_call(
        attention_forward_kernel,
        grid_spec=pltpu.PrefetchScalarGridSpec(
            num_scalar_prefetch=1,
            grid=(steps,),
            in_specs=[
                pl.BlockSpec((count, width), whole),
                weight(0, FIRST_AT),
                weight(0, SECOND_AT),
                weight(1, FIRST_AT),
                weight(1, SECOND_AT),
                pl.BlockSpec((SPAN, width // 2), lambda i, *_: (i, 0)),
                pl.BlockSpec((SPAN, width // 2), lambda i, *_: (steps + i, 0)),
                pl.BlockSpec((width, 128), lambda i, *_: (0, MISC_AT // 128)),
            ],
            out_specs=[
                pl.BlockSpec((width, count), whole),
                row_block,
                row_block,
                row_block,
                row_block,
                pl.BlockSpec((count, width), whole),
                pl.BlockSpec((count, width), whole),
                pl.BlockSpec((SPAN, count), lambda i, *_: (i, 0)),
                cell_block,
                cell_block,
                cell_block,
                pl.BlockSpec((count, 128), whole),
                pl.BlockSpec((1, width), whole),
            ],
            scratch_shapes=[pltpu.VMEM((count, width), BF)],
        ),
        out_shape=[
            turned,
            rows,
            rows,
            rows,
            rows,
            jax.ShapeDtypeStruct((count, width), F32),
            rows,
            turned,
            jax.ShapeDtypeStruct(cells, F32),
            jax.ShapeDtypeStruct(cells, BF),
            jax.ShapeDtypeStruct(cells, BF),
            jax.ShapeDtypeStruct((count, 128), F32),
            jax.ShapeDtypeStruct((1, width), F32),
        ],
        compiler_params=pltpu.CompilerParams(vmem_limit_bytes=58 * MIB),
        cost_estimate=pl.CostEstimate(
            flops=8 * count * width * width + 12 * 60 * 2 * 128**3,
            bytes_accessed=10 * width * width,
            transcendentals=0,
        ),
        name="attention_forward",
    )(length, tokens, attn, attn, attn, attn, attn, attn, attn)


FF_BLOCK = 256


def feedforward_kernel(
    core_ref,
    second_own_ref,
    second_other_ref,
    cot_own_ref,
    cot_other_ref,
    wg_ref,
    wu_ref,
    wd_ref,
    second_t_ref,
    product_t_ref,
    gate_low_ref,
    up_low_ref,
    feed_own_ref,
    feed_other_ref,
    grad_own_ref,
    grad_other_ref,
    second,
    cot,
):
    count = second_own_ref.shape[0]

    @pl.when(pl.program_id(0) == 0)
    def _():
        second[:count] = second_own_ref[...]
        second[count:] = second_other_ref[...]
        cot[:count] = cot_own_ref[...]
        cot[count:] = cot_other_ref[...]
        second_t_ref[:, :count] = second_own_ref[...].astype(F32).T.astype(BF)
        second_t_ref[:, count:] = second_other_ref[...].astype(F32).T.astype(BF)
        feed_own_ref[...] = jnp.zeros_like(feed_own_ref)
        feed_other_ref[...] = jnp.zeros_like(feed_other_ref)
        grad_own_ref[...] = jnp.zeros_like(grad_own_ref)
        grad_other_ref[...] = jnp.zeros_like(grad_other_ref)

    gate = dot(second[...], wg_ref[...])
    upward = dot(second[...], wu_ref[...])
    sigma = jax.nn.sigmoid(gate)
    silu = gate * sigma
    product = silu * upward
    product_t_ref[...] = product.T.astype(BF)
    product_grad = dot_nt(cot[...], wd_ref[...])
    gate_low = (product_grad * upward * (sigma * (1.0 + gate * (1.0 - sigma)))).astype(BF)
    up_low = (product_grad * silu).astype(BF)
    gate_low_ref[...] = gate_low
    up_low_ref[...] = up_low
    feed = dot(product.astype(BF), wd_ref[...])
    feed_own_ref[...] += feed[:count]
    feed_other_ref[...] += feed[count:]
    grad = dot_nt(gate_low, wg_ref[...]) + dot_nt(up_low, wu_ref[...])
    grad_own_ref[...] += grad[:count]
    grad_other_ref[...] += grad[count:]


def feedforward(core, seconds, cots, attn, w_down):
    count, width = seconds[0].shape
    units = w_down.shape[0]
    whole = lambda i, _: (0, 0)
    rows = pl.BlockSpec((count, width), whole)
    columns = pl.BlockSpec((2 * count, FF_BLOCK), lambda i, _: (0, i))
    turned = pl.BlockSpec((FF_BLOCK, 2 * count), lambda i, _: (i, 0))
    weight = lambda first: pl.BlockSpec(
        (width, FF_BLOCK), lambda i, c: (c[0], first // FF_BLOCK + i)
    )
    sums = jax.ShapeDtypeStruct((count, width), F32)
    acts = jax.ShapeDtypeStruct((2 * count, units), BF)
    return pl.pallas_call(
        feedforward_kernel,
        grid_spec=pltpu.PrefetchScalarGridSpec(
            num_scalar_prefetch=1,
            grid=(units // FF_BLOCK,),
            in_specs=[rows] * 4
            + [
                weight(GATE_AT),
                weight(UP_AT),
                pl.BlockSpec((FF_BLOCK, width), lambda i, _: (i, 0)),
            ],
            out_specs=[pl.BlockSpec((width, 2 * count), whole), turned, columns, columns]
            + [rows] * 4,
            scratch_shapes=[pltpu.VMEM((2 * count, width), BF)] * 2,
        ),
        out_shape=[
            jax.ShapeDtypeStruct((width, 2 * count), BF),
            jax.ShapeDtypeStruct((units, 2 * count), BF),
            acts,
            acts,
            sums,
            sums,
            sums,
            sums,
        ],
        compiler_params=pltpu.CompilerParams(vmem_limit_bytes=46 * MIB),
        cost_estimate=pl.CostEstimate(
            flops=24 * count * width * units,
            bytes_accessed=6 * width * units,
            transcendentals=0,
        ),
        name="feedforward",
    )(core, *seconds, *cots, attn, attn, w_down)


def attention_backward_kernel(
    tokens_ref,
    normed_t_ref,
    gain_ref,
    hidden_ref,
    cot_ref,
    grad_own_ref,
    grad_got_ref,
    beta_ref,
    q_ref,
    k_ref,
    v_ref,
    h_ref,
    probs_ref,
    carried_ref,
    inverse_ref,
    wo_lo_ref,
    wo_hi_ref,
    wq_ref,
    wk_ref,
    wv_ref,
    wh_ref,
    misc_ref,
    grads_ref,
    branch_ref,
    grad_tokens_ref,
    misc_grad_ref,
    normed_grad,
    beta_grad,
    hidden_grad_ref,
    ffn_gain_ref,
):
    at = pl.program_id(0)
    half = wo_lo_ref.shape[1]

    @pl.when(at == 0)
    def _():
        normed_grad[...] = jnp.zeros_like(normed_grad)
        beta_grad[...] = jnp.zeros_like(beta_grad)
        value = hidden_ref[...]
        scale = lax.rsqrt(jnp.mean(value * value, axis=1, keepdims=True) + EPSILON)
        grad = grad_own_ref[...] + grad_got_ref[...]
        scaled = grad * gain_ref[...]
        along = jnp.mean(scaled * value, axis=1, keepdims=True)
        hidden_grad = (
            cot_ref[...].astype(F32) + scale * scaled - value * (scale * scale * scale * along)
        )
        hidden_grad_ref[...] = hidden_grad
        branch_ref[...] = hidden_grad.astype(BF)
        ffn_gain_ref[...] = jnp.sum(grad * value * scale, axis=0, keepdims=True)

    att_grad_all = (
        dot_nt(branch_ref[:, :half], wo_lo_ref[...]) + dot_nt(branch_ref[:, half:], wo_hi_ref[...])
    ).astype(BF)
    count = att_grad_all.shape[0]
    row, col = triangles(count)
    strict = row > col
    upto = row >= col
    raw = beta_ref[...]
    lane = lax.broadcasted_iota(jnp.int32, raw.shape, 1)
    heads = range(BACK_STEP)
    part = lambda ref: [ref[:, 128 * i : 128 * (i + 1)] for i in heads]
    q, k, v, h = part(q_ref), part(k_ref), part(v_ref), part(h_ref)
    att_grad = [att_grad_all[:, 128 * i : 128 * (i + 1)] for i in heads]
    big = [
        dot_nt(jnp.concatenate([h[i], q[i]], axis=0), jnp.concatenate([h[i], k[i]], axis=0))
        for i in heads
    ]
    probs = [probs_ref[i] for i in heads]
    carried = [carried_ref[i] for i in heads]
    inverse = [inverse_ref[i] for i in heads]
    probs_grad = [dot_nt(att_grad[i], v[i]) for i in heads]
    value_grad = [dot_tn(probs[i].astype(BF), att_grad[i]) for i in heads]
    logit_grad = []
    for i in heads:
        total = jnp.sum(probs_grad[i] * probs[i], axis=1, keepdims=True)
        logit_grad.append((probs[i] * (probs_grad[i] - total) * 128 ** (-0.5)).astype(BF))
    through_grad = [
        jnp.where(upto, -dot_nt(logit_grad[i], carried[i]), 0.0).astype(BF) for i in heads
    ]
    carried_grad = [
        -dot_tn(jnp.where(upto, big[i][count:, :count], 0.0).astype(BF), logit_grad[i])
        for i in heads
    ]
    solved = [dot_tn(inverse[i], carried_grad[i].astype(BF)) for i in heads]
    system_grad = [
        jnp.where(strict, -dot_nt(solved[i].astype(BF), carried[i]), 0.0) for i in heads
    ]
    source_grad = [jnp.where(strict, solved[i], 0.0) for i in heads]
    total_beta = jnp.zeros_like(raw)
    q_grads, k_grads, v_grads, h_grads = [], [], [], []
    for i in heads:
        house = h[i].astype(F32)
        inverse_square = 1.0 / (jnp.sum(house * house, axis=1, keepdims=True) + EPSILON)
        sigma = jax.nn.sigmoid(beta_of(raw, at * BACK_STEP + i))
        strength = 2.0 * sigma * inverse_square
        key_part = (strength * source_grad[i]).astype(BF)
        self_part = (strength * system_grad[i]).astype(BF)
        strength_grad = jnp.sum(
            source_grad[i] * big[i][:count, count:] + system_grad[i] * big[i][:count, :count],
            axis=1,
            keepdims=True,
        )
        key_house = jnp.concatenate([k[i], h[i]], axis=0)
        query_house = jnp.concatenate([q[i], h[i]], axis=0)
        q_grads.append(
            dot(jnp.concatenate([logit_grad[i], through_grad[i]], axis=1), key_house).astype(BF)
        )
        k_grads.append(
            dot_tn(jnp.concatenate([logit_grad[i], key_part], axis=0), query_house).astype(BF)
        )
        house_grad = (
            dot_tn(jnp.concatenate([through_grad[i], self_part], axis=0), query_house)
            + dot(jnp.concatenate([key_part, self_part], axis=1), key_house)
            - (2.0 * strength_grad * strength * inverse_square) * house
        )
        h_grads.append(house_grad.astype(BF))
        v_grads.append(value_grad[i].astype(BF))
        raw_grad = strength_grad * inverse_square * (2.0 * sigma * (1.0 - sigma))
        total_beta += jnp.where(lane == at * BACK_STEP + i, raw_grad, 0.0)
    beta_grad[...] += total_beta
    update = None
    for index, (pieces, weight_ref) in enumerate(
        ((q_grads, wq_ref), (k_grads, wk_ref), (v_grads, wv_ref), (h_grads, wh_ref))
    ):
        joined = jnp.concatenate(pieces, axis=1)
        grads_ref[index] = joined
        term = dot_nt(joined, weight_ref[...])
        update = term if update is None else update + term
    normed_grad[...] += update

    @pl.when(at == pl.num_programs(0) - 1)
    def _():
        beta_low = beta_grad[...].astype(BF)
        grad = normed_grad[...] + dot_nt(beta_low, misc_ref[...])
        value = tokens_ref[...].astype(F32)
        scale = lax.rsqrt(jnp.mean(value * value, axis=1, keepdims=True) + EPSILON)
        scaled = grad * gain_row(misc_ref, 12)
        along = jnp.mean(scaled * value, axis=1, keepdims=True)
        grad_tokens_ref[...] = (
            hidden_grad_ref[...] + scale * scaled - value * (scale * scale * scale * along)
        )
        attn_gain = jnp.sum(grad * value * scale, axis=0, keepdims=True)
        attn_high, attn_low = two_parts(attn_gain)
        ffn_high, ffn_low = two_parts(ffn_gain_ref[...])
        gains = jnp.concatenate(
            [
                attn_high.astype(F32),
                attn_low.astype(F32),
                ffn_high.astype(F32),
                ffn_low.astype(F32),
                jnp.zeros((4, attn_gain.shape[1]), F32),
            ],
            axis=0,
        )
        place = lax.broadcasted_iota(jnp.int32, (8, 128), 0)
        lanes = lax.broadcasted_iota(jnp.int32, (8, 128), 1)
        pick = ((place < 4) & (lanes == 12 + place // 2)).astype(F32)
        misc_grad = dot(normed_t_ref[...], beta_low) + dot_tn(
            gains.astype(BF), pick.astype(BF)
        )
        misc_grad_ref[...] = misc_grad.astype(BF)


def attention_backward(tokens, normed_t, norm, saved, attn):
    q, k, v, h, probs, carried, inverse, beta = saved
    count, width = tokens.shape
    steps = width // BACK_SPAN
    half = width // 2
    whole = lambda i: (0, 0)
    rows = pl.BlockSpec((count, width), whole)
    row_block = pl.BlockSpec((count, BACK_SPAN), lambda i: (0, i))
    cell_block = pl.BlockSpec((BACK_STEP, count, count), lambda i: (i, 0, 0))
    weight = lambda side, first: pl.BlockSpec((width, BACK_SPAN), lambda i: (side, first // BACK_SPAN + i))
    out_rows = lambda side: pl.BlockSpec((BACK_SPAN, half), lambda i: (side * steps + i, 0))
    return pl.pallas_call(
        attention_backward_kernel,
        grid=(steps,),
        in_specs=[
            rows,
            pl.BlockSpec((width, count), whole),
            pl.BlockSpec((1, width), whole),
            rows,
            rows,
            rows,
            rows,
            pl.BlockSpec((count, 128), whole),
            row_block,
            row_block,
            row_block,
            row_block,
            cell_block,
            cell_block,
            cell_block,
            out_rows(0),
            out_rows(1),
            weight(0, FIRST_AT),
            weight(0, SECOND_AT),
            weight(1, FIRST_AT),
            weight(1, SECOND_AT),
            pl.BlockSpec((width, 128), lambda i: (0, MISC_AT // 128)),
        ],
        out_specs=[
            pl.BlockSpec((4, count, BACK_SPAN), lambda i: (0, 0, i)),
            rows,
            rows,
            pl.BlockSpec((width, 128), whole),
        ],
        out_shape=[
            jax.ShapeDtypeStruct((4, count, width), BF),
            jax.ShapeDtypeStruct((count, width), BF),
            jax.ShapeDtypeStruct((count, width), F32),
            jax.ShapeDtypeStruct((width, 128), BF),
        ],
        scratch_shapes=[
            pltpu.VMEM((count, width), F32),
            pltpu.VMEM((count, 128), F32),
            pltpu.VMEM((count, width), F32),
            pltpu.VMEM((1, width), F32),
        ],
        compiler_params=pltpu.CompilerParams(vmem_limit_bytes=58 * MIB),
        cost_estimate=SHORT,
        name="attention_backward",
    )(
        tokens,
        normed_t,
        *norm,
        beta,
        q,
        k,
        v,
        h,
        probs,
        carried,
        inverse,
        attn,
        attn,
        attn,
        attn,
        attn,
        attn,
        attn,
    )


OWNERS = 16
AHEAD = ((), (1, 2), (0,))


def weight_gradient_kernel(segments, x_counts, y_counts, has_misc, second_half, *refs):
    place_ref, refs = refs[0], list(refs[2:])
    xs = [[refs.pop(0) for _ in range(n)] for n in x_counts]
    ys = [[refs.pop(0) for _ in range(n)] for n in y_counts]
    misc_ref = refs.pop(0) if has_misc else None
    at = pl.program_id(0)
    chips, height = xs[0][0].shape[0], xs[0][0].shape[1]
    if second_half:
        spots = [(refs[0], None, i, chips // 2 + OWNERS * at + i) for i in range(OWNERS)]
    else:
        got_lo, got_hi, keep, send = refs
        half = OWNERS // 2
        spots = [(keep, got_lo, i, half * at + i) for i in range(half)]
        spots += [(send, got_hi, i, chips // 4 + half * at + i) for i in range(half)]
    owners = [place_ref[spot[3]] for spot in spots]
    lefts = []
    for pieces in xs:
        rows = [
            jnp.concatenate([piece[owner].astype(F32) for piece in pieces], axis=1)
            for owner in owners
        ]
        lefts.append(jnp.concatenate(rows, axis=0).astype(BF))
    done = 0
    for x_at, y_at, matrix, start, size in segments:
        columns = slice(start, start + size)
        part = dot(
            lefts[x_at],
            jnp.concatenate([piece[matrix, :, columns] for piece in ys[y_at]], axis=0),
        )
        for index, (out, got, i, _) in enumerate(spots):
            value = part[index * height : (index + 1) * height]
            if got is not None:
                value = value + got[i, :, done : done + size].astype(F32)
            out[i, :, done : done + size] = value.astype(BF)
        done += size
    if has_misc:
        for (out, got, i, _), owner in zip(spots, owners):
            value = misc_ref[owner].astype(F32)
            if got is not None:
                value = value + got[i, :, done:].astype(F32)
            out[i, :, done:] = value.astype(BF)


def weight_gradient(places, core, xs, ys, segments, misc=None, got=None):
    chips, height = xs[0][0].shape[:2]
    columns = sum(segment[4] for segment in segments) + (128 if misc is not None else 0)
    operands, in_specs = [], []
    for pieces in xs:
        operands += pieces
        in_specs += [pl.BlockSpec(p.shape, lambda i, *_: (0, 0, 0)) for p in pieces]
    for pieces in ys:
        operands += pieces
        shape = pieces[0].shape
        if len(pieces) == 2:
            half = (shape[0], shape[1], shape[2] // 2)
            in_specs += [pl.BlockSpec(half, lambda i, _, c: (0, 0, c[0]))] * 2
        else:
            in_specs.append(pl.BlockSpec(shape, lambda i, *_: (0, 0, 0)))
    if misc is not None:
        operands.append(misc)
        in_specs.append(pl.BlockSpec(misc.shape, lambda i, *_: (0, 0, 0)))
    steps = chips // 2 // OWNERS
    if got is None:
        out_specs = [pl.BlockSpec((OWNERS, height, columns), lambda i, *_: (i, 0, 0))]
        out_shape = [jax.ShapeDtypeStruct((chips // 2, height, columns), BF)]
    else:
        block = (OWNERS // 2, height, columns)
        operands += [got, got]
        in_specs += [
            pl.BlockSpec(block, lambda i, *_: (i, 0, 0)),
            pl.BlockSpec(block, lambda i, *_: (steps + i, 0, 0)),
        ]
        out_specs = [pl.BlockSpec(block, lambda i, *_: (i, 0, 0))] * 2
        out_shape = [jax.ShapeDtypeStruct((chips // 4, height, columns), BF)] * 2
    x_counts, y_counts = [len(p) for p in xs], [len(p) for p in ys]
    return pl.pallas_call(
        functools.partial(
            weight_gradient_kernel, segments, x_counts, y_counts, misc is not None, got is None
        ),
        grid_spec=pltpu.PrefetchScalarGridSpec(
            num_scalar_prefetch=2, grid=(steps,), in_specs=in_specs, out_specs=out_specs
        ),
        out_shape=out_shape,
        compiler_params=pltpu.CompilerParams(vmem_limit_bytes=32 * MIB),
        cost_estimate=SHORT,
        name="weight_gradient" if got is None else "weight_gradient_add",
    )(places, core, *operands)


def fold(value):
    part = value.shape[2] // 4
    last = value[:, :, 3 * part :]
    below = jnp.concatenate([last[:, 8 * i : 8 * (i + 1)] for i in range(3)], axis=2)
    return jnp.concatenate([value[:, :, : 3 * part], below], axis=1)


def unfold(value):
    part = value.shape[1] // 3
    last = [value[24:, part * i : part * (i + 1)] for i in range(3)]
    return jnp.concatenate([value[:24], jnp.concatenate(last, axis=0)], axis=1)


def add_kernel(widths, *refs):
    total = sum(len(group) for group in widths)
    ins, outs = refs[: 4 * total], refs[4 * total :]
    at = 0
    for index, group in enumerate(widths):
        start = 0
        for width in group:
            keep_lo, keep_hi, got_lo, got_hi = ins[4 * at : 4 * at + 4]
            low = keep_lo[...].astype(F32) + got_lo[...].astype(F32)
            high = keep_hi[...].astype(F32) + got_hi[...].astype(F32)
            if low.shape[1] != outs[2 * index].shape[1]:
                pad = jnp.zeros((*low.shape[:2], 4 * width // 3 - low.shape[2]), F32)
                low = fold(jnp.concatenate([low, pad], axis=2))
                high = fold(jnp.concatenate([high, pad], axis=2))
            columns = slice(start, start + width)
            outs[2 * index][:, :, columns] = low.astype(BF)
            outs[2 * index + 1][:, :, columns] = high.astype(BF)
            start += width
            at += 1


def add_halves(groups):
    rows = groups[0][0][0].shape[0] // 2
    grid = max(1, rows // 2)
    block = rows // grid
    operands, in_specs, out_specs, shapes, widths = [], [], [], [], []
    for group in groups:
        for keep, got in group:
            shape = (block,) + keep.shape[1:]
            low = pl.BlockSpec(shape, lambda i: (i, 0, 0))
            high = pl.BlockSpec(shape, lambda i: (i + grid, 0, 0))
            operands += [keep, keep, got, got]
            in_specs += [low, high, low, high]
        height = group[0][0].shape[1]
        widths.append(
            [
                keep.shape[2] if keep.shape[1] == height else -(-keep.shape[2] // 512) * 384
                for keep, _ in group
            ]
        )
        shape = (block, height, sum(widths[-1]))
        out_specs += [pl.BlockSpec(shape, lambda i: (i, 0, 0))] * 2
        shapes += [jax.ShapeDtypeStruct((rows,) + shape[1:], BF)] * 2
    outs = pl.pallas_call(
        functools.partial(add_kernel, widths),
        grid=(grid,),
        in_specs=in_specs,
        out_specs=out_specs,
        out_shape=shapes,
        compiler_params=pltpu.CompilerParams(vmem_limit_bytes=24 * MIB),
        cost_estimate=SHORT,
        name="add_halves",
    )(*operands)
    return outs[0::2], outs[1::2]


def last_add_kernel(core_ref, *refs):
    first = core_ref[0] == 0
    *ins, mine, theirs, down = refs
    values = [
        ins[index][0].astype(F32) + ins[index + 1][0].astype(F32)
        for index in range(0, len(ins), 2)
    ]
    width = down.shape[1]
    down[...] = values[2][:, :width]
    values[2] = unfold(values[2][:, width:])
    start = 0
    for value in values:
        low, high = value[:12], value[12:]
        columns = slice(start, start + value.shape[1])
        mine[:, columns] = jnp.where(first, low, high)
        theirs[:, columns] = jnp.where(first, high, low).astype(BF)
        start += value.shape[1]


def last_add(core, pairs, down_shape):
    flat = [value for pair in pairs for value in pair]
    folded = pairs[2][0].shape[2] - down_shape[1]
    width = pairs[0][0].shape[2] + pairs[1][0].shape[2] + folded // 3 * 4
    shapes = [(12, width), (12, width), down_shape]
    return pl.pallas_call(
        last_add_kernel,
        grid_spec=pltpu.PrefetchScalarGridSpec(
            num_scalar_prefetch=1,
            grid=(1,),
            in_specs=[pl.BlockSpec(v.shape, lambda i, _: (0, 0, 0)) for v in flat],
            out_specs=[pl.BlockSpec(shape, lambda i, _: (0, 0)) for shape in shapes],
        ),
        out_shape=[jax.ShapeDtypeStruct(s, t) for s, t in zip(shapes, (F32, BF, F32))],
        compiler_params=pltpu.CompilerParams(vmem_limit_bytes=16 * MIB),
        cost_estimate=SHORT,
        name="last_add",
    )(core, *flat)


PLACES = (
    ((2048, 768),),
    ((2816, 512), (5376, 256)),
    ((5632, 768),),
    ((6400, 256), (6656, 512)),
    ((7168, 768),),
)
HIDDEN_PLACES = (0, 3328)
TILE = 256


def deal(parity):
    row = lax.broadcasted_iota(jnp.int32, (TILE // 2, TILE), 0)
    col = lax.broadcasted_iota(jnp.int32, (TILE // 2, TILE), 1)
    return (col == 64 * (row // 32) + 32 * parity + row % 32).astype(F32).astype(BF)


def finish_kernel(core_ref, mine, other, *outs):
    first = core_ref[0] == 0
    for pieces, out in zip(PLACES, outs):
        half = out.shape[1] // 2
        done = 0
        for start, width in pieces:
            a = mine[:, start : start + width]
            b = other[:, start : start + width].astype(F32)
            out[:, done : done + width] = jnp.where(first, a, b)
            out[:, half + done : half + done + width] = jnp.where(first, b, a)
            done += width
    own, their = deal(core_ref[0]), deal(1 - core_ref[0])
    rows = mine.shape[0]
    pad = jnp.zeros((16 - rows, TILE // 2), F32)
    for start, out in zip(HIDDEN_PLACES, outs[5:7]):
        tiles = out.shape[1] // TILE
        stack = lambda ref: jnp.concatenate(
            [
                jnp.concatenate(
                    [ref[:, start + 128 * t : start + 128 * (t + 1)].astype(F32), pad], axis=0
                )
                for t in range(tiles)
            ],
            axis=0,
        )
        high, low = two_parts(stack(mine))
        value = dot(high, own) + dot(low, own) + dot(stack(other).astype(BF), their)
        for t in range(tiles):
            out[:, TILE * t : TILE * (t + 1)] = value[16 * t : 16 * t + rows]
    misc = mine[:, 7936:8064] + other[:, 7936:8064].astype(F32)
    heads = outs[7].shape[1]
    outs[7][...] = misc[:, :heads]
    row = lax.broadcasted_iota(jnp.int32, (rows, 128), 0)
    col = lax.broadcasted_iota(jnp.int32, (rows, 128), 1)
    eye = (row == col).astype(F32).astype(BF)
    high, low = two_parts(misc)
    turned = dot_tn(high, eye) + dot_tn(low, eye)
    outs[8][...] = turned[heads : heads + 1, :rows]
    outs[9][...] = turned[heads + 1 : heads + 2, :rows]


def finish(core, mine, other, hidden_units, heads):
    rows = mine.shape[0]
    shapes = [(rows, 2 * sum(w for _, w in pieces)) for pieces in PLACES]
    shapes += [(rows, hidden_units), (rows, hidden_units), (rows, heads), (1, rows), (1, rows)]
    operands = (mine, other)
    return pl.pallas_call(
        finish_kernel,
        grid_spec=pltpu.PrefetchScalarGridSpec(
            num_scalar_prefetch=1,
            grid=(1,),
            in_specs=[pl.BlockSpec(v.shape, lambda i, _: (0, 0)) for v in operands],
            out_specs=[pl.BlockSpec(shape, lambda i, _: (0, 0)) for shape in shapes],
        ),
        out_shape=[jax.ShapeDtypeStruct(shape, F32) for shape in shapes],
        compiler_params=pltpu.CompilerParams(vmem_limit_bytes=16 * MIB),
        cost_estimate=SHORT,
        name="finish",
    )(core, *operands)


def pack_kernel(core_ref, gain_attn, gain_ffn, *refs):
    w_out, w_query, w_key, w_value, w_house, w_beta, w_gate, w_up = refs[:8]
    mine, theirs = refs[8:]
    first = core_ref[0] == 0
    rows, width = w_out.shape
    half, units = width // 2, w_gate.shape[1]
    gains = jnp.concatenate(
        [gain_attn[...].astype(F32), gain_ffn[...].astype(F32), jnp.zeros((6, rows), F32)], axis=0
    )
    place = lax.broadcasted_iota(jnp.int32, (8, 128), 0)
    lane = lax.broadcasted_iota(jnp.int32, (8, 128), 1)
    pick = ((place < 2) & (lane == 12 + place)).astype(F32)
    misc = dot_tn(gains.astype(BF), pick.astype(BF))
    beta = w_beta[...].astype(F32)
    misc += jnp.concatenate([beta, jnp.zeros((rows, 128 - beta.shape[1]), F32)], axis=1)
    split = lambda a, b: (jnp.where(first, a, b), jnp.where(first, b, a))
    pieces = [
        split(w_out[:, :half], w_out[:, half:]),
        (misc.astype(BF), misc.astype(BF)),
        split(w_query[...], w_value[...]),
        split(w_key[...], w_house[...]),
    ]
    for start, (own, other) in zip((0, MISC_AT, FIRST_AT, SECOND_AT), pieces):
        size = own.shape[1]
        mine[:, start : start + size] = own
        theirs[:, start : start + size] = other
    pad = jnp.zeros((16 - rows, TILE), F32)
    row = lax.broadcasted_iota(jnp.int32, (TILE, TILE), 0)
    col = lax.broadcasted_iota(jnp.int32, (TILE, TILE), 1)
    parity = jnp.where(col < 128, core_ref[0], 1 - core_ref[0])
    at = col % 128
    pick = (row == 64 * (at // 32) + 32 * parity + at % 32).astype(F32).astype(BF)
    tiles = units // TILE
    for start, ref in ((GATE_AT, w_gate), (UP_AT, w_up)):
        stack = jnp.concatenate(
            [
                jnp.concatenate([ref[:, TILE * t : TILE * (t + 1)].astype(F32), pad], axis=0)
                for t in range(tiles)
            ],
            axis=0,
        ).astype(BF)
        value = dot(stack, pick)
        for t in range(tiles):
            part = value[16 * t : 16 * t + rows].astype(BF)
            mine[:, start + 128 * t : start + 128 * (t + 1)] = part[:, :128]
            theirs[:, start + 128 * t : start + 128 * (t + 1)] = part[:, 128:]


def pack(core, gains, weights):
    rows, width = weights[0].shape
    shapes = [(rows, MISC_AT + 128)] * 2
    operands = [gain[None, :] for gain in gains] + list(weights)
    return pl.pallas_call(
        pack_kernel,
        grid_spec=pltpu.PrefetchScalarGridSpec(
            num_scalar_prefetch=1,
            grid=(1,),
            in_specs=[pl.BlockSpec(v.shape, lambda i, _: (0, 0)) for v in operands],
            out_specs=[pl.BlockSpec(shape, lambda i, _: (0, 0)) for shape in shapes],
        ),
        out_shape=[jax.ShapeDtypeStruct(shape, BF) for shape in shapes],
        compiler_params=pltpu.CompilerParams(vmem_limit_bytes=58 * MIB),
        cost_estimate=SHORT,
        name="pack",
    )(core, *operands)


def send_step(value, stream, step):
    count = lax.axis_size("fsdp")
    pairs = [(d, d ^ (2 * MASKS[stream][d & 1][step])) for d in range(count)]
    return lax.ppermute(value, "fsdp", pairs)


def after(values, earlier):
    flat, tree = jax.tree.flatten(values)
    kept = lax.optimization_barrier((*flat, *jax.tree.leaves(earlier)))
    return jax.tree.unflatten(tree, kept[: len(flat)])


def exchange(sends, step):
    return [send_step(send, stream, step) for stream, send in enumerate(sends)]


def blocks(turned, height):
    return turned.reshape(turned.shape[0] // height, height, turned.shape[1])


def gather_streams(parts):
    for step in range(5, 0, -1):
        gots = exchange(parts, step)
        parts = [jnp.concatenate(pair, axis=0) for pair in zip(parts, gots)]
    return parts, exchange(parts, 0)


def in_order_kernel(place_ref, *refs):
    lows, highs, out = refs[:3], refs[3:6], refs[6]
    half, _, width = lows[0].shape
    for stream, (low, high) in enumerate(zip(lows, highs)):
        columns = slice(width * stream, width * (stream + 1))
        for place in range(half):
            out[place_ref[stream, place], :, columns] = low[place]
            out[place_ref[stream, half + place], :, columns] = high[place]


def in_order(places, lows, highs):
    half, height, width = lows[0].shape
    shape = (2 * half, height, 3 * width)
    out = pl.pallas_call(
        in_order_kernel,
        grid_spec=pltpu.PrefetchScalarGridSpec(
            num_scalar_prefetch=1,
            grid=(1,),
            in_specs=[pl.BlockSpec(lows[0].shape, lambda i, _: (0, 0, 0))] * 6,
            out_specs=pl.BlockSpec(shape, lambda i, _: (0, 0, 0)),
        ),
        out_shape=jax.ShapeDtypeStruct(shape, BF),
        compiler_params=pltpu.CompilerParams(vmem_limit_bytes=58 * MIB),
        cost_estimate=SHORT,
        name="in_order",
    )(places, *lows, *highs)
    return out.reshape(2 * half * height, 3 * width)


def body(
    tokens,
    lengths,
    gain_attn,
    w_query,
    w_key,
    w_value,
    w_house,
    w_beta,
    w_out,
    gain_ffn,
    w_gate,
    w_up,
    w_down,
    cotangent,
):
    seqs, count, width = tokens.shape
    heads = w_beta.shape[1]
    hidden_units = w_gate.shape[1]
    half = width // 2
    devices = lax.axis_size("fsdp")
    me = lax.axis_index("fsdp")
    core, chip = me % 2, me // 2
    offsets = jnp.asarray(owner_offsets())
    places = jnp.where(core == 0, offsets[0], offsets[1]) ^ chip
    core_at = core.astype(jnp.int32)[None]

    mine, theirs = pack(
        core_at,
        (gain_attn, gain_ffn),
        (w_out, w_query, w_key, w_value, w_house, w_beta, w_gate, w_up),
    )
    stack = lambda own, other: jnp.where(
        core == 0,
        jnp.concatenate([own, other], axis=0),
        jnp.concatenate([other, own], axis=0),
    )
    slab = stack(mine, swap(theirs))
    by_core = [[*range(0, devices, 2), *range(1, devices, 2)]]
    attn = lax.all_gather(slab, "fsdp", axis=0, tiled=True, axis_index_groups=by_core)
    part, third = hidden_units // 2, width // 3
    lows, highs = gather_streams([w_down[None, :, third * s : third * (s + 1)] for s in range(3)])
    full_down = in_order(places, lows, highs)

    flat = tokens.reshape(count, width)
    valid = lax.broadcasted_iota(jnp.int32, (count, 1), 0) < lengths[0]
    cot = jnp.where(valid, cotangent.reshape(count, width), jnp.zeros((), BF))
    cots = (cot, swap(cot))

    normed_t, q, k, v, h, hidden, second, att_t, *cells, beta, gain = attention_forward(
        after(flat, full_down), lengths, attn
    )
    normed_x, att_x = (
        (blocks(value, 24), blocks(swap(value), 24)) for value in (normed_t, att_t)
    )
    second_t, product_t, gate_low, up_low, feed, feed_other, second_grad, grad_other = feedforward(
        core_at, (second, swap(second)), cots, attn, full_down
    )
    grad_got = swap(grad_other)
    mixed = jnp.where(valid, hidden + feed + swap(feed_other), 0.0).astype(BF)
    second_x, product_x = (blocks(second_t, 24),), (blocks(product_t, 32),)

    jobs = [
        ([second_x], [(gate_low[None],)], [(0, 0, 0, 0, part)]),
        ([second_x], [(up_low[None],)], [(0, 0, 0, 0, part)]),
        ([product_x], [(jnp.concatenate(cots, axis=0)[None],)], [(0, 0, 0, 0, width)]),
    ]
    late = after(places, (grad_got, normed_x, att_x))
    early = [places[0], late[1], late[2]]
    sends = [weight_gradient(early[s], core_at, *job)[0] for s, job in enumerate(jobs)]
    gots = exchange(sends, 0)

    grads, branch, grad_tokens, misc_grad = attention_backward(
        flat,
        normed_t,
        (gain, after(hidden, sends), cot, second_grad, grad_got),
        (q, k, v, h, *cells, beta),
        attn,
    )
    grads_y = (grads, swap(grads))
    branch_y = (branch[None], swap(branch)[None])
    misc_x = misc_grad.reshape(-1, 24, 128)
    attn_jobs = [
        ([normed_x], [grads_y], [(0, 0, 0, 0, 768), (0, 0, 1, 0, 512)]),
        ([normed_x], [grads_y], [(0, 0, 1, 512, 256), (0, 0, 2, 0, 768), (0, 0, 3, 0, 256)]),
        ([normed_x, att_x], [grads_y, branch_y], [(0, 0, 3, 256, 512), (1, 1, 0, 0, 768)], misc_x),
    ]
    attn_sends = [
        weight_gradient(after(places[s], [gots[t] for t in AHEAD[s]]), core_at, *job)[0]
        for s, job in enumerate(attn_jobs)
    ]
    attn_gots = exchange(attn_sends, 0)

    def kept(jobs, gots):
        pairs = [
            weight_gradient(places[s], core_at, *job, got=gots[s]) for s, job in enumerate(jobs)
        ]
        return [p[0] for p in pairs], [p[1] for p in pairs]

    keeps, sends = kept(jobs, gots)
    gots = exchange([after(sends[0], attn_gots[0]), *sends[1:]], 1)
    attn_keeps, attn_sends = kept(attn_jobs, [after(got, keeps) for got in attn_gots])
    attn_gots = exchange(attn_sends, 1)
    first, second = list(zip(keeps, gots)), list(zip(attn_keeps, attn_gots))
    groups = [list(pair) for pair in zip(first, second)]
    for step in range(2, 6):
        keeps, sends = add_halves(groups)
        gots = exchange(sends, step)
        groups = [[pair] for pair in zip(keeps, gots)]
    mine, theirs, grad_down = last_add(core_at, [group[0] for group in groups], w_down.shape)
    *large, grad_gate, grad_up, grad_beta, attn_gain, ffn_gain = finish(
        core_at, mine, swap(theirs), hidden_units, heads
    )

    return (
        mixed.reshape(seqs, count, width),
        grad_tokens.reshape(seqs, count, width),
        attn_gain.reshape(-1),
        *large[:4],
        grad_beta,
        large[4],
        ffn_gain.reshape(-1),
        grad_gate,
        grad_up,
        grad_down,
    )


def solution(mesh):
    rows = P("fsdp", None)
    line = P("fsdp")
    cube = P("fsdp", None, None)
    in_specs = (cube, line, line, rows, rows, rows, rows, rows, rows, line, rows, rows, rows, cube)
    out_specs = (cube, cube, line, rows, rows, rows, rows, rows, rows, line, rows, rows, rows)
    return jax.shard_map(body, mesh=mesh, in_specs=in_specs, out_specs=out_specs, check_vma=False)
```
